256 devices in a mesh: ctx: 16 (over z, x_hi), tp: 8 (over y, core), dp: 2 (over x_lo).
Axes of the slice: x: 4 (x_hi: 2, x_lo: 2; x = x_hi * 2 + x_lo), y: 4, z: 8, core: 2. Of those that a mesh axis runs over, the one named last changes fastest.
Arguments:
- queries: bfloat16 [2, 4096, 3072], P('dp', 'ctx', 'tp'), may hold values from -6 to 6
- keys: bfloat16 [2, 4096, 3072], P('dp', 'ctx', 'tp'), may hold values from -6 to 6
- values: bfloat16 [2, 4096, 3072], P('dp', 'ctx', 'tp'), may hold values from -6 to 6
- out_grad: bfloat16 [2, 4096, 3072], P('dp', 'ctx', 'tp'), may hold values from -6 to 6
- depth_kernel: bfloat16 [27, 3072], P(None, 'tp'), may hold values from -1.25 to 1.25
- point_weight: bfloat16 [3072, 3072], P('tp'), may hold values from -0.109375 to 0.109375
- block_of_frame: int32 [32], replicated, may hold values from 0 to 15, never falling along the last dimension, each value on 1 to 4 neighbouring positions
Outputs:
- query_grad: bfloat16 [2, 4096, 3072], P('dp', 'ctx', 'tp')
- key_grad: bfloat16 [2, 4096, 3072], P('dp', 'ctx', 'tp')
- value_grad: bfloat16 [2, 4096, 3072], P('dp', 'ctx', 'tp')
- point_grad: float32 [3072, 3072], P('tp')
- depth_grad: float32 [27, 3072], P(None, 'tp')
The draws below stay inside these ranges and needn't reach their ends.
Inputs may be any that keep to these rules, and one draw needn't show every extreme that they name: `block_of_frame`: block numbers never fall along the frames; a block spans 1 to 4 frames.
All inputs are finite; a program needn't handle non-finite values.
Results may differ from the reference program's by a relative error of at most 0.023.
Values may be sent and summed in bfloat16 or wider, within the bound.
A program may use at most 128 MiB of HBM per device.

```python
import math
import jax
import jax.numpy as jnp
import numpy as np
from jax import lax

HEADS = 24
HD = 128
CH = 3072
HH = 8
WW = 16
FRAMES = 32
SEQ = 4096
CLIPS = 2
NBLOCK = 16
TAPS = 27


def drawn_pair(key):
    base = jax.random.fold_in(key, 7)
    query_key, key_key = jax.random.split(base, 2)
    shape = (CLIPS, SEQ, CH)
    query_draw = 1.6 * jax.random.truncated_normal(query_key, -3.75, 3.75, shape, jnp.float32)
    key_draw = 1.6 * jax.random.truncated_normal(key_key, -3.75, 3.75, shape, jnp.float32)
    return (query_draw, key_draw)


def draw_queries(key, part):
    return drawn_pair(key)[0].astype(jnp.bfloat16)


def draw_keys(key, part):
    return drawn_pair(key)[1].astype(jnp.bfloat16)


def block_levels(rng, dims, cuts, least, high):
    factor_of, own = 1.0, jax.random.fold_in(rng, 6)
    for dim, parts in cuts:
        heights = jnp.exp(jax.random.uniform(jax.random.fold_in(own, dim), (parts,), jnp.float32, least / len(cuts), high / len(cuts)))
        factor_of = factor_of * jnp.repeat(heights, dims[dim] // parts).reshape([-1 if axis == dim else 1 for axis in range(len(dims))])
    return factor_of


def profile(amount, total, bound, skew):
    portions = [(1 << 20) // math.isqrt(standing ** skew) + 1 for standing in range(2, amount + 1)]
    spare, counts = total - bound - (amount - 1), [1] * (amount - 1)
    while spare > 0:
        movable = [i for i in range(amount - 1) if counts[i] < bound]
        whole, remaining = sum([portions[i] for i in movable]), spare
        for i in movable:
            extra = min(bound - counts[i], max(1, remaining * portions[i] // whole), spare)
            counts[i] = counts[i] + extra
            spare = spare - extra
    return np.array([bound] + counts)


def uneven(own_key, count, total, limit, slope):
    if count == 2:
        one = jax.random.randint(own_key, (), max(1, total - limit), min(limit, total - 1) + 1)
        return jnp.stack([one, total - one])
    lengths = jnp.asarray(profile(count, total, limit, slope), jnp.int32)
    couples = (count - 1) // 2
    donor, sink = lengths[1:1 + 2 * couples:2], lengths[2:2 + 2 * couples:2]
    room = jnp.minimum(donor - 1, limit - sink)
    moved = jax.random.randint(jax.random.fold_in(own_key, 1), (couples,), 0, 1 << 20) % (room + 1)
    lengths = lengths.at[1:1 + 2 * couples:2].set(donor - moved).at[2:2 + 2 * couples:2].set(sink + moved)
    return lengths[jax.random.permutation(jax.random.fold_in(own_key, 2), count)]


def gaussian(stream_key, dims, deviation, reach, cuts=(), kind=jnp.bfloat16):
    drawn = deviation * jax.random.normal(stream_key, dims, jnp.float32)
    if cuts:
        drawn = drawn * block_levels(stream_key, dims, cuts, -0.22, 0.18)
    return jnp.clip(drawn, -reach, reach).astype(kind)


def setup_inputs(seed: int = 0) -> dict:
    arg_keys = jax.random.split(jax.random.key(seed), 8)
    return {
        "queries": draw_queries(jax.random.fold_in(arg_keys[7], 71), 0),
        "keys": draw_keys(jax.random.fold_in(arg_keys[7], 71), 0),
        "values": gaussian(arg_keys[2], (CLIPS, SEQ, CH), 1.0, 6.0, ((0, 2), (1, 16), (2, 8))),
        "out_grad": gaussian(arg_keys[3], (CLIPS, SEQ, CH), 1.0, 6.0, ((0, 2), (1, 16), (2, 8))),
        "depth_kernel": gaussian(arg_keys[4], (TAPS, CH), TAPS ** -0.5, 1.25, ((1, 8),)),
        "point_weight": gaussian(arg_keys[5], (CH, CH), CH ** -0.5, 0.109375, ((0, 8),)),
        "block_of_frame": jnp.searchsorted(jnp.cumsum(uneven(arg_keys[6], NBLOCK, FRAMES, 4, 2)), jnp.arange(FRAMES), side="right").astype(jnp.int32),
    }


NEG = -1e+30

def tap_offsets(tap_index):
    return (tap_index // 9 - 1, tap_index // 3 % 3 - 1, tap_index % 3 - 1)

def padded_grid(extended, frame_count):
    channels = extended.shape[1]
    grid = extended.astype(jnp.float32).reshape(frame_count + 2, HH, WW, channels)
    return jnp.pad(grid, ((0, 0), (1, 1), (1, 1), (0, 0)))

def depthwise(grid, kernel, frame_count, direction):
    channels = grid.shape[3]
    result = jnp.zeros((frame_count, HH, WW, channels), jnp.float32)
    for tap_index in range(27):
        frame_shift, row_shift, column_shift = tap_offsets(tap_index)
        first_frame = 1 + direction * frame_shift
        first_row = 1 + direction * row_shift
        first_column = 1 + direction * column_shift
        window = grid[first_frame:first_frame + frame_count, first_row:first_row + HH, first_column:first_column + WW]
        result = result + kernel[tap_index] * window
    return result.reshape(frame_count * HH * WW, channels)

def tap_sums(attn_grid, grad_grid, frame_count):
    collected = []
    for tap_index in range(27):
        frame_shift, row_shift, column_shift = tap_offsets(tap_index)
        window = attn_grid[1 + frame_shift:1 + frame_shift + frame_count, 1 + row_shift:1 + row_shift + HH, 1 + column_shift:1 + column_shift + WW]
        collected.append(lax.optimization_barrier(jnp.sum(window * grad_grid, axis=(0, 1, 2))))
    return jnp.stack(collected)

def reference(queries, keys, values, out_grad, depth_kernel, point_weight, block_of_frame):
    frame_size = HH * WW
    scaling = 1.0 / math.sqrt(HD)
    grad_scale = 1.0 / math.sqrt(CLIPS * SEQ)
    frame_of = jnp.arange(SEQ, dtype=jnp.int32) // frame_size
    token_blocks = block_of_frame[frame_of]
    visible = token_blocks[None, :] <= token_blocks[:, None]
    kernel = depth_kernel.astype(jnp.float32)
    point_total = jnp.zeros((CH, CH), jnp.float32)
    depth_total = jnp.zeros((27, CH), jnp.float32)
    query_list, key_list, value_list = ([], [], [])
    zero_frame = jnp.zeros((frame_size, CH), jnp.bfloat16)

    def forward_head(operands):
        query_head, key_head, value_head = operands
        scores = jnp.where(visible, jnp.dot(query_head, key_head.T, preferred_element_type=jnp.float32) * scaling, NEG)
        row_max = lax.optimization_barrier(jnp.max(scores, axis=1))
        weights = jnp.exp(scores - row_max[:, None])
        row_sum = lax.optimization_barrier(jnp.sum(weights, axis=1))
        attended = (jnp.dot(weights.astype(jnp.bfloat16), value_head, preferred_element_type=jnp.float32) / row_sum[:, None]).astype(jnp.bfloat16)
        return (attended, row_max + jnp.log(row_sum))

    def backward_head(operands):
        query_head, key_head, value_head, grad_head, log_sum, row_dot = operands
        scores = jnp.where(visible, jnp.dot(query_head, key_head.T, preferred_element_type=jnp.float32) * scaling, NEG)
        probs = jnp.exp(scores - log_sum[:, None])
        dprobs = jnp.dot(grad_head, value_head.T, preferred_element_type=jnp.float32)
        dscores = (probs * (dprobs - row_dot[:, None])).astype(jnp.bfloat16)
        grad_query = (jnp.dot(dscores, key_head, preferred_element_type=jnp.float32) * scaling).astype(jnp.bfloat16)
        grad_key = (jnp.dot(dscores.T, query_head, preferred_element_type=jnp.float32) * scaling).astype(jnp.bfloat16)
        grad_value = jnp.dot(probs.astype(jnp.bfloat16).T, grad_head, preferred_element_type=jnp.float32).astype(jnp.bfloat16)
        return (grad_query, grad_key, grad_value)
    for clip_index in range(CLIPS):
        query_heads = queries[clip_index].reshape(SEQ, HEADS, HD).transpose(1, 0, 2)
        key_heads = keys[clip_index].reshape(SEQ, HEADS, HD).transpose(1, 0, 2)
        value_heads = values[clip_index].reshape(SEQ, HEADS, HD).transpose(1, 0, 2)
        attended, log_sums = lax.map(forward_head, (query_heads, key_heads, value_heads))
        attended_rows = attended.transpose(1, 0, 2).reshape(SEQ, CH)
        attn_grid = padded_grid(jnp.concatenate([zero_frame, attended_rows, zero_frame], axis=0), FRAMES)
        mixed = depthwise(attn_grid, kernel, FRAMES, 1).astype(jnp.bfloat16)
        mixed_grad = jnp.dot(out_grad[clip_index], point_weight.T, preferred_element_type=jnp.float32).astype(jnp.bfloat16)
        point_total = point_total + jnp.dot(mixed.T, out_grad[clip_index], preferred_element_type=jnp.float32)
        grad_grid = mixed_grad.astype(jnp.float32).reshape(FRAMES, HH, WW, CH)
        depth_total = depth_total + tap_sums(attn_grid, grad_grid, FRAMES)
        grad_pad = padded_grid(jnp.concatenate([zero_frame, mixed_grad, zero_frame], axis=0), FRAMES)
        attn_grad = depthwise(grad_pad, kernel, FRAMES, -1).astype(jnp.bfloat16)
        row_dots = lax.optimization_barrier(jnp.sum(attended_rows.astype(jnp.float32).reshape(SEQ, HEADS, HD) * attn_grad.astype(jnp.float32).reshape(SEQ, HEADS, HD), axis=2)).T
        grad_heads = attn_grad.reshape(SEQ, HEADS, HD).transpose(1, 0, 2)
        grad_query, grad_key, grad_value = lax.map(backward_head, (query_heads, key_heads, value_heads, grad_heads, log_sums, row_dots))
        query_list.append(grad_query.transpose(1, 0, 2).reshape(SEQ, CH))
        key_list.append(grad_key.transpose(1, 0, 2).reshape(SEQ, CH))
        value_list.append(grad_value.transpose(1, 0, 2).reshape(SEQ, CH))
    return (jnp.stack(query_list), jnp.stack(key_list), jnp.stack(value_list), point_total * grad_scale, depth_total * grad_scale)
```

```python
import math

import jax
import jax.numpy as jnp
from jax import lax
from jax.experimental import pallas as pl
from jax.experimental.pallas import tpu as pltpu
from jax.sharding import PartitionSpec as P

HD = 128
HH = 8
WW = 16
FRAME = HH * WW
NEG = -1e30
OPEN = 3e38
MESH = pl.DeviceIdType.MESH
F32 = jnp.float32
BF16 = jnp.bfloat16

ZN = 8
XN = 4
TN = 8
CN = 16
ROWS = 256
COLS = 384
HEADS = COLS // HD
PIECE = COLS // ZN


def wait(ref, sem):
    pltpu.make_async_copy(ref, ref, sem).wait()


def nt(a, b):
    return lax.dot_general(a, b, (((1,), (1,)), ((), ())), preferred_element_type=F32)


def nn(a, b):
    return lax.dot_general(a, b, (((1,), (0,)), ((), ())), preferred_element_type=F32)


def tn(a, b):
    return lax.dot_general(a, b, (((0,), (0,)), ((), ())), preferred_element_type=F32)


def spread_columns(shifted, plain):
    column = lax.broadcasted_iota(jnp.int32, (FRAME, COLS), 0) % WW
    for frame in range(4):
        cells = plain[frame].astype(F32)
        shifted[1, frame, WW : WW + FRAME] = cells
        shifted[0, frame, WW : WW + FRAME] = jnp.where(
            column > 0, pltpu.roll(cells, 1, 0), 0.0
        )
        shifted[2, frame, WW : WW + FRAME] = jnp.where(
            column < WW - 1, pltpu.roll(cells, FRAME - 1, 0), 0.0
        )


def body(
    q_in, k_in, v_in, g_in, w_ref, kern_in, bound_ref,
    dq_out, dk_out, dv_out, point_out, depth_out,
    q, kv, og, kern, row_max, row_sum, acc, lse, dots,
    mg_send, mg_ext, at_ext, shifted, mixed, mixed_own, dsum, dsum_own,
    do, dq_acc, terms, xsend, xrecv, sbuf, rbuf,
    prod, xr, relay, qsum, zr, allq, dx, dz, fin, finr,
    swap_s, swap_r, og_s, og_r, ring_s, ring_r, sib_s, sib_r, halo_s, halo_r,
    bs_s, bs_r, bx_s, bx_r, px_s, px_r, pz_s, pz_r, gz_s, gz_r, gx_s, gx_r,
    dx_s, dx_r, dz_s, dz_r,
):
    ctx, tp, dp = lax.axis_index("ctx"), lax.axis_index("tp"), lax.axis_index("dp")
    z, half = ctx // 2, ctx % 2
    y, core = tp // 2, tp % 2
    chunk = 2 * z + core
    xi = 2 * half + dp
    off = half != core
    same = half == core
    scaling = 1.0 / math.sqrt(HD)
    factor = scaling * math.log2(math.e)

    def at_z(step):
        return (2 * lax.rem(z + step + ZN, ZN) + half, tp, dp)

    def at_x(step):
        place = lax.rem(xi + step + XN, XN)
        return (2 * z + place // 2, tp, lax.rem(place, 2))

    def at_tp(step):
        return (ctx, lax.rem(tp + step, TN), dp)

    sibling = (ctx, 2 * y + 1 - core, dp)
    partner = (2 * z + 1 - half, 2 * y + 1 - core, dp)
    below = lax.rem(z + ZN - 1 + core, ZN)
    above = lax.rem(z + core, ZN)
    prev_dev = (2 * below + half, 2 * y + 1 - core, dp)
    next_dev = (2 * above + half, 2 * y + 1 - core, dp)
    other = lax.rem(z + ZN - 1 + 2 * core, ZN)
    halo_dev = (2 * other + half, 2 * y + 1 - core, dp)

    barrier = pltpu.get_barrier_semaphore()
    peers = [at_tp(i) for i in range(1, TN)]
    peers += [at_z(i) for i in range(1, ZN)]
    peers += [at_x(i) for i in range(1, XN)]
    peers += [partner, halo_dev]
    for device in peers:
        pl.semaphore_signal(barrier, inc=1, device_id=device, device_id_type=MESH)
    pl.semaphore_wait(barrier, len(peers))

    def send(src, dst, send_sem, recv_sem, device):
        pltpu.make_async_remote_copy(
            src_ref=src, dst_ref=dst, send_sem=send_sem, recv_sem=recv_sem,
            device_id=device, device_id_type=MESH,
        ).start()

    def swap(i, src, dst):
        @pl.when(off)
        def _():
            send(src, dst, swap_s.at[i], swap_r.at[i], partner)

        @pl.when(same)
        def _():
            pltpu.make_async_copy(src, dst, swap_r.at[i]).start()

    swap(0, k_in, kv.at[0, ctx])
    swap(1, v_in, kv.at[1, ctx])
    swap(2, q_in, q)
    swap(3, kern_in, kern)
    for i in range(1, TN):
        send(g_in, og.at[tp], og_s.at[i], og_r.at[i], at_tp(i))
    keep = pltpu.make_async_copy(g_in, og.at[tp], og_r.at[0])
    keep.start()

    acc[...] = jnp.zeros_like(acc)
    row_sum[...] = jnp.zeros_like(row_sum)
    row_max[...] = jnp.full_like(row_max, NEG)
    dq_acc[...] = jnp.zeros_like(dq_acc)
    shifted[...] = jnp.zeros_like(shifted)
    rbuf[0, 3, 1] = jnp.zeros((ROWS, COLS), BF16)
    rbuf[1, 3, 0] = jnp.zeros((ROWS, COLS), BF16)

    def ring(direction, distance, part, source):
        place = kv.at[part, source]
        send(
            place, place, ring_s.at[direction, distance - 1, part],
            ring_r.at[direction, distance - 1, part], at_z(1 if direction == 0 else -1),
        )

    def ring_wait(direction, distance, part, source):
        wait(kv.at[part, source], ring_r.at[direction, distance - 1, part])

    def to_sibling(slot, source):
        send(kv.at[:, source], kv.at[:, source], sib_s.at[slot], sib_r.at[slot], sibling)

    for part in range(2):
        wait(kv.at[part, chunk], swap_r.at[part])
        ring(0, 1, part, chunk)
        ring(1, 1, part, chunk)
    to_sibling(0, chunk)

    def flip(index):
        return index + 1 - 2 * lax.rem(index, 2)

    def fwd_chunk(index):
        @pl.when(index <= chunk + 2)
        def _():
            limits = bound_ref[index]
            for head in range(HEADS):
                lanes = slice(head * HD, (head + 1) * HD)
                keys = kv[0, index, :, lanes]
                vals = kv[1, index, :, lanes]
                scores = nt(keys, q[:, lanes])
                scores = jnp.concatenate(
                    [
                        jnp.minimum(scores[:FRAME], limits[0:1]),
                        jnp.minimum(scores[FRAME:], limits[1:2]),
                    ],
                    axis=0,
                )
                old = row_max[head]
                new = jnp.maximum(old, jnp.max(scores, axis=0, keepdims=True))
                weights = jnp.exp2(scores * factor - new * factor)
                shrink = jnp.exp2((old - new) * factor)
                row_max[head] = new
                row_sum[head] = row_sum[head] * shrink + jnp.sum(weights, axis=0, keepdims=True)
                acc[head] = acc[head] * shrink + tn(vals, weights.astype(BF16))

    wait(q, swap_r.at[2])

    def near(i, carry):
        @pl.when(i == 1)
        def _():
            wait(kv.at[:, flip(chunk)], sib_r.at[0])

        fwd_chunk(jnp.where(i == 0, chunk, flip(chunk)))
        return carry

    lax.fori_loop(0, 2, near, 0)

    def fwd_step(distance):
        low = 2 * lax.rem(z - distance + ZN, ZN) + core
        high = 2 * lax.rem(z + distance, ZN) + core
        for part in range(2):
            ring_wait(0, distance, part, low)
            if distance < 3 or part == 0:
                ring(0, distance + 1, part, low)
            ring_wait(1, distance, part, high)
            if distance < 3 or part == 1:
                ring(1, distance + 1, part, high)
        to_sibling(distance, low)
        to_sibling(3 + distance, high)

        def step(i, carry):
            @pl.when(i == 2)
            def _():
                wait(kv.at[:, flip(low)], sib_r.at[distance])
                wait(kv.at[:, flip(high)], sib_r.at[3 + distance])

            index = jnp.where(lax.rem(i, 2) == 0, low, high)
            fwd_chunk(jnp.where(i < 2, index, flip(index)))
            return carry

        lax.fori_loop(0, 4, step, 0)

    fwd_step(1)

    keep.wait()
    for i in range(1, TN):
        wait(og.at[lax.rem(tp + TN - i, TN)], og_r.at[i])
    total = nt(og[0], w_ref[:, 0:COLS])
    for i in range(1, TN):
        total += nt(og[i], w_ref[:, i * COLS : (i + 1) * COLS])
    mg_send[...] = total.astype(BF16).reshape(2, FRAME, COLS)
    swap(4, mg_send, mg_ext.at[1:3])

    fwd_step(2)

    def halo(which, ext):
        @pl.when(chunk > 0)
        def _():
            send(ext.at[1], ext.at[3], halo_s.at[which, 0], halo_r.at[which, 0], prev_dev)

        @pl.when(chunk < CN - 1)
        def _():
            send(ext.at[2], ext.at[0], halo_s.at[which, 1], halo_r.at[which, 1], next_dev)

        @pl.when(chunk == 0)
        def _():
            ext[0] = jnp.zeros((FRAME, COLS), BF16)

        @pl.when(chunk == CN - 1)
        def _():
            ext[3] = jnp.zeros((FRAME, COLS), BF16)

    def halo_wait(which, ext):
        @pl.when(chunk > 0)
        def _():
            wait(ext.at[1], halo_s.at[which, 0])
            wait(ext.at[0], halo_r.at[which, 1])

        @pl.when(chunk < CN - 1)
        def _():
            wait(ext.at[2], halo_s.at[which, 1])
            wait(ext.at[3], halo_r.at[which, 0])

    wait(mg_ext.at[1:3], swap_r.at[4])
    halo(0, mg_ext)

    fwd_step(3)

    last = 2 * lax.rem(z + 4, ZN) + core
    ring_wait(0, 4, 0, last)
    ring_wait(1, 4, 1, last)
    to_sibling(7, last)

    def far(i, carry):
        @pl.when(i == 1)
        def _():
            wait(kv.at[:, flip(last)], sib_r.at[7])

        fwd_chunk(jnp.where(i == 0, last, flip(last)))
        return carry

    lax.fori_loop(0, 2, far, 0)

    for head in range(HEADS):
        lanes = slice(head * HD, (head + 1) * HD)
        sums = row_sum[head]
        lse[head] = row_max[head] * factor + jnp.log(sums) * math.log2(math.e)
        rows = jnp.transpose(acc[head] / sums).astype(BF16)
        at_ext[1, :, lanes] = rows[:FRAME]
        at_ext[2, :, lanes] = rows[FRAME:]
    halo(1, at_ext)

    wait(kern, swap_r.at[3])
    halo_wait(0, mg_ext)
    spread_columns(shifted, mg_ext)

    def taps():
        return [(a, r, c) for a in (-1, 0, 1) for r in (-1, 0, 1) for c in (-1, 0, 1)]

    for frame in range(2):
        for head in range(HEADS):
            lanes = slice(head * HD, (head + 1) * HD)
            result = jnp.zeros((FRAME, HD), F32)
            for tap, (a, r, c) in enumerate(taps()):
                first = WW - WW * r
                window = shifted[1 - c, frame + 1 - a, first : first + FRAME, lanes]
                result = result + kern[tap : tap + 1, lanes] * window
            do[frame * FRAME : (frame + 1) * FRAME, lanes] = result.astype(BF16)

    halo_wait(1, at_ext)
    for head in range(HEADS):
        lanes = slice(head * HD, (head + 1) * HD)
        attended = jnp.concatenate([at_ext[1, :, lanes], at_ext[2, :, lanes]], axis=0)
        product = attended.astype(F32) * do[:, lanes].astype(F32)
        dots[head] = jnp.sum(jnp.transpose(product), axis=0, keepdims=True)

    spread_columns(shifted, at_ext)
    dsum[...] = jnp.zeros_like(dsum)
    grad_scale = 1.0 / math.sqrt(2.0 * CN * ROWS)
    for frame in range(2):
        for head in range(HEADS):
            lanes = slice(head * HD, (head + 1) * HD)
            result = jnp.zeros((FRAME, HD), F32)
            grad = mg_ext[1 + frame, :, lanes].astype(F32)
            for tap, (a, r, c) in enumerate(taps()):
                first = WW + WW * r
                window = shifted[1 + c, frame + 1 + a, first : first + FRAME, lanes]
                result = result + kern[tap : tap + 1, lanes] * window
                dsum[tap : tap + 1, lanes] += (
                    jnp.sum(window * grad, axis=0, keepdims=True) * grad_scale
                )
            mixed[frame * FRAME : (frame + 1) * FRAME, lanes] = result.astype(BF16)
    swap(5, mixed, mixed_own)
    swap(6, dsum, dsum_own)

    def bwd_chunk(index):
        @pl.when(index > chunk + 2)
        def _():
            terms[...] = jnp.zeros_like(terms)

        @pl.when(index <= chunk + 2)
        def _():
            limits = bound_ref[index]
            for head in range(HEADS):
                lanes = slice(head * HD, (head + 1) * HD)
                keys = kv[0, index, :, lanes]
                vals = kv[1, index, :, lanes]
                queries = q[:, lanes]
                grads = do[:, lanes]
                scores = nt(keys, queries)
                scores = jnp.concatenate(
                    [
                        jnp.minimum(scores[:FRAME], limits[0:1]),
                        jnp.minimum(scores[FRAME:], limits[1:2]),
                    ],
                    axis=0,
                )
                probs = jnp.exp2(scores * factor - lse[head])
                dscores = (probs * (nt(vals, grads) - dots[head])).astype(BF16)
                terms[1, :, lanes] = nn(probs.astype(BF16), grads)
                terms[0, :, lanes] = nn(dscores, queries) * scaling
                dq_acc[head] = dq_acc[head] + tn(keys, dscores)

    def share(slot):
        xsend[slot] = terms[...].astype(BF16)
        send(xsend.at[slot], xrecv.at[slot], bx_s.at[slot], bx_r.at[slot], sibling)

    def shared(slot):
        wait(xrecv.at[slot], bx_r.at[slot])
        return terms[...] + xrecv[slot].astype(F32)

    target = 2 * lax.rem(z + 4, ZN) + core

    def bwd_far(i, carry):
        bwd_chunk(jnp.where(i == 0, flip(target), target))

        @pl.when(i == 0)
        def _():
            share(7)

        return carry

    lax.fori_loop(0, 2, bwd_far, 0)
    total = shared(7).astype(BF16)
    sbuf[0, 3, 0] = total[0]
    sbuf[1, 3, 1] = total[1]
    send(sbuf.at[0, 3, 0], rbuf.at[0, 3, 0], bs_s.at[0, 3], bs_r.at[0, 3], at_z(1))
    send(sbuf.at[1, 3, 1], rbuf.at[1, 3, 1], bs_s.at[1, 3], bs_r.at[1, 3], at_z(-1))

    def bwd_step(distance):
        up = 2 * lax.rem(z + distance, ZN) + core
        down = 2 * lax.rem(z - distance + ZN, ZN) + core

        def step(i, carry):
            side = lax.rem(i, 2)
            index = jnp.where(side == 0, up, down)
            bwd_chunk(jnp.where(i < 2, flip(index), index))
            slot = distance + 3 * side

            @pl.when(i < 2)
            def _():
                share(slot)

            @pl.when(i >= 2)
            def _():
                if distance == 3:
                    wait(rbuf.at[side, 3, side], bs_r.at[side, 3])
                else:
                    wait(rbuf.at[side, distance], bs_r.at[side, distance])
                added = shared(slot) + rbuf[side, distance].astype(F32)
                sbuf[side, distance - 1] = added.astype(BF16)
                goal = lax.rem(z + ZN + 1 - 2 * side, ZN)
                send(
                    sbuf.at[side, distance - 1], rbuf.at[side, distance - 1],
                    bs_s.at[side, distance - 1], bs_r.at[side, distance - 1],
                    (2 * goal + half, tp, dp),
                )

            return carry

        lax.fori_loop(0, 4, step, 0)

    wait(mixed_own, swap_r.at[5])

    def product(i, carry):
        block = tn(mixed_own[...], og[i]) * grad_scale
        prod[i // 2, lax.rem(i, 2)] = block.astype(BF16).reshape(ZN, PIECE, COLS)
        return carry

    lax.fori_loop(0, TN, product, 0)
    across = lax.rem(xi + 2, XN)
    right = lax.rem(xi + 1, XN)
    left = lax.rem(xi + 3, XN)
    lower, upper = slice(0, ZN // 2), slice(ZN // 2, ZN)
    send(prod.at[across, :, lower], xr.at[0, 0], px_s.at[0, 0], px_r.at[0, 0], at_x(1))
    send(prod.at[across, :, upper], xr.at[1, 0], px_s.at[1, 0], px_r.at[1, 0], at_x(-1))
    send(prod.at[right, :, upper], xr.at[0, 1], px_s.at[0, 1], px_r.at[0, 1], at_x(1))
    send(prod.at[left, :, lower], xr.at[1, 1], px_s.at[1, 1], px_r.at[1, 1], at_x(-1))
    wait(dsum_own, swap_r.at[6])
    for i in range(1, XN):
        send(dsum_own, dx.at[i], dx_s.at[i], dx_r.at[i], at_x(i))

    bwd_step(3)

    wait(xr.at[0, 0], px_r.at[0, 0])
    relay[0] = (prod[right, :, lower].astype(F32) + xr[0, 0].astype(F32)).astype(BF16)
    send(relay.at[0], xr.at[0, 2], px_s.at[0, 2], px_r.at[0, 2], at_x(1))
    wait(xr.at[1, 0], px_r.at[1, 0])
    relay[1] = (prod[left, :, upper].astype(F32) + xr[1, 0].astype(F32)).astype(BF16)
    send(relay.at[1], xr.at[1, 2], px_s.at[1, 2], px_r.at[1, 2], at_x(-1))
    sums = dsum_own[...]
    for i in range(1, XN):
        wait(dx.at[i], dx_r.at[i])
        sums = sums + dx[i]
    dz[0] = sums
    for i in range(1, ZN):
        send(dz.at[0], dz.at[i], dz_s.at[i], dz_r.at[i], at_z(i))

    bwd_step(2)

    for side in range(2):
        for slot in (1, 2):
            wait(xr.at[side, slot], px_r.at[side, slot])
    qsum[:, lower] = (
        prod[xi, :, lower].astype(F32) + xr[0, 2].astype(F32) + xr[1, 1].astype(F32)
    ).astype(BF16)
    qsum[:, upper] = (
        prod[xi, :, upper].astype(F32) + xr[0, 1].astype(F32) + xr[1, 2].astype(F32)
    ).astype(BF16)
    for i in range(1, ZN):
        goal = lax.rem(z + i, ZN)
        send(qsum.at[:, goal], zr.at[i], pz_s.at[i], pz_r.at[i], at_z(i))

    bwd_step(1)

    piece = qsum[:, z].astype(F32)
    for i in range(1, ZN):
        wait(zr.at[i], pz_r.at[i])
        piece = piece + zr[i].astype(F32)
    allq[xi, :, z] = piece.astype(BF16)
    for i in range(1, ZN):
        send(allq.at[xi, :, z], allq.at[xi, :, z], gz_s.at[i], gz_r.at[i], at_z(i))

    def bwd_own(i, carry):
        bwd_chunk(jnp.where(i == 0, flip(chunk), chunk))

        @pl.when(i == 0)
        def _():
            share(0)

        return carry

    lax.fori_loop(0, 2, bwd_own, 0)
    for head in range(HEADS):
        lanes = slice(head * HD, (head + 1) * HD)
        fin[0, :, lanes] = (jnp.transpose(dq_acc[head]) * scaling).astype(BF16)
    swap(7, fin.at[0], finr.at[0])
    total = shared(0)
    for side in range(2):
        wait(rbuf.at[side, 0], bs_r.at[side, 0])
        total = total + rbuf[side, 0].astype(F32)
    fin[1:3] = total.astype(BF16)
    swap(8, fin.at[1:3], finr.at[1:3])

    for i in range(1, ZN):
        goal = lax.rem(z + ZN - i, ZN)
        wait(allq.at[xi, :, goal], gz_r.at[i])
    send(allq.at[xi], allq.at[xi], gx_s.at[0, 0], gx_r.at[0, 0], at_x(1))
    send(allq.at[xi], allq.at[xi], gx_s.at[1, 0], gx_r.at[1, 0], at_x(-1))

    sums = dz[0]
    for i in range(1, ZN):
        wait(dz.at[i], dz_r.at[i])
        sums = sums + dz[i]
    depth_out[...] = sums

    def put(quarter):
        for block in range(2):
            cells = allq[quarter, block].reshape(COLS, COLS).astype(F32)
            first = pl.multiple_of((2 * quarter + block) * COLS, HD)
            point_out[:, pl.ds(first, COLS)] = cells

    put(xi)
    wait(allq.at[left], gx_r.at[0, 0])
    send(
        allq.at[left, :, lower], allq.at[left, :, lower], gx_s.at[0, 1], gx_r.at[0, 1], at_x(1)
    )
    wait(allq.at[right], gx_r.at[1, 0])
    send(
        allq.at[right, :, upper], allq.at[right, :, upper], gx_s.at[1, 1], gx_r.at[1, 1],
        at_x(-1),
    )
    put(left)
    put(right)
    wait(finr.at[0], swap_r.at[7])
    dq_out[...] = finr[0]
    wait(finr.at[1:3], swap_r.at[8])
    dk_out[...] = finr[1]
    dv_out[...] = finr[2]
    wait(allq.at[across, :, lower], gx_r.at[0, 1])
    wait(allq.at[across, :, upper], gx_r.at[1, 1])
    put(across)

    @pl.when(off)
    def _():
        wait(k_in, swap_s.at[0])
        wait(v_in, swap_s.at[1])
        wait(q_in, swap_s.at[2])
        wait(kern_in, swap_s.at[3])
        wait(mg_send, swap_s.at[4])
        wait(mixed, swap_s.at[5])
        wait(dsum, swap_s.at[6])
        wait(fin.at[0], swap_s.at[7])
        wait(fin.at[1:3], swap_s.at[8])

    for i in range(1, TN):
        wait(g_in, og_s.at[i])
    for direction in range(2):
        for distance in range(1, 5):
            for part in range(2):
                if distance < 4 or part == direction:
                    wait(kv.at[part, chunk], ring_s.at[direction, distance - 1, part])
            if distance < 4:
                wait(sbuf.at[direction, distance - 1], bs_s.at[direction, distance - 1])
        wait(sbuf.at[direction, 3, direction], bs_s.at[direction, 3])
    for slot in range(8):
        wait(kv.at[:, chunk], sib_s.at[slot])
        wait(xsend.at[slot], bx_s.at[slot])
    for side in range(2):
        for slot in range(3):
            wait(relay.at[side], px_s.at[side, slot])
        wait(allq.at[xi], gx_s.at[side, 0])
        wait(relay.at[side], gx_s.at[side, 1])
    for i in range(1, XN):
        wait(dsum_own, dx_s.at[i])
    for i in range(1, ZN):
        wait(dz.at[0], dz_s.at[i])
        wait(zr.at[i], pz_s.at[i])
        wait(zr.at[i], gz_s.at[i])


def local(queries, keys, values, out_grad, depth_kernel, point_weight, block_of_frame):
    ctx, core = lax.axis_index("ctx"), lax.axis_index("tp") % 2
    chunk = 2 * (ctx // 2) + core
    blocks = block_of_frame.astype(jnp.int32)
    own = lax.dynamic_slice_in_dim(blocks, 2 * chunk, 2)
    own = jnp.repeat(own, FRAME)
    bound = jnp.where(blocks[:, None] <= own[None, :], OPEN, NEG).astype(F32)
    bound = bound.reshape(CN, 2, ROWS)
    kern = jnp.pad(depth_kernel.astype(F32), ((0, 5), (0, 0)))

    vmem = pl.BlockSpec(memory_space=pltpu.VMEM)
    dma = pltpu.SemaphoreType.DMA
    wide = (2, ROWS, COLS)
    scratch = [
        pltpu.VMEM((ROWS, COLS), BF16),
        pltpu.VMEM((2, CN, ROWS, COLS), BF16),
        pltpu.VMEM((TN, ROWS, COLS), BF16),
        pltpu.VMEM((32, COLS), F32),
        pltpu.VMEM((HEADS, 1, ROWS), F32),
        pltpu.VMEM((HEADS, 1, ROWS), F32),
        pltpu.VMEM((HEADS, HD, ROWS), F32),
        pltpu.VMEM((HEADS, 1, ROWS), F32),
        pltpu.VMEM((HEADS, 1, ROWS), F32),
        pltpu.VMEM((2, FRAME, COLS), BF16),
        pltpu.VMEM((4, FRAME, COLS), BF16),
        pltpu.VMEM((4, FRAME, COLS), BF16),
        pltpu.VMEM((3, 4, FRAME + 2 * WW, COLS), F32),
        pltpu.VMEM((ROWS, COLS), BF16),
        pltpu.VMEM((ROWS, COLS), BF16),
        pltpu.VMEM((32, COLS), F32),
        pltpu.VMEM((32, COLS), F32),
        pltpu.VMEM((ROWS, COLS), BF16),
        pltpu.VMEM((HEADS, HD, ROWS), F32),
        pltpu.VMEM(wide, F32),
        pltpu.VMEM((8,) + wide, BF16),
        pltpu.VMEM((8,) + wide, BF16),
        pltpu.VMEM((2, 4) + wide, BF16),
        pltpu.VMEM((2, 4) + wide, BF16),
        pltpu.VMEM((XN, 2, ZN, PIECE, COLS), BF16),
        pltpu.VMEM((2, 3, 2, ZN // 2, PIECE, COLS), BF16),
        pltpu.VMEM((2, 2, ZN // 2, PIECE, COLS), BF16),
        pltpu.VMEM((2, ZN, PIECE, COLS), BF16),
        pltpu.VMEM((ZN, 2, PIECE, COLS), BF16),
        pltpu.VMEM((XN, 2, ZN, PIECE, COLS), BF16),
        pltpu.VMEM((XN, 32, COLS), F32),
        pltpu.VMEM((ZN, 32, COLS), F32),
        pltpu.VMEM((3, ROWS, COLS), BF16),
        pltpu.VMEM((3, ROWS, COLS), BF16),
        dma((9,)), dma((9,)),
        dma((TN,)), dma((TN,)),
        dma((2, 4, 2)), dma((2, 4, 2)),
        dma((8,)), dma((8,)),
        dma((2, 2)), dma((2, 2)),
        dma((2, 4)), dma((2, 4)),
        dma((8,)), dma((8,)),
        dma((2, 3)), dma((2, 3)),
        dma((ZN,)), dma((ZN,)),
        dma((ZN,)), dma((ZN,)),
        dma((2, 2)), dma((2, 2)),
        dma((XN,)), dma((XN,)),
        dma((ZN,)), dma((ZN,)),
    ]
    rows = jax.ShapeDtypeStruct((ROWS, COLS), BF16)
    dq, dk, dv, point, depth = pl.pallas_call(
        body,
        out_shape=(
            rows, rows, rows,
            jax.ShapeDtypeStruct(point_weight.shape, F32),
            jax.ShapeDtypeStruct((32, COLS), F32),
        ),
        in_specs=[vmem] * 7,
        out_specs=(vmem,) * 5,
        scratch_shapes=scratch,
        compiler_params=pltpu.CompilerParams(
            collective_id=0, has_side_effects=True, vmem_limit_bytes=60 * 1024 * 1024
        ),
    )(queries[0], keys[0], values[0], out_grad[0], point_weight, kern, bound)
    return dq[None], dk[None], dv[None], point, depth[:27]


def solution(mesh):
    placed = (
        P("dp", "ctx", "tp"),
        P("dp", "ctx", "tp"),
        P("dp", "ctx", "tp"),
        P("dp", "ctx", "tp"),
        P(None, "tp"),
        P("tp", None),
        P(),
    )
    return jax.shard_map(
        local,
        mesh=mesh,
        in_specs=placed,
        out_specs=(
            P("dp", "ctx", "tp"),
            P("dp", "ctx", "tp"),
            P("dp", "ctx", "tp"),
            P("tp", None),
            P(None, "tp"),
        ),
        check_vma=False,
    )
```

```python
import math

import jax
import jax.numpy as jnp
from jax import lax
from jax.experimental import pallas as pl
from jax.experimental.pallas import tpu as pltpu
from jax.sharding import PartitionSpec as P

HD = 128
HH = 8
WW = 16
FRAME = HH * WW
NEG = -1e30
OPEN = 3e38
MESH = pl.DeviceIdType.MESH
F32 = jnp.float32
BF16 = jnp.bfloat16

ZN = 8
XN = 4
TN = 8
CN = 16
ROWS = 256
COLS = 384
HEADS = COLS // HD
PIECE = COLS // ZN


def wait(ref, sem):
    pltpu.make_async_copy(ref, ref, sem).wait()


def nt(a, b):
    return lax.dot_general(a, b, (((1,), (1,)), ((), ())), preferred_element_type=F32)


def nn(a, b):
    return lax.dot_general(a, b, (((1,), (0,)), ((), ())), preferred_element_type=F32)


def tn(a, b):
    return lax.dot_general(a, b, (((0,), (0,)), ((), ())), preferred_element_type=F32)


def spread_columns(shifted, plain, frame):
    column = lax.broadcasted_iota(jnp.int32, (FRAME, COLS), 0) % WW
    cells = plain[frame].astype(F32)
    shifted[1, frame, WW : WW + FRAME] = cells
    shifted[0, frame, WW : WW + FRAME] = jnp.where(column > 0, pltpu.roll(cells, 1, 0), 0.0)
    shifted[2, frame, WW : WW + FRAME] = jnp.where(
        column < WW - 1, pltpu.roll(cells, FRAME - 1, 0), 0.0
    )


def body(
    q_in, k_in, v_in, g_in, w_ref, kern_in, blocks,
    rows_out, allq, depth_out,
    q, kv, og, kern_send, kern, row_max, row_sum, acc, lse, dots,
    mg_send, mg_ext, at_ext, shifted, mixed, mixed_own, dsum, dsum_own,
    do, dq_acc, terms, xsend, xrecv, sbuf, rbuf,
    prod, xr, relay, qsum, zs, zr, dx, dz, fin, finr,
    swap_s, swap_r, og_s, og_r, ring_s, ring_r, sib_s, sib_r, halo_s, halo_r,
    bs_s, bs_r, bx_s, bx_r, px_s, px_r, pz_s, pz_r, gz_s, gz_r, gx_s, gx_r, gy_s, gy_r,
    dx_s, dx_r, dz_s, dz_r,
):
    ctx, tp, dp = lax.axis_index("ctx"), lax.axis_index("tp"), lax.axis_index("dp")
    z, half = ctx // 2, ctx % 2
    y, core = tp // 2, tp % 2
    chunk = 2 * z + core
    xi = 2 * half + dp
    off = half != core
    same = half == core
    scaling = 1.0 / math.sqrt(HD)
    factor = scaling * math.log2(math.e)

    def at_z(step):
        return (2 * lax.rem(z + step + ZN, ZN) + half, tp, dp)

    def at_x(step):
        place = lax.rem(xi + step + XN, XN)
        return (2 * z + place // 2, tp, lax.rem(place, 2))

    def at_tp(step):
        return (ctx, lax.rem(tp + step, TN), dp)

    sibling = (ctx, 2 * y + 1 - core, dp)
    partner = (2 * z + 1 - half, 2 * y + 1 - core, dp)
    below = lax.rem(z + ZN - 1 + core, ZN)
    above = lax.rem(z + core, ZN)
    prev_dev = (2 * below + half, 2 * y + 1 - core, dp)
    next_dev = (2 * above + half, 2 * y + 1 - core, dp)
    other = lax.rem(z + ZN - 1 + 2 * core, ZN)
    halo_dev = (2 * other + half, 2 * y + 1 - core, dp)

    barrier = pltpu.get_barrier_semaphore()
    peers = [at_tp(i) for i in range(1, TN)]
    peers += [at_z(i) for i in range(1, ZN)]
    peers += [at_x(i) for i in range(1, XN)]
    peers += [partner, halo_dev]
    for device in peers:
        pl.semaphore_signal(barrier, inc=1, device_id=device, device_id_type=MESH)
    pl.semaphore_wait(barrier, len(peers))

    def send(src, dst, send_sem, recv_sem, device):
        pltpu.make_async_remote_copy(
            src_ref=src, dst_ref=dst, send_sem=send_sem, recv_sem=recv_sem,
            device_id=device, device_id_type=MESH,
        ).start()

    def swap(i, src, dst):
        @pl.when(off)
        def _():
            send(src, dst, swap_s.at[i], swap_r.at[i], partner)

        @pl.when(same)
        def _():
            pltpu.make_async_copy(src, dst, swap_r.at[i]).start()

    swap(0, k_in, kv.at[0, ctx])
    swap(1, v_in, kv.at[1, ctx])
    swap(2, q_in, q)
    kern_send[...] = jnp.zeros_like(kern_send)
    kern_send[0:27] = kern_in[...].astype(F32)
    swap(3, kern_send, kern)
    for i in range(1, TN):
        send(g_in, og.at[tp], og_s.at[i], og_r.at[i], at_tp(i))
    keep = pltpu.make_async_copy(g_in, og.at[tp], og_r.at[0])
    keep.start()

    acc[...] = jnp.zeros_like(acc)
    row_sum[...] = jnp.zeros_like(row_sum)
    row_max[...] = jnp.full_like(row_max, NEG)
    dq_acc[...] = jnp.zeros_like(dq_acc)
    shifted[...] = jnp.zeros_like(shifted)
    rbuf[0, 3, 1] = jnp.zeros((ROWS, COLS), BF16)
    rbuf[1, 3, 0] = jnp.zeros((ROWS, COLS), BF16)

    def ring(direction, distance, part, source):
        place = kv.at[part, source]
        send(
            place, place, ring_s.at[direction, distance - 1, part],
            ring_r.at[direction, distance - 1, part], at_z(1 if direction == 0 else -1),
        )

    def ring_wait(direction, distance, part, source):
        wait(kv.at[part, source], ring_r.at[direction, distance - 1, part])

    def to_sibling(slot, source):
        send(kv.at[:, source], kv.at[:, source], sib_s.at[slot], sib_r.at[slot], sibling)

    for part in range(2):
        wait(kv.at[part, chunk], swap_r.at[part])
        ring(0, 1, part, chunk)
        ring(1, 1, part, chunk)
    to_sibling(0, chunk)

    def flip(index):
        return index + 1 - 2 * lax.rem(index, 2)

    lane = lax.broadcasted_iota(jnp.int32, (1, ROWS), 1)
    own_blocks = jnp.where(lane < FRAME, blocks[2 * chunk], blocks[2 * chunk + 1])

    def limits_of(index):
        return [
            jnp.where(own_blocks >= blocks[2 * index + frame], OPEN, NEG).astype(F32)
            for frame in range(2)
        ]

    def fwd_chunk(index):
        @pl.when(index <= chunk + 2)
        def _():
            limits = limits_of(index)
            for head in range(HEADS):
                lanes = slice(head * HD, (head + 1) * HD)
                keys = kv[0, index, :, lanes]
                vals = kv[1, index, :, lanes]
                scores = nt(keys, q[:, lanes])
                scores = jnp.concatenate(
                    [
                        jnp.minimum(scores[:FRAME], limits[0]),
                        jnp.minimum(scores[FRAME:], limits[1]),
                    ],
                    axis=0,
                )
                old = row_max[head]
                new = jnp.maximum(old, jnp.max(scores, axis=0, keepdims=True))
                weights = jnp.exp2(scores * factor - new * factor)
                shrink = jnp.exp2((old - new) * factor)
                row_max[head] = new
                row_sum[head] = row_sum[head] * shrink + jnp.sum(weights, axis=0, keepdims=True)
                acc[head] = acc[head] * shrink + tn(vals, weights.astype(BF16))

    wait(q, swap_r.at[2])

    def near(i, carry):
        @pl.when(i == 1)
        def _():
            wait(kv.at[:, flip(chunk)], sib_r.at[0])

        fwd_chunk(jnp.where(i == 0, chunk, flip(chunk)))
        return carry

    lax.fori_loop(0, 2, near, 0)

    def fwd_step(distance):
        low = 2 * lax.rem(z - distance + ZN, ZN) + core
        high = 2 * lax.rem(z + distance, ZN) + core
        for part in range(2):
            ring_wait(0, distance, part, low)
            if distance < 3 or part == 0:
                ring(0, distance + 1, part, low)
            ring_wait(1, distance, part, high)
            if distance < 3 or part == 1:
                ring(1, distance + 1, part, high)
        to_sibling(distance, low)
        to_sibling(3 + distance, high)

        def step(i, carry):
            @pl.when(i == 2)
            def _():
                wait(kv.at[:, flip(low)], sib_r.at[distance])
                wait(kv.at[:, flip(high)], sib_r.at[3 + distance])

            index = jnp.where(lax.rem(i, 2) == 0, low, high)
            fwd_chunk(jnp.where(i < 2, index, flip(index)))
            return carry

        lax.fori_loop(0, 4, step, 0)

    fwd_step(1)

    keep.wait()
    for i in range(1, TN):
        wait(og.at[lax.rem(tp + TN - i, TN)], og_r.at[i])
    total = nt(og[0], w_ref[:, 0:COLS])
    for i in range(1, TN):
        total += nt(og[i], w_ref[:, i * COLS : (i + 1) * COLS])
    mg_send[...] = total.astype(BF16).reshape(2, FRAME, COLS)
    swap(4, mg_send, mg_ext.at[1:3])

    fwd_step(2)

    def halo(which, ext):
        @pl.when(chunk > 0)
        def _():
            send(ext.at[1], ext.at[3], halo_s.at[which, 0], halo_r.at[which, 0], prev_dev)

        @pl.when(chunk < CN - 1)
        def _():
            send(ext.at[2], ext.at[0], halo_s.at[which, 1], halo_r.at[which, 1], next_dev)

        @pl.when(chunk == 0)
        def _():
            ext[0] = jnp.zeros((FRAME, COLS), BF16)

        @pl.when(chunk == CN - 1)
        def _():
            ext[3] = jnp.zeros((FRAME, COLS), BF16)

    def halo_wait(which, ext):
        @pl.when(chunk > 0)
        def _():
            wait(ext.at[1], halo_s.at[which, 0])
            wait(ext.at[0], halo_r.at[which, 1])

        @pl.when(chunk < CN - 1)
        def _():
            wait(ext.at[2], halo_s.at[which, 1])
            wait(ext.at[3], halo_r.at[which, 0])

    wait(mg_ext.at[1:3], swap_r.at[4])
    halo(0, mg_ext)

    fwd_step(3)

    wait(kern, swap_r.at[3])
    halo_wait(0, mg_ext)
    for frame in range(4):
        spread_columns(shifted, mg_ext, frame)

    def taps():
        return [(a, r, c) for a in (-1, 0, 1) for r in (-1, 0, 1) for c in (-1, 0, 1)]

    for frame in range(2):
        for head in range(HEADS):
            lanes = slice(head * HD, (head + 1) * HD)
            result = jnp.zeros((FRAME, HD), F32)
            for tap, (a, r, c) in enumerate(taps()):
                first = WW - WW * r
                window = shifted[1 - c, frame + 1 - a, first : first + FRAME, lanes]
                result = result + kern[tap : tap + 1, lanes] * window
            do[frame * FRAME : (frame + 1) * FRAME, lanes] = result.astype(BF16)

    last = 2 * lax.rem(z + 4, ZN) + core
    ring_wait(0, 4, 0, last)
    ring_wait(1, 4, 1, last)
    to_sibling(7, last)

    def far(i, carry):
        @pl.when(i == 1)
        def _():
            wait(kv.at[:, flip(last)], sib_r.at[7])

        fwd_chunk(jnp.where(i == 0, last, flip(last)))
        return carry

    lax.fori_loop(0, 2, far, 0)

    for head in range(HEADS):
        lanes = slice(head * HD, (head + 1) * HD)
        sums = row_sum[head]
        lse[head] = row_max[head] * factor + jnp.log(sums) * math.log2(math.e)
        rows = jnp.transpose(acc[head] / sums).astype(BF16)
        at_ext[1, :, lanes] = rows[:FRAME]
        at_ext[2, :, lanes] = rows[FRAME:]
    halo(1, at_ext)

    for frame in (1, 2):
        spread_columns(shifted, at_ext, frame)
    for head in range(HEADS):
        lanes = slice(head * HD, (head + 1) * HD)
        attended = jnp.concatenate([at_ext[1, :, lanes], at_ext[2, :, lanes]], axis=0)
        product = attended.astype(F32) * do[:, lanes].astype(F32)
        dots[head] = jnp.sum(jnp.transpose(product), axis=0, keepdims=True)

    def bwd_chunk(index):
        @pl.when(index > chunk + 2)
        def _():
            terms[...] = jnp.zeros_like(terms)

        @pl.when(index <= chunk + 2)
        def _():
            limits = limits_of(index)
            for head in range(HEADS):
                lanes = slice(head * HD, (head + 1) * HD)
                keys = kv[0, index, :, lanes]
                vals = kv[1, index, :, lanes]
                queries = q[:, lanes]
                grads = do[:, lanes]
                scores = nt(keys, queries)
                scores = jnp.concatenate(
                    [
                        jnp.minimum(scores[:FRAME], limits[0]),
                        jnp.minimum(scores[FRAME:], limits[1]),
                    ],
                    axis=0,
                )
                probs = jnp.exp2(scores * factor - lse[head])
                dscores = (probs * (nt(vals, grads) - dots[head])).astype(BF16)
                terms[1, :, lanes] = nn(probs.astype(BF16), grads)
                terms[0, :, lanes] = nn(dscores, queries) * scaling
                dq_acc[head] = dq_acc[head] + tn(keys, dscores)

    def share(slot):
        xsend[slot] = terms[...].astype(BF16)
        send(xsend.at[slot], xrecv.at[slot], bx_s.at[slot], bx_r.at[slot], sibling)

    def shared(slot):
        wait(xrecv.at[slot], bx_r.at[slot])
        return terms[...] + xrecv[slot].astype(F32)

    target = 2 * lax.rem(z + 4, ZN) + core

    def bwd_pair(slot, index, between):
        def step(i, carry):
            bwd_chunk(jnp.where(i == 0, flip(index), index))

            @pl.when(i == 0)
            def _():
                share(slot)
                between()

            return carry

        lax.fori_loop(0, 2, step, 0)

    def bwd_step(distance, events):
        up = 2 * lax.rem(z + distance, ZN) + core
        down = 2 * lax.rem(z - distance + ZN, ZN) + core

        def step(i, carry):
            side = lax.rem(i, 2)
            index = jnp.where(side == 0, up, down)
            bwd_chunk(jnp.where(i < 2, flip(index), index))
            slot = distance + 3 * side

            @pl.when(i < 2)
            def _():
                share(slot)

            @pl.when(i >= 2)
            def _():
                if distance == 3:
                    wait(rbuf.at[side, 3, side], bs_r.at[side, 3])
                else:
                    wait(rbuf.at[side, distance], bs_r.at[side, distance])
                added = shared(slot) + rbuf[side, distance].astype(F32)
                sbuf[side, distance - 1] = added.astype(BF16)
                goal = lax.rem(z + ZN + 1 - 2 * side, ZN)
                send(
                    sbuf.at[side, distance - 1], rbuf.at[side, distance - 1],
                    bs_s.at[side, distance - 1], bs_r.at[side, distance - 1],
                    (2 * goal + half, tp, dp),
                )

            for place, event in enumerate(events):
                pl.when(i == place)(event)
            return carry

        lax.fori_loop(0, 4, step, 0)

    grad_scale = 1.0 / math.sqrt(2.0 * CN * ROWS)
    across = lax.rem(xi + 2, XN)
    right = lax.rem(xi + 1, XN)
    left = lax.rem(xi + 3, XN)
    lower, upper = slice(0, ZN // 2), slice(ZN // 2, ZN)

    def mix():
        halo_wait(1, at_ext)
        for frame in (0, 3):
            spread_columns(shifted, at_ext, frame)
        dsum[...] = jnp.zeros_like(dsum)
        for frame in range(2):
            for head in range(HEADS):
                lanes = slice(head * HD, (head + 1) * HD)
                result = jnp.zeros((FRAME, HD), F32)
                grad = mg_ext[1 + frame, :, lanes].astype(F32)
                for tap, (a, r, c) in enumerate(taps()):
                    first = WW + WW * r
                    window = shifted[1 + c, frame + 1 + a, first : first + FRAME, lanes]
                    result = result + kern[tap : tap + 1, lanes] * window
                    dsum[tap : tap + 1, lanes] += (
                        jnp.sum(window * grad, axis=0, keepdims=True) * grad_scale
                    )
                mixed[frame * FRAME : (frame + 1) * FRAME, lanes] = result.astype(BF16)
        swap(5, mixed, mixed_own)
        swap(6, dsum, dsum_own)

    def raw_sends(b):
        send(prod.at[across, b, lower], xr.at[b, 0, 0], px_s.at[b, 0, 0], px_r.at[b, 0, 0], at_x(1))
        send(prod.at[across, b, upper], xr.at[b, 1, 0], px_s.at[b, 1, 0], px_r.at[b, 1, 0], at_x(-1))
        send(prod.at[right, b, upper], xr.at[b, 0, 1], px_s.at[b, 0, 1], px_r.at[b, 0, 1], at_x(1))
        send(prod.at[left, b, lower], xr.at[b, 1, 1], px_s.at[b, 1, 1], px_r.at[b, 1, 1], at_x(-1))

    def products():
        wait(mixed_own, swap_r.at[5])
        for b in range(2):

            def product(quarter, carry, b=b):
                block = tn(mixed_own[...], og[2 * quarter + b]) * grad_scale
                prod[quarter, b] = block.astype(BF16).reshape(ZN, PIECE, COLS)
                return carry

            lax.fori_loop(0, XN, product, 0)
            if b == 0:
                raw_sends(0)
        wait(dsum_own, swap_r.at[6])
        for i in range(1, XN):
            send(dsum_own, dx.at[i], dx_s.at[i], dx_r.at[i], at_x(i))

    def relays(b):
        wait(xr.at[b, 0, 0], px_r.at[b, 0, 0])
        relay[b, 0] = (prod[right, b, lower].astype(F32) + xr[b, 0, 0].astype(F32)).astype(BF16)
        send(relay.at[b, 0], xr.at[b, 0, 2], px_s.at[b, 0, 2], px_r.at[b, 0, 2], at_x(1))
        wait(xr.at[b, 1, 0], px_r.at[b, 1, 0])
        relay[b, 1] = (prod[left, b, upper].astype(F32) + xr[b, 1, 0].astype(F32)).astype(BF16)
        send(relay.at[b, 1], xr.at[b, 1, 2], px_s.at[b, 1, 2], px_r.at[b, 1, 2], at_x(-1))

    def z_place(side, distance):
        return lax.rem(z + ZN + (distance if side == 0 else -distance), ZN)

    def z_send(b, side, distance, sums):
        zs[b, side, distance - 1] = sums.astype(BF16)
        send(
            zs.at[b, side, distance - 1], zr.at[b, side, distance - 1],
            pz_s.at[b, side, distance - 1], pz_r.at[b, side, distance - 1],
            at_z(1 if side == 0 else -1),
        )

    def z_first(b):
        for side in range(2):
            for slot in (1, 2):
                wait(xr.at[b, side, slot], px_r.at[b, side, slot])
        qsum[b, lower] = (
            prod[xi, b, lower].astype(F32) + xr[b, 0, 2].astype(F32) + xr[b, 1, 1].astype(F32)
        )
        qsum[b, upper] = (
            prod[xi, b, upper].astype(F32) + xr[b, 0, 1].astype(F32) + xr[b, 1, 2].astype(F32)
        )
        z_send(b, b, 4, qsum[b, z_place(b, 4)])

    def z_arrived(b, side, distance):
        wait(zr.at[b, side, distance - 1], pz_r.at[b, side, distance - 1])
        return zr[b, side, distance - 1].astype(F32)

    def z_next(b, distance):
        for side in (b, 1 - b):
            sums = qsum[b, z_place(side, distance)]
            if distance < 3 or side == b:
                sums = sums + z_arrived(b, side, distance + 1)
            z_send(b, side, distance, sums)

    def pass_z(b, side, distance, place):
        piece = allq.at[xi, b, place]
        send(
            piece, piece, gz_s.at[b, side, distance - 1], gz_r.at[b, side, distance - 1],
            at_z(1 if side == 0 else -1),
        )

    def pass_x(b, slot, place):
        piece = allq.at[xi, b, place]
        for side in range(2):
            send(
                piece, piece, gx_s.at[b, side, slot], gx_r.at[b, side, slot],
                at_x(1 if side == 0 else -1),
            )

    def z_last(b):
        allq[xi, b, z] = (
            qsum[b, z] + z_arrived(b, 0, 1) + z_arrived(b, 1, 1)
        ).astype(BF16)
        for side in range(2):
            pass_z(b, side, 1, z)
        pass_x(b, 0, z)

    def z_gather(b, distance):
        for side in range(2):
            if distance == 4 and side != b:
                continue
            place = z_place(side, -distance)
            wait(allq.at[xi, b, place], gz_r.at[b, side, distance - 1])
            if distance < 3 or (distance == 3 and side == b):
                pass_z(b, side, distance + 1, place)
            pass_x(b, 7 if distance == 4 else distance + 3 * side, place)

    def x_relay(b):
        for slot in range(ZN):
            wait(allq.at[left, b, 0], gx_r.at[b, 0, slot])
        here = allq.at[left, b, lower]
        send(here, here, gy_s.at[b, 0], gy_r.at[b, 0], at_x(1))
        for slot in range(ZN):
            wait(allq.at[right, b, 0], gx_r.at[b, 1, slot])
        here = allq.at[right, b, upper]
        send(here, here, gy_s.at[b, 1], gy_r.at[b, 1], at_x(-1))

    def depth_z():
        sums = dsum_own[...]
        for i in range(1, XN):
            wait(dx.at[i], dx_r.at[i])
            sums = sums + dx[i]
        dz[0] = sums
        for i in range(1, ZN):
            send(dz.at[0], dz.at[i], dz_s.at[i], dz_r.at[i], at_z(i))

    def both(*events):
        def run():
            for event in events:
                event()

        return run

    def ev(f, *values):
        return lambda: f(*values)

    bwd_pair(7, target, mix)
    total = shared(7).astype(BF16)
    sbuf[0, 3, 0] = total[0]
    sbuf[1, 3, 1] = total[1]
    send(sbuf.at[0, 3, 0], rbuf.at[0, 3, 0], bs_s.at[0, 3], bs_r.at[0, 3], at_z(1))
    send(sbuf.at[1, 3, 1], rbuf.at[1, 3, 1], bs_s.at[1, 3], bs_r.at[1, 3], at_z(-1))
    products()
    bwd_step(3, [
        lambda: None, both(ev(relays, 0), ev(raw_sends, 1)), depth_z, lambda: None,
    ])
    bwd_step(2, [
        ev(z_first, 0),
        both(ev(relays, 1), ev(z_next, 0, 3)),
        ev(z_next, 0, 2),
        both(ev(z_next, 0, 1), ev(z_first, 1)),
    ])
    bwd_step(1, [
        both(ev(z_last, 0), ev(z_next, 1, 3)),
        both(ev(z_gather, 0, 1), ev(z_next, 1, 2)),
        both(ev(z_gather, 0, 2), ev(z_next, 1, 1)),
        both(ev(z_gather, 0, 3), ev(z_last, 1)),
    ])
    bwd_pair(0, chunk, both(ev(z_gather, 0, 4), ev(z_gather, 1, 1)))
    for head in range(HEADS):
        lanes = slice(head * HD, (head + 1) * HD)
        fin[0, :, lanes] = (jnp.transpose(dq_acc[head]) * scaling).astype(BF16)
    swap(7, fin.at[0], finr.at[0])
    z_gather(1, 2)
    z_gather(1, 3)
    z_gather(1, 4)
    total = shared(0)
    for side in range(2):
        wait(rbuf.at[side, 0], bs_r.at[side, 0])
        total = total + rbuf[side, 0].astype(F32)
    fin[1:3] = total.astype(BF16)
    swap(8, fin.at[1:3], finr.at[1:3])
    x_relay(0)
    x_relay(1)

    sums = dz[0]
    for i in range(1, ZN):
        wait(dz.at[i], dz_r.at[i])
        sums = sums + dz[i]
    depth_out[...] = sums
    wait(finr.at[0], swap_r.at[7])
    rows_out[0] = finr[0]
    wait(finr.at[1:3], swap_r.at[8])
    rows_out[1:3] = finr[1:3]
    for b in range(2):
        wait(allq.at[across, b, lower], gy_r.at[b, 0])
        wait(allq.at[across, b, upper], gy_r.at[b, 1])

    @pl.when(off)
    def _():
        wait(k_in, swap_s.at[0])
        wait(v_in, swap_s.at[1])
        wait(q_in, swap_s.at[2])
        wait(kern_send, swap_s.at[3])
        wait(mg_send, swap_s.at[4])
        wait(mixed, swap_s.at[5])
        wait(dsum, swap_s.at[6])
        wait(fin.at[0], swap_s.at[7])
        wait(fin.at[1:3], swap_s.at[8])

    for i in range(1, TN):
        wait(g_in, og_s.at[i])
    for direction in range(2):
        for distance in range(1, 5):
            for part in range(2):
                if distance < 4 or part == direction:
                    wait(kv.at[part, chunk], ring_s.at[direction, distance - 1, part])
            if distance < 4:
                wait(sbuf.at[direction, distance - 1], bs_s.at[direction, distance - 1])
        wait(sbuf.at[direction, 3, direction], bs_s.at[direction, 3])
    for slot in range(8):
        wait(kv.at[:, chunk], sib_s.at[slot])
        wait(xsend.at[slot], bx_s.at[slot])
    for i in range(1, XN):
        wait(dsum_own, dx_s.at[i])
    for i in range(1, ZN):
        wait(dz.at[0], dz_s.at[i])
    for b in range(2):
        for side in range(2):
            for slot in range(3):
                wait(relay.at[b, side], px_s.at[b, side, slot])
            for distance in range(1, 5):
                if distance < 4 or side == b:
                    wait(zs.at[b, side, distance - 1], pz_s.at[b, side, distance - 1])
                    wait(zs.at[b, side, distance - 1], gz_s.at[b, side, distance - 1])
            for slot in range(ZN):
                wait(zs.at[b, side, 0], gx_s.at[b, side, slot])
            wait(relay.at[b, side], gy_s.at[b, side])


def finish(rows_ref, quarters, depth_ref, dq_out, dk_out, dv_out, point_out, depth_out):
    dq_out[0] = rows_ref[0]
    dk_out[0] = rows_ref[1]
    dv_out[0] = rows_ref[2]
    for block in range(TN):
        cells = quarters[block // 2, block % 2].reshape(COLS, COLS).astype(F32)
        point_out[:, block * COLS : (block + 1) * COLS] = cells
    depth_out[...] = depth_ref[0:27]


def local(queries, keys, values, out_grad, depth_kernel, point_weight, block_of_frame):
    vmem = pl.BlockSpec(memory_space=pltpu.VMEM)
    dma = pltpu.SemaphoreType.DMA
    wide = (2, ROWS, COLS)
    scratch = [
        pltpu.VMEM((ROWS, COLS), BF16),
        pltpu.VMEM((2, CN, ROWS, COLS), BF16),
        pltpu.VMEM((TN, ROWS, COLS), BF16),
        pltpu.VMEM((32, COLS), F32),
        pltpu.VMEM((32, COLS), F32),
        pltpu.VMEM((HEADS, 1, ROWS), F32),
        pltpu.VMEM((HEADS, 1, ROWS), F32),
        pltpu.VMEM((HEADS, HD, ROWS), F32),
        pltpu.VMEM((HEADS, 1, ROWS), F32),
        pltpu.VMEM((HEADS, 1, ROWS), F32),
        pltpu.VMEM((2, FRAME, COLS), BF16),
        pltpu.VMEM((4, FRAME, COLS), BF16),
        pltpu.VMEM((4, FRAME, COLS), BF16),
        pltpu.VMEM((3, 4, FRAME + 2 * WW, COLS), F32),
        pltpu.VMEM((ROWS, COLS), BF16),
        pltpu.VMEM((ROWS, COLS), BF16),
        pltpu.VMEM((32, COLS), F32),
        pltpu.VMEM((32, COLS), F32),
        pltpu.VMEM((ROWS, COLS), BF16),
        pltpu.VMEM((HEADS, HD, ROWS), F32),
        pltpu.VMEM(wide, F32),
        pltpu.VMEM((8,) + wide, BF16),
        pltpu.VMEM((8,) + wide, BF16),
        pltpu.VMEM((2, 4) + wide, BF16),
        pltpu.VMEM((2, 4) + wide, BF16),
        pltpu.VMEM((XN, 2, ZN, PIECE, COLS), BF16),
        pltpu.VMEM((2, 2, 3, ZN // 2, PIECE, COLS), BF16),
        pltpu.VMEM((2, 2, ZN // 2, PIECE, COLS), BF16),
        pltpu.VMEM((2, ZN, PIECE, COLS), F32),
        pltpu.VMEM((2, 2, 4, PIECE, COLS), BF16),
        pltpu.VMEM((2, 2, 4, PIECE, COLS), BF16),
        pltpu.VMEM((XN, 32, COLS), F32),
        pltpu.VMEM((ZN, 32, COLS), F32),
        pltpu.VMEM((3, ROWS, COLS), BF16),
        pltpu.VMEM((3, ROWS, COLS), BF16),
        dma((9,)), dma((9,)),
        dma((TN,)), dma((TN,)),
        dma((2, 4, 2)), dma((2, 4, 2)),
        dma((8,)), dma((8,)),
        dma((2, 2)), dma((2, 2)),
        dma((2, 4)), dma((2, 4)),
        dma((8,)), dma((8,)),
        dma((2, 2, 3)), dma((2, 2, 3)),
        dma((2, 2, 4)), dma((2, 2, 4)),
        dma((2, 2, 4)), dma((2, 2, 4)),
        dma((2, 2, ZN)), dma((2, 2, ZN)),
        dma((2, 2)), dma((2, 2)),
        dma((XN,)), dma((XN,)),
        dma((ZN,)), dma((ZN,)),
    ]
    rows, quarters, depth = pl.pallas_call(
        body,
        out_shape=(
            jax.ShapeDtypeStruct((3, ROWS, COLS), BF16),
            jax.ShapeDtypeStruct((XN, 2, ZN, PIECE, COLS), BF16),
            jax.ShapeDtypeStruct((32, COLS), F32),
        ),
        in_specs=[vmem] * 6 + [pl.BlockSpec(memory_space=pltpu.SMEM)],
        out_specs=(vmem,) * 3,
        scratch_shapes=scratch,
        compiler_params=pltpu.CompilerParams(
            collective_id=0, has_side_effects=True, vmem_limit_bytes=60 * 1024 * 1024
        ),
        name="layer_backward",
    )(queries[0], keys[0], values[0], out_grad[0], point_weight, depth_kernel, block_of_frame)
    part = jax.ShapeDtypeStruct((1, ROWS, COLS), BF16)
    return pl.pallas_call(
        finish,
        out_shape=(
            part, part, part,
            jax.ShapeDtypeStruct(point_weight.shape, F32),
            jax.ShapeDtypeStruct(depth_kernel.shape, F32),
        ),
        in_specs=[vmem] * 3,
        out_specs=(vmem,) * 5,
        compiler_params=pltpu.CompilerParams(vmem_limit_bytes=32 * 1024 * 1024),
        name="write_outputs",
    )(rows, quarters, depth)


def solution(mesh):
    placed = (
        P("dp", "ctx", "tp"),
        P("dp", "ctx", "tp"),
        P("dp", "ctx", "tp"),
        P("dp", "ctx", "tp"),
        P(None, "tp"),
        P("tp", None),
        P(),
    )
    return jax.shard_map(
        local,
        mesh=mesh,
        in_specs=placed,
        out_specs=(
            P("dp", "ctx", "tp"),
            P("dp", "ctx", "tp"),
            P("dp", "ctx", "tp"),
            P("tp", None),
            P(None, "tp"),
        ),
        check_vma=False,
    )
```

```python
import math

import jax
import jax.numpy as jnp
from jax import lax
from jax.experimental import pallas as pl
from jax.experimental.pallas import tpu as pltpu
from jax.sharding import PartitionSpec as P

HD = 128
HH = 8
WW = 16
FRAME = HH * WW
NEG = -1e30
OPEN = 3e38
MESH = pl.DeviceIdType.MESH
F32 = jnp.float32
BF16 = jnp.bfloat16

ZN = 8
XN = 4
TN = 8
CN = 16
ROWS = 256
COLS = 384
HEADS = COLS // HD
PIECE = COLS // ZN


def wait(ref, sem):
    pltpu.make_async_copy(ref, ref, sem).wait()


def nt(a, b):
    return lax.dot_general(a, b, (((1,), (1,)), ((), ())), preferred_element_type=F32)


def nn(a, b):
    return lax.dot_general(a, b, (((1,), (0,)), ((), ())), preferred_element_type=F32)


def tn(a, b):
    return lax.dot_general(a, b, (((0,), (0,)), ((), ())), preferred_element_type=F32)


def spread_columns(shifted, plain, frame):
    column = lax.broadcasted_iota(jnp.int32, (FRAME, COLS), 0) % WW
    cells = plain[frame].astype(F32)
    shifted[1, frame, WW : WW + FRAME] = cells
    shifted[0, frame, WW : WW + FRAME] = jnp.where(column > 0, pltpu.roll(cells, 1, 0), 0.0)
    shifted[2, frame, WW : WW + FRAME] = jnp.where(
        column < WW - 1, pltpu.roll(cells, FRAME - 1, 0), 0.0
    )


def body(
    q_in, k_in, v_in, g_in, w_in, kern_in, blocks,
    rows_out, quarters_out, depth_out,
    q, kv, og, kern_send, kern, row_max, row_sum, acc, lse, dots,
    w_ref, mg_send, mg_ext, at_ext, shifted, mixed, mixed_all, dsum, dsum_send, ogx,
    do, dq_acc, terms, xsend, xrecv, sbuf, rbuf,
    qsum, zs, zr, allq, dx, dz, depth, fin, finr, out_sem,
    swap_s, swap_r, og_s, og_r, ring_s, ring_r, sib_s, sib_r, halo_s, halo_r,
    bs_s, bs_r, bx_s, bx_r, ox_s, ox_r, oy_s, oy_r, pz_s, pz_r, gz_s, gz_r,
    gx_s, gx_r, gy_s, gy_r, mb_s, mb_r, dx_s, dx_r, dz_s, dz_r,
):
    ctx, tp, dp = lax.axis_index("ctx"), lax.axis_index("tp"), lax.axis_index("dp")
    z, half = ctx // 2, ctx % 2
    y, core = tp // 2, tp % 2
    chunk = 2 * z + core
    xi = 2 * half + dp
    off = half != core
    same = half == core
    scaling = 1.0 / math.sqrt(HD)
    factor = scaling * math.log2(math.e)

    def at_z(step):
        return (2 * lax.rem(z + step + ZN, ZN) + half, tp, dp)

    def at_x(step):
        place = lax.rem(xi + step + XN, XN)
        return (2 * z + place // 2, tp, lax.rem(place, 2))

    def crossed(step):
        place = lax.rem(xi + step + XN, XN)
        return (2 * z + place // 2, 2 * y + 1 - core, lax.rem(place, 2))

    def at_half(step):
        place = lax.rem(xi + step + XN, XN)
        return (2 * z + place // 2, 2 * y + half, lax.rem(place, 2))

    def at_tp(step):
        return (ctx, lax.rem(tp + step, TN), dp)

    sibling = (ctx, 2 * y + 1 - core, dp)
    partner = (2 * z + 1 - half, 2 * y + 1 - core, dp)
    below = lax.rem(z + ZN - 1 + core, ZN)
    above = lax.rem(z + core, ZN)
    prev_dev = (2 * below + half, 2 * y + 1 - core, dp)
    next_dev = (2 * above + half, 2 * y + 1 - core, dp)
    other = lax.rem(z + ZN - 1 + 2 * core, ZN)
    halo_dev = (2 * other + half, 2 * y + 1 - core, dp)

    barrier = pltpu.get_barrier_semaphore()
    peers = [at_tp(i) for i in range(1, TN)]
    peers += [at_z(i) for i in range(1, ZN)]
    peers += [at_x(i) for i in range(1, XN)]
    peers += [crossed(i) for i in range(1, XN)]
    peers += [halo_dev]
    for device in peers:
        pl.semaphore_signal(barrier, inc=1, device_id=device, device_id_type=MESH)
    pl.semaphore_wait(barrier, len(peers))

    def send(src, dst, send_sem, recv_sem, device):
        pltpu.make_async_remote_copy(
            src_ref=src, dst_ref=dst, send_sem=send_sem, recv_sem=recv_sem,
            device_id=device, device_id_type=MESH,
        ).start()

    def swap(i, src, dst):
        @pl.when(off)
        def _():
            send(src, dst, swap_s.at[i], swap_r.at[i], partner)

        @pl.when(same)
        def _():
            pltpu.make_async_copy(src, dst, swap_r.at[i]).start()

    swap(0, k_in, kv.at[0, ctx])
    swap(1, v_in, kv.at[1, ctx])
    swap(2, q_in, q)
    kern_send[...] = jnp.zeros_like(kern_send)
    kern_send[0:27] = kern_in[...].astype(F32)
    swap(3, kern_send, kern)
    for i in range(1, TN):
        send(g_in, og.at[tp], og_s.at[i], og_r.at[i], at_tp(i))
    keep = pltpu.make_async_copy(g_in, og.at[tp], og_r.at[0])
    keep.start()
    weights_in = pltpu.make_async_copy(w_in, w_ref, out_sem.at[0])
    weights_in.start()

    acc[...] = jnp.zeros_like(acc)
    row_sum[...] = jnp.zeros_like(row_sum)
    row_max[...] = jnp.full_like(row_max, NEG)
    dq_acc[...] = jnp.zeros_like(dq_acc)
    shifted[...] = jnp.zeros_like(shifted)
    rbuf[0, 3, 1] = jnp.zeros((ROWS, COLS), BF16)
    rbuf[1, 3, 0] = jnp.zeros((ROWS, COLS), BF16)
    zr[0, 3, 1] = jnp.zeros((PIECE, COLS), BF16)
    zr[1, 3, 0] = jnp.zeros((PIECE, COLS), BF16)
    dsum[...] = jnp.zeros_like(dsum)

    def ring(direction, distance, part, source):
        place = kv.at[part, source]
        send(
            place, place, ring_s.at[direction, distance - 1, part],
            ring_r.at[direction, distance - 1, part], at_z(1 if direction == 0 else -1),
        )

    def ring_wait(direction, distance, part, source):
        wait(kv.at[part, source], ring_r.at[direction, distance - 1, part])

    def to_sibling(slot, source):
        send(kv.at[:, source], kv.at[:, source], sib_s.at[slot], sib_r.at[slot], sibling)

    for part in range(2):
        wait(kv.at[part, chunk], swap_r.at[part])
        ring(0, 1, part, chunk)
        ring(1, 1, part, chunk)
    to_sibling(0, chunk)

    def flip(index):
        return index + 1 - 2 * lax.rem(index, 2)

    lane = lax.broadcasted_iota(jnp.int32, (1, ROWS), 1)
    own_blocks = jnp.where(lane < FRAME, blocks[2 * chunk], blocks[2 * chunk + 1])

    def limits_of(index):
        return [
            jnp.where(own_blocks >= blocks[2 * index + frame], OPEN, NEG).astype(F32)
            for frame in range(2)
        ]

    def fwd_chunk(index):
        @pl.when(index <= chunk + 2)
        def _():
            limits = limits_of(index)
            for head in range(HEADS):
                lanes = slice(head * HD, (head + 1) * HD)
                keys = kv[0, index, :, lanes]
                vals = kv[1, index, :, lanes]
                scores = nt(keys, q[:, lanes])
                scores = jnp.concatenate(
                    [
                        jnp.minimum(scores[:FRAME], limits[0]),
                        jnp.minimum(scores[FRAME:], limits[1]),
                    ],
                    axis=0,
                )
                old = row_max[head]
                new = jnp.maximum(old, jnp.max(scores, axis=0, keepdims=True))
                weights = jnp.exp2(scores * factor - new * factor)
                shrink = jnp.exp2((old - new) * factor)
                row_max[head] = new
                row_sum[head] = row_sum[head] * shrink + jnp.sum(weights, axis=0, keepdims=True)
                acc[head] = acc[head] * shrink + tn(vals, weights.astype(BF16))

    wait(q, swap_r.at[2])

    def near(i, carry):
        @pl.when(i == 1)
        def _():
            wait(kv.at[:, flip(chunk)], sib_r.at[0])

        fwd_chunk(jnp.where(i == 0, chunk, flip(chunk)))
        return carry

    lax.fori_loop(0, 2, near, 0)

    def fwd_step(distance):
        low = 2 * lax.rem(z - distance + ZN, ZN) + core
        high = 2 * lax.rem(z + distance, ZN) + core
        for part in range(2):
            ring_wait(0, distance, part, low)
            if distance < 3 or part == 0:
                ring(0, distance + 1, part, low)
            ring_wait(1, distance, part, high)
            if distance < 3 or part == 1:
                ring(1, distance + 1, part, high)
        to_sibling(distance, low)
        to_sibling(3 + distance, high)

        def step(i, carry):
            @pl.when(i == 2)
            def _():
                wait(kv.at[:, flip(low)], sib_r.at[distance])
                wait(kv.at[:, flip(high)], sib_r.at[3 + distance])

            index = jnp.where(lax.rem(i, 2) == 0, low, high)
            fwd_chunk(jnp.where(i < 2, index, flip(index)))
            return carry

        lax.fori_loop(0, 4, step, 0)

    fwd_step(1)

    keep.wait()
    for i in range(1, TN):
        wait(og.at[lax.rem(tp + TN - i, TN)], og_r.at[i])
    weights_in.wait()
    total = nt(og[0], w_ref[:, 0:COLS])
    for i in range(1, TN):
        total += nt(og[i], w_ref[:, i * COLS : (i + 1) * COLS])
    mg_send[...] = total.astype(BF16).reshape(2, FRAME, COLS)
    swap(4, mg_send, mg_ext.at[1:3])

    quarter = og.at[pl.ds(2 * xi, 2)]
    own_quarter = pltpu.make_async_copy(quarter, ogx.at[xi], ox_r.at[0])
    own_quarter.start()
    for i in range(1, XN):
        goal = lax.rem(xi + i, XN)
        send(og.at[2 * goal + core], ogx.at[xi, core], ox_s.at[i], ox_r.at[i], at_x(i))

    fwd_step(2)

    def halo(which, ext):
        @pl.when(chunk > 0)
        def _():
            send(ext.at[1], ext.at[3], halo_s.at[which, 0], halo_r.at[which, 0], prev_dev)

        @pl.when(chunk < CN - 1)
        def _():
            send(ext.at[2], ext.at[0], halo_s.at[which, 1], halo_r.at[which, 1], next_dev)

        @pl.when(chunk == 0)
        def _():
            ext[0] = jnp.zeros((FRAME, COLS), BF16)

        @pl.when(chunk == CN - 1)
        def _():
            ext[3] = jnp.zeros((FRAME, COLS), BF16)

    def halo_wait(which, ext):
        @pl.when(chunk > 0)
        def _():
            wait(ext.at[1], halo_s.at[which, 0])
            wait(ext.at[0], halo_r.at[which, 1])

        @pl.when(chunk < CN - 1)
        def _():
            wait(ext.at[2], halo_s.at[which, 1])
            wait(ext.at[3], halo_r.at[which, 0])

    wait(mg_ext.at[1:3], swap_r.at[4])
    halo(0, mg_ext)
    for i in range(1, XN):
        place = ogx.at[lax.rem(xi + XN - i, XN), core]
        wait(place, ox_r.at[i])
        send(place, place, oy_s.at[i], oy_r.at[i], sibling)

    fwd_step(3)

    wait(kern, swap_r.at[3])
    halo_wait(0, mg_ext)
    for frame in range(4):
        spread_columns(shifted, mg_ext, frame)

    def taps():
        return [(a, r, c) for a in (-1, 0, 1) for r in (-1, 0, 1) for c in (-1, 0, 1)]

    for frame in range(2):
        for head in range(HEADS):
            lanes = slice(head * HD, (head + 1) * HD)
            result = jnp.zeros((FRAME, HD), F32)
            for tap, (a, r, c) in enumerate(taps()):
                first = WW - WW * r
                window = shifted[1 - c, frame + 1 - a, first : first + FRAME, lanes]
                result = result + kern[tap : tap + 1, lanes] * window
            do[frame * FRAME : (frame + 1) * FRAME, lanes] = result.astype(BF16)

    last = 2 * lax.rem(z + 4, ZN) + core
    ring_wait(0, 4, 0, last)
    ring_wait(1, 4, 1, last)
    to_sibling(7, last)

    def far(i, carry):
        @pl.when(i == 1)
        def _():
            wait(kv.at[:, flip(last)], sib_r.at[7])

        fwd_chunk(jnp.where(i == 0, last, flip(last)))
        return carry

    lax.fori_loop(0, 2, far, 0)

    for head in range(HEADS):
        lanes = slice(head * HD, (head + 1) * HD)
        sums = row_sum[head]
        lse[head] = row_max[head] * factor + jnp.log(sums) * math.log2(math.e)
        rows = jnp.transpose(acc[head] / sums).astype(BF16)
        at_ext[1, :, lanes] = rows[:FRAME]
        at_ext[2, :, lanes] = rows[FRAME:]
    halo(1, at_ext)

    for frame in (1, 2):
        spread_columns(shifted, at_ext, frame)
    for head in range(HEADS):
        lanes = slice(head * HD, (head + 1) * HD)
        attended = jnp.concatenate([at_ext[1, :, lanes], at_ext[2, :, lanes]], axis=0)
        product = attended.astype(F32) * do[:, lanes].astype(F32)
        dots[head] = jnp.sum(jnp.transpose(product), axis=0, keepdims=True)

    def bwd_chunk(index):
        @pl.when(index > chunk + 2)
        def _():
            terms[...] = jnp.zeros_like(terms)

        @pl.when(index <= chunk + 2)
        def _():
            limits = limits_of(index)
            for head in range(HEADS):
                lanes = slice(head * HD, (head + 1) * HD)
                keys = kv[0, index, :, lanes]
                vals = kv[1, index, :, lanes]
                queries = q[:, lanes]
                grads = do[:, lanes]
                scores = nt(keys, queries)
                scores = jnp.concatenate(
                    [
                        jnp.minimum(scores[:FRAME], limits[0]),
                        jnp.minimum(scores[FRAME:], limits[1]),
                    ],
                    axis=0,
                )
                probs = jnp.exp2(scores * factor - lse[head])
                dscores = (probs * (nt(vals, grads) - dots[head])).astype(BF16)
                terms[1, :, lanes] = nn(probs.astype(BF16), grads)
                terms[0, :, lanes] = nn(dscores, queries) * scaling
                dq_acc[head] = dq_acc[head] + tn(keys, dscores)

    def share(slot):
        xsend[slot] = terms[...].astype(BF16)
        send(xsend.at[slot], xrecv.at[slot], bx_s.at[slot], bx_r.at[slot], sibling)

    def shared(slot):
        wait(xrecv.at[slot], bx_r.at[slot])
        return terms[...] + xrecv[slot].astype(F32)

    target = 2 * lax.rem(z + 4, ZN) + core

    def bwd_pair(slot, index, between):
        def step(i, carry):
            bwd_chunk(jnp.where(i == 0, flip(index), index))

            @pl.when(i == 0)
            def _():
                share(slot)
                between()

            return carry

        lax.fori_loop(0, 2, step, 0)

    def bwd_step(distance, events):
        up = 2 * lax.rem(z + distance, ZN) + core
        down = 2 * lax.rem(z - distance + ZN, ZN) + core

        def step(i, carry):
            side = lax.rem(i, 2)
            index = jnp.where(side == 0, up, down)
            bwd_chunk(jnp.where(i < 2, flip(index), index))
            slot = distance + 3 * side

            @pl.when(i < 2)
            def _():
                share(slot)

            @pl.when(i >= 2)
            def _():
                if distance == 3:
                    wait(rbuf.at[side, 3, side], bs_r.at[side, 3, side])
                else:
                    for part in range(2):
                        wait(rbuf.at[side, distance, part], bs_r.at[side, distance, part])
                added = shared(slot) + rbuf[side, distance].astype(F32)
                sbuf[side, distance - 1] = added.astype(BF16)
                goal = lax.rem(z + ZN + 1 - 2 * side, ZN)
                send(
                    sbuf.at[side, distance - 1, 0], rbuf.at[side, distance - 1, 0],
                    bs_s.at[side, distance - 1, 0], bs_r.at[side, distance - 1, 0],
                    (2 * goal + half, tp, dp),
                )

            for place, event in enumerate(events):
                pl.when(i == place)(event)
            return carry

        lax.fori_loop(0, 4, step, 0)

    grad_scale = 1.0 / math.sqrt(2.0 * CN * ROWS)
    across = lax.rem(xi + 2, XN)
    right = lax.rem(xi + 1, XN)
    left = lax.rem(xi + 3, XN)
    lower, upper = slice(0, ZN // 2), slice(ZN // 2, ZN)

    def mix():
        halo_wait(1, at_ext)
        for frame in (0, 3):
            spread_columns(shifted, at_ext, frame)
        for frame in range(2):
            for head in range(HEADS):
                lanes = slice(head * HD, (head + 1) * HD)
                result = jnp.zeros((FRAME, HD), F32)
                for tap, (a, r, c) in enumerate(taps()):
                    first = WW + WW * r
                    window = shifted[1 + c, frame + 1 + a, first : first + FRAME, lanes]
                    result = result + kern[tap : tap + 1, lanes] * window
                mixed[frame * FRAME : (frame + 1) * FRAME, lanes] = result.astype(BF16)
        spread_out(mixed, mixed_all, mb_s, mb_r)

    def spread_out(src, dst, send_sems, recv_sems):
        slot = 2 * core + dp
        for i in range(1, XN):
            send(src, dst.at[slot], send_sems.at[i], recv_sems.at[slot], at_half(i))

        @pl.when(off)
        def _():
            send(src, dst.at[slot], send_sems.at[0], recv_sems.at[slot], sibling)

        @pl.when(same)
        def _():
            pltpu.make_async_copy(src, dst.at[slot], recv_sems.at[slot]).start()

    def tap_sums():
        for head in range(HEADS):
            lanes = slice(head * HD, (head + 1) * HD)
            for tap, (a, r, c) in enumerate(taps()):
                first = WW + WW * r
                sums = jnp.zeros((1, HD), F32)
                for frame in range(2):
                    window = shifted[1 + c, frame + 1 + a, first : first + FRAME, lanes]
                    grad = mg_ext[1 + frame, :, lanes].astype(F32)
                    sums = sums + jnp.sum(window * grad, axis=0, keepdims=True)
                dsum[tap : tap + 1, lanes] = sums * grad_scale
        dsum_send[...] = dsum[...].astype(BF16)
        spread_out(dsum_send, dx, dx_s, dx_r)

    def products():
        own_quarter.wait()
        for i in range(1, XN):
            wait(ogx.at[lax.rem(xi + XN - i, XN), 1 - core], oy_r.at[i])
        for slot in range(XN):
            wait(mixed_all.at[slot], mb_r.at[slot])
            for b in range(2):
                block = (tn(mixed_all[slot], ogx[slot, b]) * grad_scale).reshape(ZN, PIECE, COLS)
                qsum[:, b] = block if slot == 0 else qsum[:, b] + block

    def z_place(side, distance):
        return lax.rem(z + ZN + (distance if side == 0 else -distance), ZN)

    def z_send(side, distance, sums):
        zs[side, distance - 1] = sums.astype(BF16)
        send(
            zs.at[side, distance - 1], zr.at[side, distance - 1],
            pz_s.at[side, distance - 1], pz_r.at[side, distance - 1],
            at_z(1 if side == 0 else -1),
        )

    def z_first():
        sums = qsum[z_place(0, 4)].astype(BF16)
        for side in range(2):
            zs[side, 3, side] = sums[side]
            send(
                zs.at[side, 3, side], zr.at[side, 3, side],
                pz_s.at[side, 3], pz_r.at[side, 3], at_z(1 if side == 0 else -1),
            )

    def z_arrived(side, distance):
        if distance == 4:
            wait(zr.at[side, 3, side], pz_r.at[side, 3])
        else:
            wait(zr.at[side, distance - 1], pz_r.at[side, distance - 1])
        return zr[side, distance - 1].astype(F32)

    def z_next(distance):
        for side in range(2):
            sums = qsum[z_place(side, distance)] + z_arrived(side, distance + 1)
            z_send(side, distance, sums)

    def pass_z(side, distance, piece):
        send(
            piece, piece, gz_s.at[side, distance - 1], gz_r.at[side, distance - 1],
            at_z(1 if side == 0 else -1),
        )

    def pass_x(slot, place):
        piece = allq.at[xi, place]
        for side in range(2):
            send(
                piece, piece, gx_s.at[side, slot], gx_r.at[side, slot],
                at_x(1 if side == 0 else -1),
            )

    def z_last():
        allq[xi, z] = (qsum[z] + z_arrived(0, 1) + z_arrived(1, 1)).astype(BF16)
        for side in range(2):
            pass_z(side, 1, allq.at[xi, z])
        pass_x(0, z)

    def z_gather(distance):
        for side in range(2):
            place = z_place(side, -distance)
            wait(allq.at[xi, place], gz_r.at[side, distance - 1])
            if distance < 3:
                pass_z(side, distance + 1, allq.at[xi, place])
            else:
                pass_z(side, 4, allq.at[xi, place, side])
            pass_x(distance + 3 * side, place)

    def z_gather_far():
        place = z_place(0, 4)
        for side in range(2):
            wait(allq.at[xi, place, side], gz_r.at[side, 3])
        pass_x(7, place)

    def put(quarter, i):
        pltpu.make_async_copy(allq.at[quarter], quarters_out.at[quarter], out_sem.at[i]).start()

    def x_relay():
        put(xi, 1)
        for slot in range(ZN):
            wait(allq.at[left, 0], gx_r.at[0, slot])
        here = allq.at[left, lower]
        send(here, here, gy_s.at[0], gy_r.at[0], at_x(1))
        for slot in range(ZN):
            wait(allq.at[right, 0], gx_r.at[1, slot])
        here = allq.at[right, upper]
        send(here, here, gy_s.at[1], gy_r.at[1], at_x(-1))
        put(left, 2)
        put(right, 3)

    def depth_z():
        for slot in range(XN):
            wait(dx.at[slot], dx_r.at[slot])
        sums = dx[0].astype(F32) + dx[1].astype(F32) + dx[2].astype(F32) + dx[3].astype(F32)
        dz[0] = sums.astype(BF16)
        for i in range(1, ZN):
            send(dz.at[0], dz.at[i], dz_s.at[i], dz_r.at[i], at_z(i))

    def terms_send(side, distance, part):
        def run():
            send(
                sbuf.at[side, distance - 1, part], rbuf.at[side, distance - 1, part],
                bs_s.at[side, distance - 1, part], bs_r.at[side, distance - 1, part],
                at_z(1 if side == 0 else -1),
            )

        return run

    def both(*events):
        def run():
            for event in events:
                event()

        return run

    def ev(f, *values):
        return lambda: f(*values)

    def nothing():
        pass

    bwd_pair(7, target, mix)
    total = shared(7).astype(BF16)
    sbuf[0, 3, 0] = total[0]
    sbuf[1, 3, 1] = total[1]
    terms_send(0, 4, 0)()
    terms_send(1, 4, 1)()
    bwd_step(3, [tap_sums, nothing, nothing, terms_send(0, 3, 1)])
    products()
    z_first()
    terms_send(1, 3, 1)()
    bwd_step(2, [
        ev(z_next, 3),
        both(ev(z_next, 2), depth_z),
        ev(z_next, 1),
        both(z_last, terms_send(0, 2, 1)),
    ])
    bwd_step(1, [
        both(ev(z_gather, 1), terms_send(1, 2, 1)),
        nothing,
        ev(z_gather, 2),
        terms_send(0, 1, 1),
    ])
    terms_send(1, 1, 1)()
    bwd_pair(0, chunk, ev(z_gather, 3))
    for head in range(HEADS):
        lanes = slice(head * HD, (head + 1) * HD)
        fin[0, :, lanes] = (jnp.transpose(dq_acc[head]) * scaling).astype(BF16)
    swap(7, fin.at[0], finr.at[0])
    z_gather_far()
    total = shared(0)
    for side in range(2):
        for part in range(2):
            wait(rbuf.at[side, 0, part], bs_r.at[side, 0, part])
        total = total + rbuf[side, 0].astype(F32)
    fin[1:3] = total.astype(BF16)
    swap(8, fin.at[1:3], finr.at[1:3])
    x_relay()

    sums = dz[0].astype(F32)
    for i in range(1, ZN):
        wait(dz.at[i], dz_r.at[i])
        sums = sums + dz[i].astype(F32)
    depth[...] = sums[0:27]
    depth_copy = pltpu.make_async_copy(depth, depth_out, out_sem.at[5])
    depth_copy.start()
    wait(finr.at[0], swap_r.at[7])
    wait(finr.at[1:3], swap_r.at[8])
    rows_copy = pltpu.make_async_copy(finr, rows_out, out_sem.at[6])
    rows_copy.start()
    wait(allq.at[across, lower], gy_r.at[0])
    wait(allq.at[across, upper], gy_r.at[1])
    put(across, 4)

    @pl.when(off)
    def _():
        wait(k_in, swap_s.at[0])
        wait(v_in, swap_s.at[1])
        wait(q_in, swap_s.at[2])
        wait(kern_send, swap_s.at[3])
        wait(mg_send, swap_s.at[4])
        wait(mixed, mb_s.at[0])
        wait(dsum_send, dx_s.at[0])
        wait(fin.at[0], swap_s.at[7])
        wait(fin.at[1:3], swap_s.at[8])

    for i in range(1, TN):
        wait(g_in, og_s.at[i])
    for direction in range(2):
        for distance in range(1, 5):
            for part in range(2):
                if distance < 4 or part == direction:
                    wait(kv.at[part, chunk], ring_s.at[direction, distance - 1, part])
                    wait(sbuf.at[direction, 0, part], bs_s.at[direction, distance - 1, part])
    for slot in range(8):
        wait(kv.at[:, chunk], sib_s.at[slot])
        wait(xsend.at[slot], bx_s.at[slot])
    for i in range(1, XN):
        wait(mixed, mb_s.at[i])
        wait(dsum_send, dx_s.at[i])
        wait(mixed, ox_s.at[i])
        wait(mixed, oy_s.at[i])
    for i in range(1, ZN):
        wait(dz.at[0], dz_s.at[i])
    for side in range(2):
        for distance in range(1, 4):
            wait(zs.at[side, 0], pz_s.at[side, distance - 1])
            wait(zs.at[side, 0], gz_s.at[side, distance - 1])
        wait(zs.at[side, 3, side], pz_s.at[side, 3])
        wait(zs.at[side, 3, side], gz_s.at[side, 3])
        for slot in range(ZN):
            wait(zs.at[side, 0], gx_s.at[side, slot])
        wait(allq.at[xi, lower], gy_s.at[side])
    for i in range(1, 5):
        wait(allq.at[xi], out_sem.at[i])
    depth_copy.wait()
    rows_copy.wait()


def finish(
    rows_in, quarters, depth_in, dq_out, dk_out, dv_out, point_out, depth_out,
    blocks, cells, load, store, small,
):
    loads = [
        pltpu.make_async_copy(quarters.at[i // 2, :, i % 2], blocks.at[i], load.at[i])
        for i in range(TN)
    ]
    for copy in loads:
        copy.start()
    others = [
        pltpu.make_async_copy(rows_in.at[0], dq_out.at[0], small.at[0]),
        pltpu.make_async_copy(rows_in.at[1], dk_out.at[0], small.at[1]),
        pltpu.make_async_copy(rows_in.at[2], dv_out.at[0], small.at[2]),
        pltpu.make_async_copy(depth_in, depth_out, small.at[3]),
    ]
    for copy in others:
        copy.start()
    stores = []
    for i in range(TN):
        loads[i].wait()
        cells[i] = blocks[i].reshape(COLS, COLS).astype(F32)
        stores.append(
            pltpu.make_async_copy(
                cells.at[i], point_out.at[:, i * COLS : (i + 1) * COLS], store.at[i]
            )
        )
        stores[i].start()
    for copy in stores + others:
        copy.wait()


def local(queries, keys, values, out_grad, depth_kernel, point_weight, block_of_frame):
    vmem = pl.BlockSpec(memory_space=pltpu.VMEM)
    hbm = pl.BlockSpec(memory_space=pl.ANY)
    dma = pltpu.SemaphoreType.DMA
    wide = (2, ROWS, COLS)
    scratch = [
        pltpu.VMEM((ROWS, COLS), BF16),
        pltpu.VMEM((2, CN, ROWS, COLS), BF16),
        pltpu.VMEM((TN, ROWS, COLS), BF16),
        pltpu.VMEM((32, COLS), F32),
        pltpu.VMEM((32, COLS), F32),
        pltpu.VMEM((HEADS, 1, ROWS), F32),
        pltpu.VMEM((HEADS, 1, ROWS), F32),
        pltpu.VMEM((HEADS, HD, ROWS), F32),
        pltpu.VMEM((HEADS, 1, ROWS), F32),
        pltpu.VMEM((HEADS, 1, ROWS), F32),
        pltpu.VMEM(point_weight.shape, BF16),
        pltpu.VMEM((2, FRAME, COLS), BF16),
        pltpu.VMEM((4, FRAME, COLS), BF16),
        pltpu.VMEM((4, FRAME, COLS), BF16),
        pltpu.VMEM((3, 4, FRAME + 2 * WW, COLS), F32),
        pltpu.VMEM((ROWS, COLS), BF16),
        pltpu.VMEM((XN, ROWS, COLS), BF16),
        pltpu.VMEM((32, COLS), F32),
        pltpu.VMEM((32, COLS), BF16),
        pltpu.VMEM((XN, 2, ROWS, COLS), BF16),
        pltpu.VMEM((ROWS, COLS), BF16),
        pltpu.VMEM((HEADS, HD, ROWS), F32),
        pltpu.VMEM(wide, F32),
        pltpu.VMEM((8,) + wide, BF16),
        pltpu.VMEM((8,) + wide, BF16),
        pltpu.VMEM((2, 4) + wide, BF16),
        pltpu.VMEM((2, 4) + wide, BF16),
        pltpu.VMEM((ZN, 2, PIECE, COLS), F32),
        pltpu.VMEM((2, 4, 2, PIECE, COLS), BF16),
        pltpu.VMEM((2, 4, 2, PIECE, COLS), BF16),
        pltpu.VMEM((XN, ZN, 2, PIECE, COLS), BF16),
        pltpu.VMEM((XN, 32, COLS), BF16),
        pltpu.VMEM((ZN, 32, COLS), BF16),
        pltpu.VMEM((27, COLS), F32),
        pltpu.VMEM((3, ROWS, COLS), BF16),
        pltpu.VMEM((3, ROWS, COLS), BF16),
        dma((7,)),
        dma((9,)), dma((9,)),
        dma((TN,)), dma((TN,)),
        dma((2, 4, 2)), dma((2, 4, 2)),
        dma((8,)), dma((8,)),
        dma((2, 2)), dma((2, 2)),
        dma((2, 4, 2)), dma((2, 4, 2)),
        dma((8,)), dma((8,)),
        dma((XN,)), dma((XN,)),
        dma((XN,)), dma((XN,)),
        dma((2, 4)), dma((2, 4)),
        dma((2, 4)), dma((2, 4)),
        dma((2, ZN)), dma((2, ZN)),
        dma((2,)), dma((2,)),
        dma((XN,)), dma((XN,)),
        dma((XN,)), dma((XN,)),
        dma((ZN,)), dma((ZN,)),
    ]
    rows, quarters, depth = pl.pallas_call(
        body,
        out_shape=(
            jax.ShapeDtypeStruct((3, ROWS, COLS), BF16),
            jax.ShapeDtypeStruct((XN, ZN, 2, PIECE, COLS), BF16),
            jax.ShapeDtypeStruct(depth_kernel.shape, F32),
        ),
        in_specs=[hbm] * 5 + [vmem, pl.BlockSpec(memory_space=pltpu.SMEM)],
        out_specs=(hbm,) * 3,
        scratch_shapes=scratch,
        compiler_params=pltpu.CompilerParams(
            collective_id=0, has_side_effects=True, vmem_limit_bytes=60 * 1024 * 1024
        ),
        name="layer_backward",
    )(queries[0], keys[0], values[0], out_grad[0], point_weight, depth_kernel, block_of_frame)
    part = jax.ShapeDtypeStruct((1, ROWS, COLS), BF16)
    return pl.pallas_call(
        finish,
        out_shape=(
            part, part, part,
            jax.ShapeDtypeStruct(point_weight.shape, F32),
            jax.ShapeDtypeStruct(depth_kernel.shape, F32),
        ),
        in_specs=[hbm] * 3,
        out_specs=(hbm,) * 5,
        scratch_shapes=[
            pltpu.VMEM((TN, ZN, PIECE, COLS), BF16),
            pltpu.VMEM((TN, COLS, COLS), F32),
            dma((TN,)), dma((TN,)), dma((4,)),
        ],
        compiler_params=pltpu.CompilerParams(vmem_limit_bytes=32 * 1024 * 1024),
        name="write_outputs",
    )(rows, quarters, depth)


def solution(mesh):
    placed = (
        P("dp", "ctx", "tp"),
        P("dp", "ctx", "tp"),
        P("dp", "ctx", "tp"),
        P("dp", "ctx", "tp"),
        P(None, "tp"),
        P("tp", None),
        P(),
    )
    return jax.shard_map(
        local,
        mesh=mesh,
        in_specs=placed,
        out_specs=(
            P("dp", "ctx", "tp"),
            P("dp", "ctx", "tp"),
            P("dp", "ctx", "tp"),
            P("tp", None),
            P(None, "tp"),
        ),
        check_vma=False,
    )
```

```python
import math

import jax
import jax.numpy as jnp
from jax import lax
from jax.experimental import pallas as pl
from jax.experimental.pallas import tpu as pltpu
from jax.sharding import PartitionSpec as P

HD = 128
HH = 8
WW = 16
FRAME = HH * WW
NEG = -1e30
OPEN = 3e38
MESH = pl.DeviceIdType.MESH
F32 = jnp.float32
BF16 = jnp.bfloat16

ZN = 8
XN = 4
TN = 8
CN = 16
ROWS = 256
COLS = 384
HEADS = COLS // HD
PIECE = COLS // ZN


def wait(ref, sem):
    pltpu.make_async_copy(ref, ref, sem).wait()


def nt(a, b):
    return lax.dot_general(a, b, (((1,), (1,)), ((), ())), preferred_element_type=F32)


def nn(a, b):
    return lax.dot_general(a, b, (((1,), (0,)), ((), ())), preferred_element_type=F32)


def tn(a, b):
    return lax.dot_general(a, b, (((0,), (0,)), ((), ())), preferred_element_type=F32)


def spread_columns(shifted, plain, frame):
    column = lax.broadcasted_iota(jnp.int32, (FRAME, COLS), 0) % WW
    cells = plain[frame].astype(F32)
    shifted[1, frame, WW : WW + FRAME] = cells
    shifted[0, frame, WW : WW + FRAME] = jnp.where(column > 0, pltpu.roll(cells, 1, 0), 0.0)
    shifted[2, frame, WW : WW + FRAME] = jnp.where(
        column < WW - 1, pltpu.roll(cells, FRAME - 1, 0), 0.0
    )


def body(
    q_in, k_in, v_in, g_in, w_in, kern_in, blocks,
    rows_out, quarters_out, depth_out,
    q, kv, og, kern_send, kern, row_max, row_sum, acc, lse, dots,
    w_ref, mg_send, mg_ext, at_ext, shifted, mixed, mixed_all, dsum, dsum_send, ogx,
    do, dq_acc, terms, xsend, xrecv, sbuf, rbuf,
    qsum, zs, zr, allq, dx, dz, depth, fin, finr, out_sem,
    swap_s, swap_r, og_s, og_r, ring_s, ring_r, sib_s, sib_r, halo_s, halo_r,
    bs_s, bs_r, bx_s, bx_r, ox_s, ox_r, oy_s, oy_r, pz_s, pz_r, gz_s, gz_r,
    gx_s, gx_r, gy_s, gy_r, mb_s, mb_r, dx_s, dx_r, dz_s, dz_r,
):
    ctx, tp, dp = lax.axis_index("ctx"), lax.axis_index("tp"), lax.axis_index("dp")
    z, half = ctx // 2, ctx % 2
    y, core = tp // 2, tp % 2
    chunk = 2 * z + core
    xi = 2 * half + dp
    off = half != core
    same = half == core
    scaling = 1.0 / math.sqrt(HD)
    factor = scaling * math.log2(math.e)

    def at_z(step):
        return (2 * lax.rem(z + step + ZN, ZN) + half, tp, dp)

    def at_x(step):
        place = lax.rem(xi + step + XN, XN)
        return (2 * z + place // 2, tp, lax.rem(place, 2))

    def crossed(step):
        place = lax.rem(xi + step + XN, XN)
        return (2 * z + place // 2, 2 * y + 1 - core, lax.rem(place, 2))

    def at_half(step):
        place = lax.rem(xi + step + XN, XN)
        return (2 * z + place // 2, 2 * y + half, lax.rem(place, 2))

    def at_tp(step):
        return (ctx, lax.rem(tp + step, TN), dp)

    sibling = (ctx, 2 * y + 1 - core, dp)
    partner = (2 * z + 1 - half, 2 * y + 1 - core, dp)
    below = lax.rem(z + ZN - 1 + core, ZN)
    above = lax.rem(z + core, ZN)
    prev_dev = (2 * below + half, 2 * y + 1 - core, dp)
    next_dev = (2 * above + half, 2 * y + 1 - core, dp)
    other = lax.rem(z + ZN - 1 + 2 * core, ZN)
    halo_dev = (2 * other + half, 2 * y + 1 - core, dp)

    barrier = pltpu.get_barrier_semaphore()
    peers = [at_tp(i) for i in range(1, TN)]
    peers += [at_z(i) for i in range(1, ZN)]
    peers += [at_x(i) for i in range(1, XN)]
    peers += [crossed(i) for i in range(1, XN)]
    peers += [halo_dev]
    for device in peers:
        pl.semaphore_signal(barrier, inc=1, device_id=device, device_id_type=MESH)
    pl.semaphore_wait(barrier, len(peers))

    def send(src, dst, send_sem, recv_sem, device):
        pltpu.make_async_remote_copy(
            src_ref=src, dst_ref=dst, send_sem=send_sem, recv_sem=recv_sem,
            device_id=device, device_id_type=MESH,
        ).start()

    def swap(i, src, dst):
        @pl.when(off)
        def _():
            send(src, dst, swap_s.at[i], swap_r.at[i], partner)

        @pl.when(same)
        def _():
            pltpu.make_async_copy(src, dst, swap_r.at[i]).start()

    swap(0, k_in, kv.at[0, ctx])
    swap(1, v_in, kv.at[1, ctx])
    swap(2, q_in, q)
    kern_send[...] = jnp.zeros_like(kern_send)
    kern_send[0:27] = kern_in[...].astype(F32)
    swap(3, kern_send, kern)
    for i in range(1, TN):
        send(g_in, og.at[tp], og_s.at[i], og_r.at[i], at_tp(i))
    keep = pltpu.make_async_copy(g_in, og.at[tp], og_r.at[0])
    keep.start()
    weights_in = pltpu.make_async_copy(w_in, w_ref, out_sem.at[0])
    weights_in.start()

    acc[...] = jnp.zeros_like(acc)
    row_sum[...] = jnp.zeros_like(row_sum)
    row_max[...] = jnp.full_like(row_max, NEG)
    dq_acc[...] = jnp.zeros_like(dq_acc)
    shifted[...] = jnp.zeros_like(shifted)
    rbuf[0, 3, 1] = jnp.zeros((ROWS, COLS), BF16)
    rbuf[1, 3, 0] = jnp.zeros((ROWS, COLS), BF16)
    zr[0, 3, 1] = jnp.zeros((PIECE, COLS), BF16)
    zr[1, 3, 0] = jnp.zeros((PIECE, COLS), BF16)
    dsum[...] = jnp.zeros_like(dsum)

    def ring(direction, distance, part, source):
        place = kv.at[part, source]
        send(
            place, place, ring_s.at[direction, distance - 1, part],
            ring_r.at[direction, distance - 1, part], at_z(1 if direction == 0 else -1),
        )

    def ring_wait(direction, distance, part, source):
        wait(kv.at[part, source], ring_r.at[direction, distance - 1, part])

    def to_sibling(slot, source):
        send(kv.at[:, source], kv.at[:, source], sib_s.at[slot], sib_r.at[slot], sibling)

    for part in range(2):
        wait(kv.at[part, chunk], swap_r.at[part])
        ring(0, 1, part, chunk)
        ring(1, 1, part, chunk)
    to_sibling(0, chunk)

    def flip(index):
        return index + 1 - 2 * lax.rem(index, 2)

    lane = lax.broadcasted_iota(jnp.int32, (1, ROWS), 1)
    own_blocks = jnp.where(lane < FRAME, blocks[2 * chunk], blocks[2 * chunk + 1])

    def limits_of(index):
        return [
            jnp.where(own_blocks >= blocks[2 * index + frame], OPEN, NEG).astype(F32)
            for frame in range(2)
        ]

    def fwd_chunk(index):
        @pl.when(index <= chunk + 2)
        def _():
            limits = limits_of(index)
            for head in range(HEADS):
                lanes = slice(head * HD, (head + 1) * HD)
                keys = kv[0, index, :, lanes]
                vals = kv[1, index, :, lanes]
                scores = nt(keys, q[:, lanes])
                scores = jnp.concatenate(
                    [
                        jnp.minimum(scores[:FRAME], limits[0]),
                        jnp.minimum(scores[FRAME:], limits[1]),
                    ],
                    axis=0,
                )
                old = row_max[head]
                new = jnp.maximum(old, jnp.max(scores, axis=0, keepdims=True))
                weights = jnp.exp2(scores * factor - new * factor)
                shrink = jnp.exp2((old - new) * factor)
                row_max[head] = new
                row_sum[head] = row_sum[head] * shrink + jnp.sum(weights, axis=0, keepdims=True)
                acc[head] = acc[head] * shrink + tn(vals, weights.astype(BF16))

    wait(q, swap_r.at[2])

    def near(i, carry):
        @pl.when(i == 1)
        def _():
            wait(kv.at[:, flip(chunk)], sib_r.at[0])

        fwd_chunk(jnp.where(i == 0, chunk, flip(chunk)))
        return carry

    lax.fori_loop(0, 2, near, 0)

    def fwd_step(distance):
        low = 2 * lax.rem(z - distance + ZN, ZN) + core
        high = 2 * lax.rem(z + distance, ZN) + core
        for part in range(2):
            ring_wait(0, distance, part, low)
            if distance < 3 or part == 0:
                ring(0, distance + 1, part, low)
            ring_wait(1, distance, part, high)
            if distance < 3 or part == 1:
                ring(1, distance + 1, part, high)
        to_sibling(distance, low)
        to_sibling(3 + distance, high)

        def step(i, carry):
            @pl.when(i == 2)
            def _():
                wait(kv.at[:, flip(low)], sib_r.at[distance])
                wait(kv.at[:, flip(high)], sib_r.at[3 + distance])

            index = jnp.where(lax.rem(i, 2) == 0, low, high)
            fwd_chunk(jnp.where(i < 2, index, flip(index)))
            return carry

        lax.fori_loop(0, 4, step, 0)

    fwd_step(1)

    keep.wait()
    for i in range(1, TN):
        wait(og.at[lax.rem(tp + TN - i, TN)], og_r.at[i])
    weights_in.wait()
    total = nt(og[0], w_ref[:, 0:COLS])
    for i in range(1, TN):
        total += nt(og[i], w_ref[:, i * COLS : (i + 1) * COLS])
    mg_send[...] = total.astype(BF16).reshape(2, FRAME, COLS)
    swap(4, mg_send, mg_ext.at[1:3])

    quarter = og.at[pl.ds(2 * xi, 2)]
    own_quarter = pltpu.make_async_copy(quarter, ogx.at[xi], ox_r.at[0])
    own_quarter.start()
    for i in range(1, XN):
        goal = lax.rem(xi + i, XN)
        send(og.at[2 * goal + core], ogx.at[xi, core], ox_s.at[i], ox_r.at[i], at_x(i))

    fwd_step(2)

    def halo(which, ext):
        @pl.when(chunk > 0)
        def _():
            send(ext.at[1], ext.at[3], halo_s.at[which, 0], halo_r.at[which, 0], prev_dev)

        @pl.when(chunk < CN - 1)
        def _():
            send(ext.at[2], ext.at[0], halo_s.at[which, 1], halo_r.at[which, 1], next_dev)

        @pl.when(chunk == 0)
        def _():
            ext[0] = jnp.zeros((FRAME, COLS), BF16)

        @pl.when(chunk == CN - 1)
        def _():
            ext[3] = jnp.zeros((FRAME, COLS), BF16)

    def halo_wait(which, ext):
        @pl.when(chunk > 0)
        def _():
            wait(ext.at[1], halo_s.at[which, 0])
            wait(ext.at[0], halo_r.at[which, 1])

        @pl.when(chunk < CN - 1)
        def _():
            wait(ext.at[2], halo_s.at[which, 1])
            wait(ext.at[3], halo_r.at[which, 0])

    wait(mg_ext.at[1:3], swap_r.at[4])
    halo(0, mg_ext)
    for i in range(1, XN):
        place = ogx.at[lax.rem(xi + XN - i, XN), core]
        wait(place, ox_r.at[i])
        send(place, place, oy_s.at[i], oy_r.at[i], sibling)

    fwd_step(3)

    wait(kern, swap_r.at[3])
    halo_wait(0, mg_ext)
    for frame in range(4):
        spread_columns(shifted, mg_ext, frame)

    def taps():
        return [(a, r, c) for a in (-1, 0, 1) for r in (-1, 0, 1) for c in (-1, 0, 1)]

    for frame in range(2):
        for head in range(HEADS):
            lanes = slice(head * HD, (head + 1) * HD)
            result = jnp.zeros((FRAME, HD), F32)
            for tap, (a, r, c) in enumerate(taps()):
                first = WW - WW * r
                window = shifted[1 - c, frame + 1 - a, first : first + FRAME, lanes]
                result = result + kern[tap : tap + 1, lanes] * window
            do[frame * FRAME : (frame + 1) * FRAME, lanes] = result.astype(BF16)

    last = 2 * lax.rem(z + 4, ZN) + core
    ring_wait(0, 4, 0, last)
    ring_wait(1, 4, 1, last)
    to_sibling(7, last)

    def far(i, carry):
        @pl.when(i == 1)
        def _():
            wait(kv.at[:, flip(last)], sib_r.at[7])

        fwd_chunk(jnp.where(i == 0, last, flip(last)))
        return carry

    lax.fori_loop(0, 2, far, 0)

    for head in range(HEADS):
        lanes = slice(head * HD, (head + 1) * HD)
        sums = row_sum[head]
        lse[head] = row_max[head] * factor + jnp.log(sums) * math.log2(math.e)
        rows = jnp.transpose(acc[head] / sums).astype(BF16)
        at_ext[1, :, lanes] = rows[:FRAME]
        at_ext[2, :, lanes] = rows[FRAME:]
    halo(1, at_ext)

    for frame in (1, 2):
        spread_columns(shifted, at_ext, frame)
    for head in range(HEADS):
        lanes = slice(head * HD, (head + 1) * HD)
        attended = jnp.concatenate([at_ext[1, :, lanes], at_ext[2, :, lanes]], axis=0)
        product = attended.astype(F32) * do[:, lanes].astype(F32)
        dots[head] = jnp.sum(jnp.transpose(product), axis=0, keepdims=True)

    def bwd_chunk(index):
        @pl.when(index > chunk + 2)
        def _():
            terms[...] = jnp.zeros_like(terms)

        @pl.when(index <= chunk + 2)
        def _():
            limits = limits_of(index)
            for head in range(HEADS):
                lanes = slice(head * HD, (head + 1) * HD)
                keys = kv[0, index, :, lanes]
                vals = kv[1, index, :, lanes]
                queries = q[:, lanes]
                grads = do[:, lanes]
                scores = nt(keys, queries)
                scores = jnp.concatenate(
                    [
                        jnp.minimum(scores[:FRAME], limits[0]),
                        jnp.minimum(scores[FRAME:], limits[1]),
                    ],
                    axis=0,
                )
                probs = jnp.exp2(scores * factor - lse[head])
                dscores = (probs * (nt(vals, grads) - dots[head])).astype(BF16)
                terms[1, :, lanes] = nn(probs.astype(BF16), grads)
                terms[0, :, lanes] = nn(dscores, queries) * scaling
                dq_acc[head] = dq_acc[head] + tn(keys, dscores)

    def share(slot):
        xsend[slot] = terms[...].astype(BF16)
        send(xsend.at[slot], xrecv.at[slot], bx_s.at[slot], bx_r.at[slot], sibling)

    def shared(slot):
        wait(xrecv.at[slot], bx_r.at[slot])
        return terms[...] + xrecv[slot].astype(F32)

    target = 2 * lax.rem(z + 4, ZN) + core

    def terms_to(side, distance, part, device):
        rows = pl.ds((part % 2) * FRAME, FRAME)
        send(
            sbuf.at[side, distance - 1, part // 2, rows],
            rbuf.at[side, distance - 1, part // 2, rows],
            bs_s.at[side, distance - 1, part], bs_r.at[side, distance - 1, part], device,
        )

    def terms_wait(side, distance, part):
        rows = pl.ds((part % 2) * FRAME, FRAME)
        wait(rbuf.at[side, distance - 1, part // 2, rows], bs_r.at[side, distance - 1, part])

    def terms_wait_far(side, part):
        rows = pl.ds(part * FRAME, FRAME)
        wait(rbuf.at[side, 3, side, rows], bs_r.at[side, 3, 2 * side + part])

    def terms_send(distance, part):
        def run():
            for side in range(2):
                terms_to(side, distance, part, at_z(1 if side == 0 else -1))

        return run

    def bwd_pair(slot, index, between):
        def step(i, carry):
            bwd_chunk(jnp.where(i == 0, flip(index), index))

            @pl.when(i == 0)
            def _():
                share(slot)
                between()

            return carry

        lax.fori_loop(0, 2, step, 0)

    def bwd_step(distance, events):
        up = 2 * lax.rem(z + distance, ZN) + core
        down = 2 * lax.rem(z - distance + ZN, ZN) + core

        def step(i, carry):
            side = lax.rem(i, 2)
            index = jnp.where(side == 0, up, down)
            bwd_chunk(jnp.where(i < 2, flip(index), index))
            slot = distance + 3 * side

            @pl.when(i < 2)
            def _():
                share(slot)

            @pl.when(i >= 2)
            def _():
                if distance == 3:
                    for part in range(2):
                        terms_wait_far(side, part)
                else:
                    for part in range(4):
                        terms_wait(side, distance + 1, part)
                added = shared(slot) + rbuf[side, distance].astype(F32)
                sbuf[side, distance - 1] = added.astype(BF16)
                goal = lax.rem(z + ZN + 1 - 2 * side, ZN)
                terms_to(side, distance, 0, (2 * goal + half, tp, dp))

            for place, event in enumerate(events):
                pl.when(i == place)(event)
            return carry

        lax.fori_loop(0, 4, step, 0)

    grad_scale = 1.0 / math.sqrt(2.0 * CN * ROWS)
    across = lax.rem(xi + 2, XN)
    right = lax.rem(xi + 1, XN)
    left = lax.rem(xi + 3, XN)

    def mix():
        halo_wait(1, at_ext)
        for frame in (0, 3):
            spread_columns(shifted, at_ext, frame)
        for frame in range(2):
            for head in range(HEADS):
                lanes = slice(head * HD, (head + 1) * HD)
                result = jnp.zeros((FRAME, HD), F32)
                for tap, (a, r, c) in enumerate(taps()):
                    first = WW + WW * r
                    window = shifted[1 + c, frame + 1 + a, first : first + FRAME, lanes]
                    result = result + kern[tap : tap + 1, lanes] * window
                mixed[frame * FRAME : (frame + 1) * FRAME, lanes] = result.astype(BF16)
        spread_out(mixed, mixed_all, mb_s, mb_r)

    def spread_out(src, dst, send_sems, recv_sems):
        slot = 2 * core + dp
        for i in range(1, XN):
            send(src, dst.at[slot], send_sems.at[i], recv_sems.at[slot], at_half(i))

        @pl.when(off)
        def _():
            send(src, dst.at[slot], send_sems.at[0], recv_sems.at[slot], sibling)

        @pl.when(same)
        def _():
            pltpu.make_async_copy(src, dst.at[slot], recv_sems.at[slot]).start()

    def tap_sums():
        for head in range(HEADS):
            lanes = slice(head * HD, (head + 1) * HD)
            for tap, (a, r, c) in enumerate(taps()):
                first = WW + WW * r
                sums = jnp.zeros((1, HD), F32)
                for frame in range(2):
                    window = shifted[1 + c, frame + 1 + a, first : first + FRAME, lanes]
                    grad = mg_ext[1 + frame, :, lanes].astype(F32)
                    sums = sums + jnp.sum(window * grad, axis=0, keepdims=True)
                dsum[tap : tap + 1, lanes] = sums * grad_scale
        dsum_send[...] = dsum[...].astype(BF16)
        spread_out(dsum_send, dx, dx_s, dx_r)

    def products():
        own_quarter.wait()
        for i in range(1, XN):
            wait(ogx.at[lax.rem(xi + XN - i, XN), 1 - core], oy_r.at[i])
        for slot in range(XN):
            wait(mixed_all.at[slot], mb_r.at[slot])
            for b in range(2):
                block = (tn(mixed_all[slot], ogx[slot, b]) * grad_scale).reshape(ZN, PIECE, COLS)
                qsum[:, b] = block if slot == 0 else qsum[:, b] + block

    def z_place(side, distance):
        return lax.rem(z + ZN + (distance if side == 0 else -distance), ZN)

    def z_send(side, distance, sums):
        zs[side, distance - 1] = sums.astype(BF16)
        send(
            zs.at[side, distance - 1], zr.at[side, distance - 1],
            pz_s.at[side, distance - 1], pz_r.at[side, distance - 1],
            at_z(1 if side == 0 else -1),
        )

    def z_first():
        sums = qsum[z_place(0, 4)].astype(BF16)
        for side in range(2):
            zs[side, 3, side] = sums[side]
            send(
                zs.at[side, 3, side], zr.at[side, 3, side],
                pz_s.at[side, 3], pz_r.at[side, 3], at_z(1 if side == 0 else -1),
            )

    def z_arrived(side, distance):
        if distance == 4:
            wait(zr.at[side, 3, side], pz_r.at[side, 3])
        else:
            wait(zr.at[side, distance - 1], pz_r.at[side, distance - 1])
        return zr[side, distance - 1].astype(F32)

    def z_next(distance):
        for side in range(2):
            sums = qsum[z_place(side, distance)] + z_arrived(side, distance + 1)
            z_send(side, distance, sums)

    def pass_z(side, distance, piece):
        send(
            piece, piece, gz_s.at[side, distance - 1], gz_r.at[side, distance - 1],
            at_z(1 if side == 0 else -1),
        )

    def pass_x(slot, place):
        piece = allq.at[xi, place]
        for side in range(2):
            send(
                piece, piece, gx_s.at[side, slot], gx_r.at[side, slot],
                at_x(1 if side == 0 else -1),
            )

    def z_last():
        allq[xi, z] = (qsum[z] + z_arrived(0, 1) + z_arrived(1, 1)).astype(BF16)
        for side in range(2):
            pass_z(side, 1, allq.at[xi, z])
        pass_x(0, z)

    def z_gather(distance):
        for side in range(2):
            place = z_place(side, -distance)
            wait(allq.at[xi, place], gz_r.at[side, distance - 1])
            if distance < 3:
                pass_z(side, distance + 1, allq.at[xi, place])
            else:
                pass_z(side, 4, allq.at[xi, place, side])
            pass_x(distance + 3 * side, place)
        if distance == 1:
            x_relay(0)
        else:
            x_relay(distance - 1)
            x_relay(distance + 2)

    def z_gather_far():
        place = z_place(0, 4)
        for side in range(2):
            wait(allq.at[xi, place, side], gz_r.at[side, 3])
        pass_x(7, place)

    def put(quarter, i):
        pltpu.make_async_copy(allq.at[quarter], quarters_out.at[quarter], out_sem.at[i]).start()

    def slot_place(slot):
        if slot == 7:
            return z_place(0, 4)
        return z_place(0, -slot) if slot <= 3 else z_place(0, slot - 3)

    def x_relay(slot):
        place = slot_place(slot)
        wait(allq.at[left, place], gx_r.at[0, slot])
        here = allq.at[left, place, 0]
        send(here, here, gy_s.at[0, slot], gy_r.at[0, slot], at_x(1))
        wait(allq.at[right, place], gx_r.at[1, slot])
        here = allq.at[right, place, 1]
        send(here, here, gy_s.at[1, slot], gy_r.at[1, slot], at_x(-1))

    def depth_z():
        for slot in range(XN):
            wait(dx.at[slot], dx_r.at[slot])
        sums = dx[0].astype(F32) + dx[1].astype(F32) + dx[2].astype(F32) + dx[3].astype(F32)
        dz[0] = sums.astype(BF16)
        for i in range(1, ZN):
            send(dz.at[0], dz.at[i], dz_s.at[i], dz_r.at[i], at_z(i))

    def both(*events):
        def run():
            for event in events:
                event()

        return run

    def ev(f, *values):
        return lambda: f(*values)

    def nothing():
        pass

    bwd_pair(7, target, mix)
    total = shared(7).astype(BF16)
    sbuf[0, 3, 0] = total[0]
    sbuf[1, 3, 1] = total[1]
    for part in range(2):
        terms_to(0, 4, part, at_z(1))
        terms_to(1, 4, 2 + part, at_z(-1))
    bwd_step(3, [tap_sums, nothing, nothing, both(*[terms_send(3, part) for part in (1, 2, 3)])])
    products()
    z_first()
    bwd_step(2, [
        nothing,
        ev(z_next, 3),
        nothing,
        both(ev(z_next, 2), terms_send(2, 1)),
    ])
    bwd_step(1, [
        both(ev(z_next, 1), terms_send(2, 2)),
        both(z_last, terms_send(2, 3)),
        ev(z_gather, 1),
        both(ev(z_gather, 2), terms_send(1, 1)),
    ])
    bwd_pair(0, chunk, both(ev(z_gather, 3), terms_send(1, 2), terms_send(1, 3), depth_z))
    for head in range(HEADS):
        lanes = slice(head * HD, (head + 1) * HD)
        fin[0, :, lanes] = (jnp.transpose(dq_acc[head]) * scaling).astype(BF16)
    swap(7, fin.at[0], finr.at[0])
    z_gather_far()
    put(xi, 1)
    total = shared(0)
    for part in range(2):
        for side in range(2):
            terms_wait(side, 1, 2 * part)
            terms_wait(side, 1, 2 * part + 1)
        done = total[part] + rbuf[0, 0, part].astype(F32) + rbuf[1, 0, part].astype(F32)
        fin[1 + part] = done.astype(BF16)
        swap(8 if part == 0 else 5, fin.at[1 + part], finr.at[1 + part])
        if part == 0:
            x_relay(3)
            x_relay(6)
    x_relay(7)

    sums = dz[0].astype(F32)
    for i in range(1, ZN):
        wait(dz.at[i], dz_r.at[i])
        sums = sums + dz[i].astype(F32)
    depth[...] = sums[0:27]
    depth_copy = pltpu.make_async_copy(depth, depth_out, out_sem.at[5])
    depth_copy.start()
    wait(finr.at[0], swap_r.at[7])
    wait(finr.at[1], swap_r.at[8])
    wait(finr.at[2], swap_r.at[5])
    rows_copy = pltpu.make_async_copy(finr, rows_out, out_sem.at[6])
    rows_copy.start()
    put(left, 2)
    put(right, 3)
    for slot in range(ZN):
        for side in range(2):
            wait(allq.at[across, 0, side], gy_r.at[side, slot])
    put(across, 4)

    @pl.when(off)
    def _():
        wait(k_in, swap_s.at[0])
        wait(v_in, swap_s.at[1])
        wait(q_in, swap_s.at[2])
        wait(kern_send, swap_s.at[3])
        wait(mg_send, swap_s.at[4])
        wait(mixed, mb_s.at[0])
        wait(dsum_send, dx_s.at[0])
        wait(fin.at[0], swap_s.at[7])
        wait(fin.at[1], swap_s.at[8])
        wait(fin.at[2], swap_s.at[5])

    for i in range(1, TN):
        wait(g_in, og_s.at[i])
    for direction in range(2):
        for distance in range(1, 5):
            for part in range(2):
                if distance < 4 or part == direction:
                    wait(kv.at[part, chunk], ring_s.at[direction, distance - 1, part])
                    for rows in range(2):
                        wait(mg_send.at[rows], bs_s.at[direction, distance - 1, 2 * part + rows])
    for slot in range(8):
        wait(kv.at[:, chunk], sib_s.at[slot])
        wait(xsend.at[slot], bx_s.at[slot])
    for i in range(1, XN):
        wait(mixed, mb_s.at[i])
        wait(dsum_send, dx_s.at[i])
        wait(mixed, ox_s.at[i])
        wait(mixed, oy_s.at[i])
    for i in range(1, ZN):
        wait(dz.at[0], dz_s.at[i])
    for side in range(2):
        for distance in range(1, 4):
            wait(zs.at[side, 0], pz_s.at[side, distance - 1])
            wait(zs.at[side, 0], gz_s.at[side, distance - 1])
        wait(zs.at[side, 3, side], pz_s.at[side, 3])
        wait(zs.at[side, 3, side], gz_s.at[side, 3])
        for slot in range(ZN):
            wait(zs.at[side, 0], gx_s.at[side, slot])
            wait(zs.at[side, 0, 0], gy_s.at[side, slot])
    for i in range(1, 5):
        wait(allq.at[xi], out_sem.at[i])
    depth_copy.wait()
    rows_copy.wait()


def finish(
    rows_in, quarters, depth_in, dq_out, dk_out, dv_out, point_out, depth_out,
    blocks, cells, rows, depth, load, store, small,
):
    loads = [
        pltpu.make_async_copy(quarters.at[i // 2, :, i % 2], blocks.at[i], load.at[i])
        for i in range(TN)
    ]
    for copy in loads:
        copy.start()
    rows_load = pltpu.make_async_copy(rows_in, rows, small.at[0])
    rows_load.start()
    depth_load = pltpu.make_async_copy(depth_in, depth, small.at[1])
    depth_load.start()
    stores = []
    for i in range(TN):
        loads[i].wait()
        cells[i] = blocks[i].reshape(COLS, COLS).astype(F32)
        stores.append(
            pltpu.make_async_copy(
                cells.at[i], point_out.at[:, i * COLS : (i + 1) * COLS], store.at[i]
            )
        )
        stores[i].start()
    rows_load.wait()
    depth_load.wait()
    stores += [
        pltpu.make_async_copy(rows.at[0], dq_out.at[0], small.at[2]),
        pltpu.make_async_copy(rows.at[1], dk_out.at[0], small.at[3]),
        pltpu.make_async_copy(rows.at[2], dv_out.at[0], small.at[4]),
        pltpu.make_async_copy(depth, depth_out, small.at[5]),
    ]
    for copy in stores[TN:]:
        copy.start()
    for copy in stores:
        copy.wait()


def local(queries, keys, values, out_grad, depth_kernel, point_weight, block_of_frame):
    vmem = pl.BlockSpec(memory_space=pltpu.VMEM)
    hbm = pl.BlockSpec(memory_space=pl.ANY)
    dma = pltpu.SemaphoreType.DMA
    wide = (2, ROWS, COLS)
    scratch = [
        pltpu.VMEM((ROWS, COLS), BF16),
        pltpu.VMEM((2, CN, ROWS, COLS), BF16),
        pltpu.VMEM((TN, ROWS, COLS), BF16),
        pltpu.VMEM((32, COLS), F32),
        pltpu.VMEM((32, COLS), F32),
        pltpu.VMEM((HEADS, 1, ROWS), F32),
        pltpu.VMEM((HEADS, 1, ROWS), F32),
        pltpu.VMEM((HEADS, HD, ROWS), F32),
        pltpu.VMEM((HEADS, 1, ROWS), F32),
        pltpu.VMEM((HEADS, 1, ROWS), F32),
        pltpu.VMEM(point_weight.shape, BF16),
        pltpu.VMEM((2, FRAME, COLS), BF16),
        pltpu.VMEM((4, FRAME, COLS), BF16),
        pltpu.VMEM((4, FRAME, COLS), BF16),
        pltpu.VMEM((3, 4, FRAME + 2 * WW, COLS), F32),
        pltpu.VMEM((ROWS, COLS), BF16),
        pltpu.VMEM((XN, ROWS, COLS), BF16),
        pltpu.VMEM((32, COLS), F32),
        pltpu.VMEM((32, COLS), BF16),
        pltpu.VMEM((XN, 2, ROWS, COLS), BF16),
        pltpu.VMEM((ROWS, COLS), BF16),
        pltpu.VMEM((HEADS, HD, ROWS), F32),
        pltpu.VMEM(wide, F32),
        pltpu.VMEM((8,) + wide, BF16),
        pltpu.VMEM((8,) + wide, BF16),
        pltpu.VMEM((2, 4) + wide, BF16),
        pltpu.VMEM((2, 4) + wide, BF16),
        pltpu.VMEM((ZN, 2, PIECE, COLS), F32),
        pltpu.VMEM((2, 4, 2, PIECE, COLS), BF16),
        pltpu.VMEM((2, 4, 2, PIECE, COLS), BF16),
        pltpu.VMEM((XN, ZN, 2, PIECE, COLS), BF16),
        pltpu.VMEM((XN, 32, COLS), BF16),
        pltpu.VMEM((ZN, 32, COLS), BF16),
        pltpu.VMEM((27, COLS), F32),
        pltpu.VMEM((3, ROWS, COLS), BF16),
        pltpu.VMEM((3, ROWS, COLS), BF16),
        dma((7,)),
        dma((9,)), dma((9,)),
        dma((TN,)), dma((TN,)),
        dma((2, 4, 2)), dma((2, 4, 2)),
        dma((8,)), dma((8,)),
        dma((2, 2)), dma((2, 2)),
        dma((2, 4, 4)), dma((2, 4, 4)),
        dma((8,)), dma((8,)),
        dma((XN,)), dma((XN,)),
        dma((XN,)), dma((XN,)),
        dma((2, 4)), dma((2, 4)),
        dma((2, 4)), dma((2, 4)),
        dma((2, ZN)), dma((2, ZN)),
        dma((2, ZN)), dma((2, ZN)),
        dma((XN,)), dma((XN,)),
        dma((XN,)), dma((XN,)),
        dma((ZN,)), dma((ZN,)),
    ]
    rows, quarters, depth = pl.pallas_call(
        body,
        out_shape=(
            jax.ShapeDtypeStruct((3, ROWS, COLS), BF16),
            jax.ShapeDtypeStruct((XN, ZN, 2, PIECE, COLS), BF16),
            jax.ShapeDtypeStruct(depth_kernel.shape, F32),
        ),
        in_specs=[hbm] * 5 + [vmem, pl.BlockSpec(memory_space=pltpu.SMEM)],
        out_specs=(hbm,) * 3,
        scratch_shapes=scratch,
        compiler_params=pltpu.CompilerParams(
            collective_id=0, has_side_effects=True, vmem_limit_bytes=60 * 1024 * 1024
        ),
        name="layer_backward",
    )(queries[0], keys[0], values[0], out_grad[0], point_weight, depth_kernel, block_of_frame)
    part = jax.ShapeDtypeStruct((1, ROWS, COLS), BF16)
    return pl.pallas_call(
        finish,
        out_shape=(
            part, part, part,
            jax.ShapeDtypeStruct(point_weight.shape, F32),
            jax.ShapeDtypeStruct(depth_kernel.shape, F32),
        ),
        in_specs=[hbm] * 3,
        out_specs=(hbm,) * 5,
        scratch_shapes=[
            pltpu.VMEM((TN, ZN, PIECE, COLS), BF16),
            pltpu.VMEM((TN, COLS, COLS), F32),
            pltpu.VMEM((3, ROWS, COLS), BF16),
            pltpu.VMEM(depth_kernel.shape, F32),
            dma((TN,)), dma((TN,)), dma((6,)),
        ],
        compiler_params=pltpu.CompilerParams(vmem_limit_bytes=60 * 1024 * 1024),
        name="write_outputs",
    )(rows, quarters, depth)


def solution(mesh):
    placed = (
        P("dp", "ctx", "tp"),
        P("dp", "ctx", "tp"),
        P("dp", "ctx", "tp"),
        P("dp", "ctx", "tp"),
        P(None, "tp"),
        P("tp", None),
        P(),
    )
    return jax.shard_map(
        local,
        mesh=mesh,
        in_specs=placed,
        out_specs=(
            P("dp", "ctx", "tp"),
            P("dp", "ctx", "tp"),
            P("dp", "ctx", "tp"),
            P("tp", None),
            P(None, "tp"),
        ),
        check_vma=False,
    )
```

```python
import math

import jax
import jax.numpy as jnp
from jax import lax
from jax.experimental import pallas as pl
from jax.experimental.pallas import tpu as pltpu
from jax.sharding import PartitionSpec as P

HD = 128
HH = 8
WW = 16
FRAME = HH * WW
NEG = -1e30
OPEN = 3e38
MESH = pl.DeviceIdType.MESH
F32 = jnp.float32
BF16 = jnp.bfloat16

ZN = 8
XN = 4
TN = 8
CN = 16
ROWS = 256
COLS = 384
HEADS = COLS // HD
PIECE = COLS // ZN


def wait(ref, sem):
    pltpu.make_async_copy(ref, ref, sem).wait()


def nt(a, b):
    return lax.dot_general(a, b, (((1,), (1,)), ((), ())), preferred_element_type=F32)


def nn(a, b):
    return lax.dot_general(a, b, (((1,), (0,)), ((), ())), preferred_element_type=F32)


def tn(a, b):
    return lax.dot_general(a, b, (((0,), (0,)), ((), ())), preferred_element_type=F32)


def spread_columns(shifted, plain, frame):
    column = lax.broadcasted_iota(jnp.int32, (FRAME, COLS), 0) % WW
    cells = plain[frame].astype(F32)
    shifted[1, frame, WW : WW + FRAME] = cells
    shifted[0, frame, WW : WW + FRAME] = jnp.where(column > 0, pltpu.roll(cells, 1, 0), 0.0)
    shifted[2, frame, WW : WW + FRAME] = jnp.where(
        column < WW - 1, pltpu.roll(cells, FRAME - 1, 0), 0.0
    )


def body(
    q_in, k_in, v_in, g_in, w_in, kern_in, blocks,
    rows_out, quarters_out, depth_out,
    q, kv, og, kern_send, kern, row_max, row_sum, acc, lse, dots,
    w_ref, mg_send, mg_ext, at_ext, shifted, mixed, mixed_all, dsum, dsum_send, ogx,
    do, dq_acc, terms, xsend, xrecv, sbuf, rbuf,
    qsum, zs, zr, allq, dx, dz, depth, fin, finr, out_sem,
    swap_s, swap_r, og_s, og_r, ring_s, ring_r, sib_s, sib_r, halo_s, halo_r,
    bs_s, bs_r, bx_s, bx_r, ox_s, ox_r, oy_s, oy_r, pz_s, pz_r, gz_s, gz_r,
    gx_s, gx_r, gy_s, gy_r, mb_s, mb_r, dx_s, dx_r, dz_s, dz_r,
):
    ctx, tp, dp = lax.axis_index("ctx"), lax.axis_index("tp"), lax.axis_index("dp")
    z, half = ctx // 2, ctx % 2
    y, core = tp // 2, tp % 2
    chunk = 2 * z + core
    xi = 2 * half + dp
    off = half != core
    same = half == core
    scaling = 1.0 / math.sqrt(HD)
    factor = scaling * math.log2(math.e)

    def at_z(step):
        return (2 * lax.rem(z + step + ZN, ZN) + half, tp, dp)

    def at_x(step):
        place = lax.rem(xi + step + XN, XN)
        return (2 * z + place // 2, tp, lax.rem(place, 2))

    def crossed(step):
        place = lax.rem(xi + step + XN, XN)
        return (2 * z + place // 2, 2 * y + 1 - core, lax.rem(place, 2))

    def at_half(step):
        place = lax.rem(xi + step + XN, XN)
        return (2 * z + place // 2, 2 * y + half, lax.rem(place, 2))

    def at_tp(step):
        return (ctx, lax.rem(tp + step, TN), dp)

    sibling = (ctx, 2 * y + 1 - core, dp)
    partner = (2 * z + 1 - half, 2 * y + 1 - core, dp)
    below = lax.rem(z + ZN - 1 + core, ZN)
    above = lax.rem(z + core, ZN)
    prev_dev = (2 * below + half, 2 * y + 1 - core, dp)
    next_dev = (2 * above + half, 2 * y + 1 - core, dp)
    other = lax.rem(z + ZN - 1 + 2 * core, ZN)
    halo_dev = (2 * other + half, 2 * y + 1 - core, dp)

    barrier = pltpu.get_barrier_semaphore()
    peers = [at_tp(i) for i in range(1, TN)]
    peers += [at_z(i) for i in range(1, ZN)]
    peers += [at_x(i) for i in range(1, XN)]
    peers += [crossed(i) for i in range(1, XN)]
    peers += [halo_dev]
    for device in peers:
        pl.semaphore_signal(barrier, inc=1, device_id=device, device_id_type=MESH)
    pl.semaphore_wait(barrier, len(peers))

    def send(src, dst, send_sem, recv_sem, device):
        pltpu.make_async_remote_copy(
            src_ref=src, dst_ref=dst, send_sem=send_sem, recv_sem=recv_sem,
            device_id=device, device_id_type=MESH,
        ).start()

    def swap(i, src, dst):
        @pl.when(off)
        def _():
            send(src, dst, swap_s.at[i], swap_r.at[i], partner)

        @pl.when(same)
        def _():
            pltpu.make_async_copy(src, dst, swap_r.at[i]).start()

    swap(0, k_in, kv.at[0, ctx])
    swap(1, v_in, kv.at[1, ctx])
    swap(2, q_in, q)
    kern_send[...] = jnp.zeros_like(kern_send)
    kern_send[0:27] = kern_in[...].astype(F32)
    swap(3, kern_send, kern)
    for i in range(1, TN):
        send(g_in, og.at[tp], og_s.at[i], og_r.at[i], at_tp(i))
    keep = pltpu.make_async_copy(g_in, og.at[tp], og_r.at[0])
    keep.start()
    weights_in = pltpu.make_async_copy(w_in, w_ref, out_sem.at[0])
    weights_in.start()

    acc[...] = jnp.zeros_like(acc)
    row_sum[...] = jnp.zeros_like(row_sum)
    row_max[...] = jnp.full_like(row_max, NEG)
    dq_acc[...] = jnp.zeros_like(dq_acc)
    shifted[...] = jnp.zeros_like(shifted)
    rbuf[0, 3, 1] = jnp.zeros((ROWS, COLS), BF16)
    rbuf[1, 3, 0] = jnp.zeros((ROWS, COLS), BF16)
    zr[0, 3, 1] = jnp.zeros((PIECE, COLS), BF16)
    zr[1, 3, 0] = jnp.zeros((PIECE, COLS), BF16)
    dsum[...] = jnp.zeros_like(dsum)

    def ring(direction, distance, part, source):
        place = kv.at[part, source]
        send(
            place, place, ring_s.at[direction, distance - 1, part],
            ring_r.at[direction, distance - 1, part], at_z(1 if direction == 0 else -1),
        )

    def ring_wait(direction, distance, part, source):
        wait(kv.at[part, source], ring_r.at[direction, distance - 1, part])

    def to_sibling(slot, source):
        send(kv.at[:, source], kv.at[:, source], sib_s.at[slot], sib_r.at[slot], sibling)

    for part in range(2):
        wait(kv.at[part, chunk], swap_r.at[part])
        ring(0, 1, part, chunk)
        ring(1, 1, part, chunk)
    to_sibling(0, chunk)

    def flip(index):
        return index + 1 - 2 * lax.rem(index, 2)

    lane = lax.broadcasted_iota(jnp.int32, (1, ROWS), 1)
    own_blocks = jnp.where(lane < FRAME, blocks[2 * chunk], blocks[2 * chunk + 1])

    def limits_of(index):
        return [
            jnp.where(own_blocks >= blocks[2 * index + frame], OPEN, NEG).astype(F32)
            for frame in range(2)
        ]

    def fwd_chunk(index):
        @pl.when(index <= chunk + 2)
        def _():
            limits = limits_of(index)
            for head in range(HEADS):
                lanes = slice(head * HD, (head + 1) * HD)
                keys = kv[0, index, :, lanes]
                vals = kv[1, index, :, lanes]
                scores = nt(keys, q[:, lanes])
                scores = jnp.concatenate(
                    [
                        jnp.minimum(scores[:FRAME], limits[0]),
                        jnp.minimum(scores[FRAME:], limits[1]),
                    ],
                    axis=0,
                )
                old = row_max[head]
                new = jnp.maximum(old, jnp.max(scores, axis=0, keepdims=True))
                weights = jnp.exp2(scores * factor - new * factor)
                shrink = jnp.exp2((old - new) * factor)
                row_max[head] = new
                row_sum[head] = row_sum[head] * shrink + jnp.sum(weights, axis=0, keepdims=True)
                acc[head] = acc[head] * shrink + tn(vals, weights.astype(BF16))

    wait(q, swap_r.at[2])

    def near(i, carry):
        @pl.when(i == 1)
        def _():
            wait(kv.at[:, flip(chunk)], sib_r.at[0])

        fwd_chunk(jnp.where(i == 0, chunk, flip(chunk)))
        return carry

    lax.fori_loop(0, 2, near, 0)

    def fwd_step(distance):
        low = 2 * lax.rem(z - distance + ZN, ZN) + core
        high = 2 * lax.rem(z + distance, ZN) + core
        for part in range(2):
            ring_wait(0, distance, part, low)
            if distance < 3 or part == 0:
                ring(0, distance + 1, part, low)
            ring_wait(1, distance, part, high)
            if distance < 3 or part == 1:
                ring(1, distance + 1, part, high)
        to_sibling(distance, low)
        to_sibling(3 + distance, high)

        def step(i, carry):
            @pl.when(i == 2)
            def _():
                wait(kv.at[:, flip(low)], sib_r.at[distance])
                wait(kv.at[:, flip(high)], sib_r.at[3 + distance])

            index = jnp.where(lax.rem(i, 2) == 0, low, high)
            fwd_chunk(jnp.where(i < 2, index, flip(index)))
            return carry

        lax.fori_loop(0, 4, step, 0)

    fwd_step(1)

    keep.wait()
    for i in range(1, TN):
        wait(og.at[lax.rem(tp + TN - i, TN)], og_r.at[i])
    weights_in.wait()
    total = nt(og[0], w_ref[:, 0:COLS])
    for i in range(1, TN):
        total += nt(og[i], w_ref[:, i * COLS : (i + 1) * COLS])
    mg_send[...] = total.astype(BF16).reshape(2, FRAME, COLS)
    swap(4, mg_send, mg_ext.at[1:3])

    quarter = og.at[pl.ds(2 * xi, 2)]
    own_quarter = pltpu.make_async_copy(quarter, ogx.at[xi], ox_r.at[0])
    own_quarter.start()
    for i in range(1, XN):
        goal = lax.rem(xi + i, XN)
        send(og.at[2 * goal + core], ogx.at[xi, core], ox_s.at[i], ox_r.at[i], at_x(i))

    fwd_step(2)

    def halo(which, ext):
        @pl.when(chunk > 0)
        def _():
            send(ext.at[1], ext.at[3], halo_s.at[which, 0], halo_r.at[which, 0], prev_dev)

        @pl.when(chunk < CN - 1)
        def _():
            send(ext.at[2], ext.at[0], halo_s.at[which, 1], halo_r.at[which, 1], next_dev)

        @pl.when(chunk == 0)
        def _():
            ext[0] = jnp.zeros((FRAME, COLS), BF16)

        @pl.when(chunk == CN - 1)
        def _():
            ext[3] = jnp.zeros((FRAME, COLS), BF16)

    def halo_wait(which, ext):
        @pl.when(chunk > 0)
        def _():
            wait(ext.at[1], halo_s.at[which, 0])
            wait(ext.at[0], halo_r.at[which, 1])

        @pl.when(chunk < CN - 1)
        def _():
            wait(ext.at[2], halo_s.at[which, 1])
            wait(ext.at[3], halo_r.at[which, 0])

    wait(mg_ext.at[1:3], swap_r.at[4])
    halo(0, mg_ext)
    for i in range(1, XN):
        place = ogx.at[lax.rem(xi + XN - i, XN), core]
        wait(place, ox_r.at[i])
        send(place, place, oy_s.at[i], oy_r.at[i], sibling)

    fwd_step(3)

    wait(kern, swap_r.at[3])
    halo_wait(0, mg_ext)
    for frame in range(4):
        spread_columns(shifted, mg_ext, frame)

    def taps():
        return [(a, r, c) for a in (-1, 0, 1) for r in (-1, 0, 1) for c in (-1, 0, 1)]

    for frame in range(2):
        for head in range(HEADS):
            lanes = slice(head * HD, (head + 1) * HD)
            result = jnp.zeros((FRAME, HD), F32)
            for tap, (a, r, c) in enumerate(taps()):
                first = WW - WW * r
                window = shifted[1 - c, frame + 1 - a, first : first + FRAME, lanes]
                result = result + kern[tap : tap + 1, lanes] * window
            do[frame * FRAME : (frame + 1) * FRAME, lanes] = result.astype(BF16)

    last = 2 * lax.rem(z + 4, ZN) + core
    ring_wait(0, 4, 0, last)
    ring_wait(1, 4, 1, last)
    to_sibling(7, last)

    def far(i, carry):
        @pl.when(i == 1)
        def _():
            wait(kv.at[:, flip(last)], sib_r.at[7])

        fwd_chunk(jnp.where(i == 0, last, flip(last)))
        return carry

    lax.fori_loop(0, 2, far, 0)

    for head in range(HEADS):
        lanes = slice(head * HD, (head + 1) * HD)
        sums = row_sum[head]
        lse[head] = row_max[head] * factor + jnp.log(sums) * math.log2(math.e)
        rows = jnp.transpose(acc[head] / sums).astype(BF16)
        at_ext[1, :, lanes] = rows[:FRAME]
        at_ext[2, :, lanes] = rows[FRAME:]
    halo(1, at_ext)

    for head in range(HEADS):
        lanes = slice(head * HD, (head + 1) * HD)
        attended = jnp.concatenate([at_ext[1, :, lanes], at_ext[2, :, lanes]], axis=0)
        product = attended.astype(F32) * do[:, lanes].astype(F32)
        dots[head] = jnp.sum(jnp.transpose(product), axis=0, keepdims=True)

    def bwd_chunk(index):
        @pl.when(index > chunk + 2)
        def _():
            terms[...] = jnp.zeros_like(terms)

        @pl.when(index <= chunk + 2)
        def _():
            limits = limits_of(index)
            for head in range(HEADS):
                lanes = slice(head * HD, (head + 1) * HD)
                keys = kv[0, index, :, lanes]
                vals = kv[1, index, :, lanes]
                queries = q[:, lanes]
                grads = do[:, lanes]
                scores = nt(keys, queries)
                scores = jnp.concatenate(
                    [
                        jnp.minimum(scores[:FRAME], limits[0]),
                        jnp.minimum(scores[FRAME:], limits[1]),
                    ],
                    axis=0,
                )
                probs = jnp.exp2(scores * factor - lse[head])
                dscores = (probs * (nt(vals, grads) - dots[head])).astype(BF16)
                terms[1, :, lanes] = nn(probs.astype(BF16), grads)
                terms[0, :, lanes] = nn(dscores, queries) * scaling
                dq_acc[head] = dq_acc[head] + tn(keys, dscores)

    def share(slot):
        xsend[slot] = terms[...].astype(BF16)
        send(xsend.at[slot], xrecv.at[slot], bx_s.at[slot], bx_r.at[slot], sibling)

    def shared(slot):
        wait(xrecv.at[slot], bx_r.at[slot])
        return terms[...] + xrecv[slot].astype(F32)

    target = 2 * lax.rem(z + 4, ZN) + core

    def terms_to(side, distance, part, device):
        rows = pl.ds((part % 2) * FRAME, FRAME)
        send(
            sbuf.at[side, distance - 1, part // 2, rows],
            rbuf.at[side, distance - 1, part // 2, rows],
            bs_s.at[side, distance - 1, part], bs_r.at[side, distance - 1, part], device,
        )

    def terms_wait(side, distance, part):
        rows = pl.ds((part % 2) * FRAME, FRAME)
        wait(rbuf.at[side, distance - 1, part // 2, rows], bs_r.at[side, distance - 1, part])

    def terms_wait_far(side, part):
        rows = pl.ds(part * FRAME, FRAME)
        wait(rbuf.at[side, 3, side, rows], bs_r.at[side, 3, 2 * side + part])

    def terms_send(distance, part):
        def run():
            for side in range(2):
                terms_to(side, distance, part, at_z(1 if side == 0 else -1))

        return run

    def bwd_pair(slot, index, between):
        def step(i, carry):
            bwd_chunk(jnp.where(i == 0, flip(index), index))

            @pl.when(i == 0)
            def _():
                share(slot)
                between()

            return carry

        lax.fori_loop(0, 2, step, 0)

    def bwd_step(distance, events):
        up = 2 * lax.rem(z + distance, ZN) + core
        down = 2 * lax.rem(z - distance + ZN, ZN) + core

        def step(i, carry):
            side = lax.rem(i, 2)
            index = jnp.where(side == 0, up, down)
            bwd_chunk(jnp.where(i < 2, flip(index), index))
            slot = distance + 3 * side

            @pl.when(i < 2)
            def _():
                share(slot)

            @pl.when(i >= 2)
            def _():
                if distance == 3:
                    for part in range(2):
                        terms_wait_far(side, part)
                else:
                    for part in range(4):
                        terms_wait(side, distance + 1, part)
                added = shared(slot) + rbuf[side, distance].astype(F32)
                sbuf[side, distance - 1] = added.astype(BF16)
                goal = lax.rem(z + ZN + 1 - 2 * side, ZN)
                for part in range(2):
                    terms_to(side, distance, part, (2 * goal + half, tp, dp))

            for place, event in enumerate(events):
                pl.when(i == place)(event)
            return carry

        lax.fori_loop(0, 4, step, 0)

    grad_scale = 1.0 / math.sqrt(2.0 * CN * ROWS)
    across = lax.rem(xi + 2, XN)
    right = lax.rem(xi + 1, XN)
    left = lax.rem(xi + 3, XN)

    def mix():
        halo_wait(1, at_ext)
        for frame in range(4):
            spread_columns(shifted, at_ext, frame)
        for frame in range(2):
            for head in range(HEADS):
                lanes = slice(head * HD, (head + 1) * HD)
                result = jnp.zeros((FRAME, HD), F32)
                for tap, (a, r, c) in enumerate(taps()):
                    first = WW + WW * r
                    window = shifted[1 + c, frame + 1 + a, first : first + FRAME, lanes]
                    result = result + kern[tap : tap + 1, lanes] * window
                mixed[frame * FRAME : (frame + 1) * FRAME, lanes] = result.astype(BF16)
        spread_out(mixed, mixed_all, mb_s, mb_r)

    def spread_out(src, dst, send_sems, recv_sems):
        slot = 2 * core + dp
        for i in range(1, XN):
            send(src, dst.at[slot], send_sems.at[i], recv_sems.at[slot], at_half(i))

        @pl.when(off)
        def _():
            send(src, dst.at[slot], send_sems.at[0], recv_sems.at[slot], sibling)

        @pl.when(same)
        def _():
            pltpu.make_async_copy(src, dst.at[slot], recv_sems.at[slot]).start()

    def tap_sums():
        for head in range(HEADS):
            lanes = slice(head * HD, (head + 1) * HD)
            for tap, (a, r, c) in enumerate(taps()):
                first = WW + WW * r
                sums = jnp.zeros((1, HD), F32)
                for frame in range(2):
                    window = shifted[1 + c, frame + 1 + a, first : first + FRAME, lanes]
                    grad = mg_ext[1 + frame, :, lanes].astype(F32)
                    sums = sums + jnp.sum(window * grad, axis=0, keepdims=True)
                dsum[tap : tap + 1, lanes] = sums * grad_scale
        dsum_send[...] = dsum[...].astype(BF16)
        spread_out(dsum_send, dx, dx_s, dx_r)

    def products():
        own_quarter.wait()
        for i in range(1, XN):
            wait(ogx.at[lax.rem(xi + XN - i, XN), 1 - core], oy_r.at[i])
        for slot in range(XN):
            wait(mixed_all.at[slot], mb_r.at[slot])
            for b in range(2):
                block = (tn(mixed_all[slot], ogx[slot, b]) * grad_scale).reshape(ZN, PIECE, COLS)
                qsum[:, b] = block if slot == 0 else qsum[:, b] + block

    def z_place(side, distance):
        return lax.rem(z + ZN + (distance if side == 0 else -distance), ZN)

    def z_send(side, distance, sums):
        zs[side, distance - 1] = sums.astype(BF16)
        send(
            zs.at[side, distance - 1], zr.at[side, distance - 1],
            pz_s.at[side, distance - 1], pz_r.at[side, distance - 1],
            at_z(1 if side == 0 else -1),
        )

    def z_first():
        sums = qsum[z_place(0, 4)].astype(BF16)
        for side in range(2):
            zs[side, 3, side] = sums[side]
            send(
                zs.at[side, 3, side], zr.at[side, 3, side],
                pz_s.at[side, 3], pz_r.at[side, 3], at_z(1 if side == 0 else -1),
            )

    def z_arrived(side, distance):
        if distance == 4:
            wait(zr.at[side, 3, side], pz_r.at[side, 3])
        else:
            wait(zr.at[side, distance - 1], pz_r.at[side, distance - 1])
        return zr[side, distance - 1].astype(F32)

    def z_next(distance):
        for side in range(2):
            sums = qsum[z_place(side, distance)] + z_arrived(side, distance + 1)
            z_send(side, distance, sums)

    def pass_z(side, distance, piece):
        send(
            piece, piece, gz_s.at[side, distance - 1], gz_r.at[side, distance - 1],
            at_z(1 if side == 0 else -1),
        )

    def pass_x(slot, place):
        piece = allq.at[xi, place]
        for side in range(2):
            send(
                piece, piece, gx_s.at[side, slot], gx_r.at[side, slot],
                at_x(1 if side == 0 else -1),
            )

    def z_last():
        allq[xi, z] = (qsum[z] + z_arrived(0, 1) + z_arrived(1, 1)).astype(BF16)
        for side in range(2):
            pass_z(side, 1, allq.at[xi, z])
        pass_x(0, z)

    def z_gather(distance):
        for side in range(2):
            place = z_place(side, -distance)
            wait(allq.at[xi, place], gz_r.at[side, distance - 1])
            if distance < 3:
                pass_z(side, distance + 1, allq.at[xi, place])
            else:
                pass_z(side, 4, allq.at[xi, place, side])
            pass_x(distance + 3 * side, place)
        if distance == 1:
            x_relay(0)
        else:
            x_relay(distance - 1)
            x_relay(distance + 2)

    def z_gather_far():
        place = z_place(0, 4)
        for side in range(2):
            wait(allq.at[xi, place, side], gz_r.at[side, 3])
        pass_x(7, place)

    def put(quarter, i):
        pltpu.make_async_copy(allq.at[quarter], quarters_out.at[quarter], out_sem.at[i]).start()

    def slot_place(slot):
        if slot == 7:
            return z_place(0, 4)
        return z_place(0, -slot) if slot <= 3 else z_place(0, slot - 3)

    def x_relay(slot):
        place = slot_place(slot)
        wait(allq.at[left, place], gx_r.at[0, slot])
        here = allq.at[left, place, 0]
        send(here, here, gy_s.at[0, slot], gy_r.at[0, slot], at_x(1))
        wait(allq.at[right, place], gx_r.at[1, slot])
        here = allq.at[right, place, 1]
        send(here, here, gy_s.at[1, slot], gy_r.at[1, slot], at_x(-1))

    def depth_z():
        for slot in range(XN):
            wait(dx.at[slot], dx_r.at[slot])
        sums = dx[0].astype(F32) + dx[1].astype(F32) + dx[2].astype(F32) + dx[3].astype(F32)
        dz[0] = sums.astype(BF16)
        for i in range(1, ZN):
            send(dz.at[0], dz.at[i], dz_s.at[i], dz_r.at[i], at_z(i))

    def both(*events):
        def run():
            for event in events:
                event()

        return run

    def ev(f, *values):
        return lambda: f(*values)

    def nothing():
        pass

    bwd_pair(7, target, nothing)
    total = shared(7).astype(BF16)
    sbuf[0, 3, 0] = total[0]
    sbuf[1, 3, 1] = total[1]
    for part in range(2):
        terms_to(0, 4, part, at_z(1))
        terms_to(1, 4, 2 + part, at_z(-1))
    mix()
    bwd_step(3, [nothing, nothing, nothing, both(*[terms_send(3, part) for part in (2, 3)])])
    tap_sums()
    products()
    z_first()
    bwd_step(2, [
        nothing,
        ev(z_next, 3),
        nothing,
        both(ev(z_next, 2), terms_send(2, 2)),
    ])
    bwd_step(1, [
        both(ev(z_next, 1), terms_send(2, 3)),
        z_last,
        ev(z_gather, 1),
        both(ev(z_gather, 2), terms_send(1, 2)),
    ])
    bwd_pair(0, chunk, both(terms_send(1, 3), ev(z_gather, 3), depth_z))
    for head in range(HEADS):
        lanes = slice(head * HD, (head + 1) * HD)
        fin[0, :, lanes] = (jnp.transpose(dq_acc[head]) * scaling).astype(BF16)
    swap(7, fin.at[0], finr.at[0])
    z_gather_far()
    put(xi, 1)
    total = shared(0)
    x_relay(3)
    x_relay(6)
    for part in range(2):
        for side in range(2):
            terms_wait(side, 1, 2 * part)
            terms_wait(side, 1, 2 * part + 1)
        done = total[part] + rbuf[0, 0, part].astype(F32) + rbuf[1, 0, part].astype(F32)
        fin[1 + part] = done.astype(BF16)
        swap(8 if part == 0 else 5, fin.at[1 + part], finr.at[1 + part])
        if part == 0:
            x_relay(7)

    sums = dz[0].astype(F32)
    for i in range(1, ZN):
        wait(dz.at[i], dz_r.at[i])
        sums = sums + dz[i].astype(F32)
    depth[...] = sums[0:27]
    depth_copy = pltpu.make_async_copy(depth, depth_out, out_sem.at[5])
    depth_copy.start()
    wait(finr.at[0], swap_r.at[7])
    wait(finr.at[1], swap_r.at[8])
    wait(finr.at[2], swap_r.at[5])
    rows_copy = pltpu.make_async_copy(finr, rows_out, out_sem.at[6])
    rows_copy.start()
    put(left, 2)
    put(right, 3)
    for slot in range(ZN):
        for side in range(2):
            wait(allq.at[across, 0, side], gy_r.at[side, slot])
    put(across, 4)

    @pl.when(off)
    def _():
        wait(k_in, swap_s.at[0])
        wait(v_in, swap_s.at[1])
        wait(q_in, swap_s.at[2])
        wait(kern_send, swap_s.at[3])
        wait(mg_send, swap_s.at[4])
        wait(mixed, mb_s.at[0])
        wait(dsum_send, dx_s.at[0])
        wait(fin.at[0], swap_s.at[7])
        wait(fin.at[1], swap_s.at[8])
        wait(fin.at[2], swap_s.at[5])

    for i in range(1, TN):
        wait(g_in, og_s.at[i])
    for direction in range(2):
        for distance in range(1, 5):
            for part in range(2):
                if distance < 4 or part == direction:
                    wait(kv.at[part, chunk], ring_s.at[direction, distance - 1, part])
                    for rows in range(2):
                        wait(mg_send.at[rows], bs_s.at[direction, distance - 1, 2 * part + rows])
    for slot in range(8):
        wait(kv.at[:, chunk], sib_s.at[slot])
        wait(xsend.at[slot], bx_s.at[slot])
    for i in range(1, XN):
        wait(mixed, mb_s.at[i])
        wait(dsum_send, dx_s.at[i])
        wait(mixed, ox_s.at[i])
        wait(mixed, oy_s.at[i])
    for i in range(1, ZN):
        wait(dz.at[0], dz_s.at[i])
    for side in range(2):
        for distance in range(1, 4):
            wait(zs.at[side, 0], pz_s.at[side, distance - 1])
            wait(zs.at[side, 0], gz_s.at[side, distance - 1])
        wait(zs.at[side, 3, side], pz_s.at[side, 3])
        wait(zs.at[side, 3, side], gz_s.at[side, 3])
        for slot in range(ZN):
            wait(zs.at[side, 0], gx_s.at[side, slot])
            wait(zs.at[side, 0, 0], gy_s.at[side, slot])
    for i in range(1, 5):
        wait(allq.at[xi], out_sem.at[i])
    depth_copy.wait()
    rows_copy.wait()


def finish(
    rows_in, quarters, depth_in, dq_out, dk_out, dv_out, point_out, depth_out,
    blocks, cells, rows, depth, load, store, small,
):
    loads = [
        pltpu.make_async_copy(quarters.at[i // 2, :, i % 2], blocks.at[i], load.at[i])
        for i in range(TN)
    ]
    rows_load = pltpu.make_async_copy(rows_in, rows, small.at[0])
    rows_load.start()
    depth_load = pltpu.make_async_copy(depth_in, depth, small.at[1])
    depth_load.start()
    for copy in loads:
        copy.start()
    rows_load.wait()
    depth_load.wait()
    stores = [
        pltpu.make_async_copy(rows.at[0], dq_out.at[0], small.at[2]),
        pltpu.make_async_copy(rows.at[1], dk_out.at[0], small.at[3]),
        pltpu.make_async_copy(rows.at[2], dv_out.at[0], small.at[4]),
        pltpu.make_async_copy(depth, depth_out, small.at[5]),
    ]
    for copy in stores:
        copy.start()
    for i in range(TN):
        loads[i].wait()
        cells[i] = blocks[i].reshape(COLS, COLS).astype(F32)
        stores.append(
            pltpu.make_async_copy(
                cells.at[i], point_out.at[:, i * COLS : (i + 1) * COLS], store.at[i]
            )
        )
        stores[-1].start()
    for copy in stores:
        copy.wait()


def local(queries, keys, values, out_grad, depth_kernel, point_weight, block_of_frame):
    vmem = pl.BlockSpec(memory_space=pltpu.VMEM)
    hbm = pl.BlockSpec(memory_space=pl.ANY)
    dma = pltpu.SemaphoreType.DMA
    wide = (2, ROWS, COLS)
    scratch = [
        pltpu.VMEM((ROWS, COLS), BF16),
        pltpu.VMEM((2, CN, ROWS, COLS), BF16),
        pltpu.VMEM((TN, ROWS, COLS), BF16),
        pltpu.VMEM((32, COLS), F32),
        pltpu.VMEM((32, COLS), F32),
        pltpu.VMEM((HEADS, 1, ROWS), F32),
        pltpu.VMEM((HEADS, 1, ROWS), F32),
        pltpu.VMEM((HEADS, HD, ROWS), F32),
        pltpu.VMEM((HEADS, 1, ROWS), F32),
        pltpu.VMEM((HEADS, 1, ROWS), F32),
        pltpu.VMEM(point_weight.shape, BF16),
        pltpu.VMEM((2, FRAME, COLS), BF16),
        pltpu.VMEM((4, FRAME, COLS), BF16),
        pltpu.VMEM((4, FRAME, COLS), BF16),
        pltpu.VMEM((3, 4, FRAME + 2 * WW, COLS), F32),
        pltpu.VMEM((ROWS, COLS), BF16),
        pltpu.VMEM((XN, ROWS, COLS), BF16),
        pltpu.VMEM((32, COLS), F32),
        pltpu.VMEM((32, COLS), BF16),
        pltpu.VMEM((XN, 2, ROWS, COLS), BF16),
        pltpu.VMEM((ROWS, COLS), BF16),
        pltpu.VMEM((HEADS, HD, ROWS), F32),
        pltpu.VMEM(wide, F32),
        pltpu.VMEM((8,) + wide, BF16),
        pltpu.VMEM((8,) + wide, BF16),
        pltpu.VMEM((2, 4) + wide, BF16),
        pltpu.VMEM((2, 4) + wide, BF16),
        pltpu.VMEM((ZN, 2, PIECE, COLS), F32),
        pltpu.VMEM((2, 4, 2, PIECE, COLS), BF16),
        pltpu.VMEM((2, 4, 2, PIECE, COLS), BF16),
        pltpu.VMEM((XN, ZN, 2, PIECE, COLS), BF16),
        pltpu.VMEM((XN, 32, COLS), BF16),
        pltpu.VMEM((ZN, 32, COLS), BF16),
        pltpu.VMEM((27, COLS), F32),
        pltpu.VMEM((3, ROWS, COLS), BF16),
        pltpu.VMEM((3, ROWS, COLS), BF16),
        dma((7,)),
        dma((9,)), dma((9,)),
        dma((TN,)), dma((TN,)),
        dma((2, 4, 2)), dma((2, 4, 2)),
        dma((8,)), dma((8,)),
        dma((2, 2)), dma((2, 2)),
        dma((2, 4, 4)), dma((2, 4, 4)),
        dma((8,)), dma((8,)),
        dma((XN,)), dma((XN,)),
        dma((XN,)), dma((XN,)),
        dma((2, 4)), dma((2, 4)),
        dma((2, 4)), dma((2, 4)),
        dma((2, ZN)), dma((2, ZN)),
        dma((2, ZN)), dma((2, ZN)),
        dma((XN,)), dma((XN,)),
        dma((XN,)), dma((XN,)),
        dma((ZN,)), dma((ZN,)),
    ]
    rows, quarters, depth = pl.pallas_call(
        body,
        out_shape=(
            jax.ShapeDtypeStruct((3, ROWS, COLS), BF16),
            jax.ShapeDtypeStruct((XN, ZN, 2, PIECE, COLS), BF16),
            jax.ShapeDtypeStruct(depth_kernel.shape, F32),
        ),
        in_specs=[hbm] * 5 + [vmem, pl.BlockSpec(memory_space=pltpu.SMEM)],
        out_specs=(hbm,) * 3,
        scratch_shapes=scratch,
        compiler_params=pltpu.CompilerParams(
            collective_id=0, has_side_effects=True, vmem_limit_bytes=60 * 1024 * 1024
        ),
        name="layer_backward",
    )(queries[0], keys[0], values[0], out_grad[0], point_weight, depth_kernel, block_of_frame)
    part = jax.ShapeDtypeStruct((1, ROWS, COLS), BF16)
    return pl.pallas_call(
        finish,
        out_shape=(
            part, part, part,
            jax.ShapeDtypeStruct(point_weight.shape, F32),
            jax.ShapeDtypeStruct(depth_kernel.shape, F32),
        ),
        in_specs=[hbm] * 3,
        out_specs=(hbm,) * 5,
        scratch_shapes=[
            pltpu.VMEM((TN, ZN, PIECE, COLS), BF16),
            pltpu.VMEM((TN, COLS, COLS), F32),
            pltpu.VMEM((3, ROWS, COLS), BF16),
            pltpu.VMEM(depth_kernel.shape, F32),
            dma((TN,)), dma((TN,)), dma((6,)),
        ],
        compiler_params=pltpu.CompilerParams(vmem_limit_bytes=60 * 1024 * 1024),
        name="write_outputs",
    )(rows, quarters, depth)


def solution(mesh):
    placed = (
        P("dp", "ctx", "tp"),
        P("dp", "ctx", "tp"),
        P("dp", "ctx", "tp"),
        P("dp", "ctx", "tp"),
        P(None, "tp"),
        P("tp", None),
        P(),
    )
    return jax.shard_map(
        local,
        mesh=mesh,
        in_specs=placed,
        out_specs=(
            P("dp", "ctx", "tp"),
            P("dp", "ctx", "tp"),
            P("dp", "ctx", "tp"),
            P("tp", None),
            P(None, "tp"),
        ),
        check_vma=False,
    )
```

```python
import math

import jax
import jax.numpy as jnp
from jax import lax
from jax.experimental import pallas as pl
from jax.experimental.pallas import tpu as pltpu
from jax.sharding import PartitionSpec as P

HD = 128
HH = 8
WW = 16
FRAME = HH * WW
NEG = -1e30
OPEN = 3e38
MESH = pl.DeviceIdType.MESH
F32 = jnp.float32
BF16 = jnp.bfloat16

ZN = 8
XN = 4
TN = 8
CN = 16
ROWS = 256
COLS = 384
HEADS = COLS // HD
PIECE = COLS // ZN


def wait(ref, sem):
    pltpu.make_async_copy(ref, ref, sem).wait()


def nt(a, b):
    return lax.dot_general(a, b, (((1,), (1,)), ((), ())), preferred_element_type=F32)


def nn(a, b):
    return lax.dot_general(a, b, (((1,), (0,)), ((), ())), preferred_element_type=F32)


def tn(a, b):
    return lax.dot_general(a, b, (((0,), (0,)), ((), ())), preferred_element_type=F32)


def spread_columns(shifted, plain, frame):
    column = lax.broadcasted_iota(jnp.int32, (FRAME, COLS), 0) % WW
    cells = plain[frame].astype(F32)
    shifted[1, frame, WW : WW + FRAME] = cells
    shifted[0, frame, WW : WW + FRAME] = jnp.where(column > 0, pltpu.roll(cells, 1, 0), 0.0)
    shifted[2, frame, WW : WW + FRAME] = jnp.where(
        column < WW - 1, pltpu.roll(cells, FRAME - 1, 0), 0.0
    )


def body(
    q_in, k_in, v_in, g_in, w_in, kern_in, blocks,
    rows_out, quarters_out, depth_out,
    q, kv, og, kern_send, kern, row_max, row_sum, acc, lse, dots,
    w_ref, mg_send, mg_ext, at_ext, shifted, mixed, mixed_all, dsum, dsum_send, ogx,
    do, dq_acc, terms, xsend, xrecv, sbuf, rbuf,
    qsum, zs, zr, allq, dx, dz, depth, fin, finr, out_sem,
    swap_s, swap_r, og_s, og_r, ring_s, ring_r, sib_s, sib_r, halo_s, halo_r,
    bs_s, bs_r, bx_s, bx_r, ox_s, ox_r, oy_s, oy_r, pz_s, pz_r, gz_s, gz_r,
    gx_s, gx_r, gy_s, gy_r, mb_s, mb_r, dx_s, dx_r, dz_s, dz_r,
):
    ctx, tp, dp = lax.axis_index("ctx"), lax.axis_index("tp"), lax.axis_index("dp")
    z, half = ctx // 2, ctx % 2
    y, core = tp // 2, tp % 2
    chunk = 2 * z + core
    xi = 2 * half + dp
    off = half != core
    same = half == core
    scaling = 1.0 / math.sqrt(HD)
    factor = scaling * math.log2(math.e)

    def at_z(step):
        return (2 * lax.rem(z + step + ZN, ZN) + half, tp, dp)

    def at_x(step):
        place = lax.rem(xi + step + XN, XN)
        return (2 * z + place // 2, tp, lax.rem(place, 2))

    def crossed(step):
        place = lax.rem(xi + step + XN, XN)
        return (2 * z + place // 2, 2 * y + 1 - core, lax.rem(place, 2))

    def at_half(step):
        place = lax.rem(xi + step + XN, XN)
        return (2 * z + place // 2, 2 * y + half, lax.rem(place, 2))

    def at_tp(step):
        return (ctx, lax.rem(tp + step, TN), dp)

    sibling = (ctx, 2 * y + 1 - core, dp)
    partner = (2 * z + 1 - half, 2 * y + 1 - core, dp)
    below = lax.rem(z + ZN - 1 + core, ZN)
    above = lax.rem(z + core, ZN)
    prev_dev = (2 * below + half, 2 * y + 1 - core, dp)
    next_dev = (2 * above + half, 2 * y + 1 - core, dp)
    other = lax.rem(z + ZN - 1 + 2 * core, ZN)
    halo_dev = (2 * other + half, 2 * y + 1 - core, dp)

    barrier = pltpu.get_barrier_semaphore()
    peers = [at_tp(i) for i in range(1, TN)]
    peers += [at_z(i) for i in range(1, ZN)]
    peers += [at_x(i) for i in range(1, XN)]
    peers += [crossed(i) for i in range(1, XN)]
    peers += [halo_dev]
    for device in peers:
        pl.semaphore_signal(barrier, inc=1, device_id=device, device_id_type=MESH)
    pl.semaphore_wait(barrier, len(peers))

    def send(src, dst, send_sem, recv_sem, device):
        pltpu.make_async_remote_copy(
            src_ref=src, dst_ref=dst, send_sem=send_sem, recv_sem=recv_sem,
            device_id=device, device_id_type=MESH,
        ).start()

    def swap(i, src, dst):
        @pl.when(off)
        def _():
            send(src, dst, swap_s.at[i], swap_r.at[i], partner)

        @pl.when(same)
        def _():
            pltpu.make_async_copy(src, dst, swap_r.at[i]).start()

    swap(0, k_in, kv.at[0, ctx])
    swap(1, v_in, kv.at[1, ctx])
    swap(2, q_in, q)
    kern_send[...] = jnp.zeros_like(kern_send)
    kern_send[0:27] = kern_in[...].astype(F32)
    swap(3, kern_send, kern)
    for i in range(1, TN):
        send(g_in, og.at[tp], og_s.at[i], og_r.at[i], at_tp(i))
    keep = pltpu.make_async_copy(g_in, og.at[tp], og_r.at[0])
    keep.start()
    weights_in = pltpu.make_async_copy(w_in, w_ref, out_sem.at[0])
    weights_in.start()

    acc[...] = jnp.zeros_like(acc)
    row_sum[...] = jnp.zeros_like(row_sum)
    row_max[...] = jnp.full_like(row_max, NEG)
    dq_acc[...] = jnp.zeros_like(dq_acc)
    shifted[...] = jnp.zeros_like(shifted)
    rbuf[0, 3, 1] = jnp.zeros((ROWS, COLS), BF16)
    rbuf[1, 3, 0] = jnp.zeros((ROWS, COLS), BF16)
    zr[0, 3, 1] = jnp.zeros((PIECE, COLS), BF16)
    zr[1, 3, 0] = jnp.zeros((PIECE, COLS), BF16)
    dsum[...] = jnp.zeros_like(dsum)

    def ring(direction, distance, part, source):
        place = kv.at[part, source]
        send(
            place, place, ring_s.at[direction, distance - 1, part],
            ring_r.at[direction, distance - 1, part], at_z(1 if direction == 0 else -1),
        )

    def ring_wait(direction, distance, part, source):
        wait(kv.at[part, source], ring_r.at[direction, distance - 1, part])

    def to_sibling(slot, source):
        send(kv.at[:, source], kv.at[:, source], sib_s.at[slot], sib_r.at[slot], sibling)

    for part in range(2):
        wait(kv.at[part, chunk], swap_r.at[part])
        ring(0, 1, part, chunk)
        ring(1, 1, part, chunk)
    to_sibling(0, chunk)

    def flip(index):
        return index + 1 - 2 * lax.rem(index, 2)

    lane = lax.broadcasted_iota(jnp.int32, (1, ROWS), 1)
    own_blocks = jnp.where(lane < FRAME, blocks[2 * chunk], blocks[2 * chunk + 1])

    def limits_of(index):
        return [
            jnp.where(own_blocks >= blocks[2 * index + frame], OPEN, NEG).astype(F32)
            for frame in range(2)
        ]

    def fwd_chunk(index):
        @pl.when(index <= chunk + 2)
        def _():
            limits = limits_of(index)
            for head in range(HEADS):
                lanes = slice(head * HD, (head + 1) * HD)
                keys = kv[0, index, :, lanes]
                vals = kv[1, index, :, lanes]
                scores = nt(keys, q[:, lanes])
                scores = jnp.concatenate(
                    [
                        jnp.minimum(scores[:FRAME], limits[0]),
                        jnp.minimum(scores[FRAME:], limits[1]),
                    ],
                    axis=0,
                )
                old = row_max[head]
                new = jnp.maximum(old, jnp.max(scores, axis=0, keepdims=True))
                weights = jnp.exp2(scores * factor - new * factor)
                shrink = jnp.exp2((old - new) * factor)
                row_max[head] = new
                row_sum[head] = row_sum[head] * shrink + jnp.sum(weights, axis=0, keepdims=True)
                acc[head] = acc[head] * shrink + tn(vals, weights.astype(BF16))

    wait(q, swap_r.at[2])

    def near(i, carry):
        @pl.when(i == 1)
        def _():
            wait(kv.at[:, flip(chunk)], sib_r.at[0])

        fwd_chunk(jnp.where(i == 0, chunk, flip(chunk)))
        return carry

    lax.fori_loop(0, 2, near, 0)

    def fwd_step(distance):
        low = 2 * lax.rem(z - distance + ZN, ZN) + core
        high = 2 * lax.rem(z + distance, ZN) + core
        for part in range(2):
            ring_wait(0, distance, part, low)
            if distance < 3 or part == 0:
                ring(0, distance + 1, part, low)
            ring_wait(1, distance, part, high)
            if distance < 3 or part == 1:
                ring(1, distance + 1, part, high)
        to_sibling(distance, low)
        to_sibling(3 + distance, high)

        def step(i, carry):
            @pl.when(i == 2)
            def _():
                wait(kv.at[:, flip(low)], sib_r.at[distance])
                wait(kv.at[:, flip(high)], sib_r.at[3 + distance])

            index = jnp.where(lax.rem(i, 2) == 0, low, high)
            fwd_chunk(jnp.where(i < 2, index, flip(index)))
            return carry

        lax.fori_loop(0, 4, step, 0)

    fwd_step(1)

    keep.wait()
    for i in range(1, TN):
        wait(og.at[lax.rem(tp + TN - i, TN)], og_r.at[i])
    weights_in.wait()
    total = nt(og[0], w_ref[:, 0:COLS])
    for i in range(1, TN):
        total += nt(og[i], w_ref[:, i * COLS : (i + 1) * COLS])
    mg_send[...] = total.astype(BF16).reshape(2, FRAME, COLS)
    swap(4, mg_send, mg_ext.at[1:3])

    quarter = og.at[pl.ds(2 * xi, 2)]
    own_quarter = pltpu.make_async_copy(quarter, ogx.at[xi], ox_r.at[0])
    own_quarter.start()
    for i in range(1, XN):
        goal = lax.rem(xi + i, XN)
        send(og.at[2 * goal + core], ogx.at[xi, core], ox_s.at[i], ox_r.at[i], at_x(i))

    fwd_step(2)

    def halo(which, ext):
        @pl.when(chunk > 0)
        def _():
            send(ext.at[1], ext.at[3], halo_s.at[which, 0], halo_r.at[which, 0], prev_dev)

        @pl.when(chunk < CN - 1)
        def _():
            send(ext.at[2], ext.at[0], halo_s.at[which, 1], halo_r.at[which, 1], next_dev)

        @pl.when(chunk == 0)
        def _():
            ext[0] = jnp.zeros((FRAME, COLS), BF16)

        @pl.when(chunk == CN - 1)
        def _():
            ext[3] = jnp.zeros((FRAME, COLS), BF16)

    def halo_wait(which, ext):
        @pl.when(chunk > 0)
        def _():
            wait(ext.at[1], halo_s.at[which, 0])
            wait(ext.at[0], halo_r.at[which, 1])

        @pl.when(chunk < CN - 1)
        def _():
            wait(ext.at[2], halo_s.at[which, 1])
            wait(ext.at[3], halo_r.at[which, 0])

    wait(mg_ext.at[1:3], swap_r.at[4])
    halo(0, mg_ext)
    for i in range(1, XN):
        place = ogx.at[lax.rem(xi + XN - i, XN), core]
        wait(place, ox_r.at[i])
        send(place, place, oy_s.at[i], oy_r.at[i], sibling)

    fwd_step(3)

    last = 2 * lax.rem(z + 4, ZN) + core
    ring_wait(0, 4, 0, last)
    ring_wait(1, 4, 1, last)
    to_sibling(7, last)

    wait(kern, swap_r.at[3])
    halo_wait(0, mg_ext)
    for frame in range(4):
        spread_columns(shifted, mg_ext, frame)

    def taps():
        return [(a, r, c) for a in (-1, 0, 1) for r in (-1, 0, 1) for c in (-1, 0, 1)]

    for frame in range(2):
        for head in range(HEADS):
            lanes = slice(head * HD, (head + 1) * HD)
            result = jnp.zeros((FRAME, HD), F32)
            for tap, (a, r, c) in enumerate(taps()):
                first = WW - WW * r
                window = shifted[1 - c, frame + 1 - a, first : first + FRAME, lanes]
                result = result + kern[tap : tap + 1, lanes] * window
            do[frame * FRAME : (frame + 1) * FRAME, lanes] = result.astype(BF16)


    def far(i, carry):
        @pl.when(i == 1)
        def _():
            wait(kv.at[:, flip(last)], sib_r.at[7])

        fwd_chunk(jnp.where(i == 0, last, flip(last)))
        return carry

    lax.fori_loop(0, 2, far, 0)

    for head in range(HEADS):
        lanes = slice(head * HD, (head + 1) * HD)
        sums = row_sum[head]
        lse[head] = row_max[head] * factor + jnp.log(sums) * math.log2(math.e)
        rows = jnp.transpose(acc[head] / sums).astype(BF16)
        at_ext[1, :, lanes] = rows[:FRAME]
        at_ext[2, :, lanes] = rows[FRAME:]
    halo(1, at_ext)

    for frame in (1, 2):
        spread_columns(shifted, at_ext, frame)
    for head in range(HEADS):
        lanes = slice(head * HD, (head + 1) * HD)
        attended = jnp.concatenate([at_ext[1, :, lanes], at_ext[2, :, lanes]], axis=0)
        product = attended.astype(F32) * do[:, lanes].astype(F32)
        dots[head] = jnp.sum(jnp.transpose(product), axis=0, keepdims=True)

    def bwd_chunk(index):
        @pl.when(index > chunk + 2)
        def _():
            terms[...] = jnp.zeros_like(terms)

        @pl.when(index <= chunk + 2)
        def _():
            limits = limits_of(index)
            for head in range(HEADS):
                lanes = slice(head * HD, (head + 1) * HD)
                keys = kv[0, index, :, lanes]
                vals = kv[1, index, :, lanes]
                queries = q[:, lanes]
                grads = do[:, lanes]
                scores = nt(keys, queries)
                scores = jnp.concatenate(
                    [
                        jnp.minimum(scores[:FRAME], limits[0]),
                        jnp.minimum(scores[FRAME:], limits[1]),
                    ],
                    axis=0,
                )
                probs = jnp.exp2(scores * factor - lse[head])
                dscores = (probs * (nt(vals, grads) - dots[head])).astype(BF16)
                terms[1, :, lanes] = nn(probs.astype(BF16), grads)
                terms[0, :, lanes] = nn(dscores, queries) * scaling
                dq_acc[head] = dq_acc[head] + tn(keys, dscores)

    def share(slot):
        xsend[slot] = terms[...].astype(BF16)
        send(xsend.at[slot], xrecv.at[slot], bx_s.at[slot], bx_r.at[slot], sibling)

    def shared(slot):
        wait(xrecv.at[slot], bx_r.at[slot])
        return terms[...] + xrecv[slot].astype(F32)

    target = 2 * lax.rem(z + 4, ZN) + core

    def terms_to(side, distance, part, device):
        rows = pl.ds((part % 2) * FRAME, FRAME)
        send(
            sbuf.at[side, distance - 1, part // 2, rows],
            rbuf.at[side, distance - 1, part // 2, rows],
            bs_s.at[side, distance - 1, part], bs_r.at[side, distance - 1, part], device,
        )

    def terms_wait(side, distance, part):
        rows = pl.ds((part % 2) * FRAME, FRAME)
        wait(rbuf.at[side, distance - 1, part // 2, rows], bs_r.at[side, distance - 1, part])

    def terms_wait_far(side, part):
        rows = pl.ds(part * FRAME, FRAME)
        wait(rbuf.at[side, 3, side, rows], bs_r.at[side, 3, 2 * side + part])

    def terms_send(distance, part):
        def run():
            for side in range(2):
                terms_to(side, distance, part, at_z(1 if side == 0 else -1))

        return run

    def bwd_pair(slot, index, between):
        def step(i, carry):
            bwd_chunk(jnp.where(i == 0, flip(index), index))

            @pl.when(i == 0)
            def _():
                share(slot)
                between()

            return carry

        lax.fori_loop(0, 2, step, 0)

    def bwd_step(distance, events):
        up = 2 * lax.rem(z + distance, ZN) + core
        down = 2 * lax.rem(z - distance + ZN, ZN) + core

        def step(i, carry):
            side = lax.rem(i, 2)
            index = jnp.where(side == 0, up, down)
            bwd_chunk(jnp.where(i < 2, flip(index), index))
            slot = distance + 3 * side

            @pl.when(i < 2)
            def _():
                share(slot)

            @pl.when(i >= 2)
            def _():
                if distance == 3:
                    for part in range(2):
                        terms_wait_far(side, part)
                else:
                    for part in range(4):
                        terms_wait(side, distance + 1, part)
                added = shared(slot) + rbuf[side, distance].astype(F32)
                sbuf[side, distance - 1] = added.astype(BF16)
                goal = lax.rem(z + ZN + 1 - 2 * side, ZN)
                terms_to(side, distance, 0, (2 * goal + half, tp, dp))

            for place, event in enumerate(events):
                pl.when(i == place)(event)
            return carry

        lax.fori_loop(0, 4, step, 0)

    grad_scale = 1.0 / math.sqrt(2.0 * CN * ROWS)
    across = lax.rem(xi + 2, XN)
    right = lax.rem(xi + 1, XN)
    left = lax.rem(xi + 3, XN)

    def mix():
        halo_wait(1, at_ext)
        for frame in (0, 3):
            spread_columns(shifted, at_ext, frame)
        for frame in range(2):
            for head in range(HEADS):
                lanes = slice(head * HD, (head + 1) * HD)
                result = jnp.zeros((FRAME, HD), F32)
                for tap, (a, r, c) in enumerate(taps()):
                    first = WW + WW * r
                    window = shifted[1 + c, frame + 1 + a, first : first + FRAME, lanes]
                    result = result + kern[tap : tap + 1, lanes] * window
                mixed[frame * FRAME : (frame + 1) * FRAME, lanes] = result.astype(BF16)
        spread_out(mixed, mixed_all, mb_s, mb_r)

    def spread_out(src, dst, send_sems, recv_sems):
        slot = 2 * core + dp
        for i in range(1, XN):
            send(src, dst.at[slot], send_sems.at[i], recv_sems.at[slot], at_half(i))

        @pl.when(off)
        def _():
            send(src, dst.at[slot], send_sems.at[0], recv_sems.at[slot], sibling)

        @pl.when(same)
        def _():
            pltpu.make_async_copy(src, dst.at[slot], recv_sems.at[slot]).start()

    def tap_sums():
        for head in range(HEADS):
            lanes = slice(head * HD, (head + 1) * HD)
            for tap, (a, r, c) in enumerate(taps()):
                first = WW + WW * r
                sums = jnp.zeros((1, HD), F32)
                for frame in range(2):
                    window = shifted[1 + c, frame + 1 + a, first : first + FRAME, lanes]
                    grad = mg_ext[1 + frame, :, lanes].astype(F32)
                    sums = sums + jnp.sum(window * grad, axis=0, keepdims=True)
                dsum[tap : tap + 1, lanes] = sums * grad_scale
        dsum_send[...] = dsum[...].astype(BF16)
        spread_out(dsum_send, dx, dx_s, dx_r)

    def products():
        own_quarter.wait()
        for i in range(1, XN):
            wait(ogx.at[lax.rem(xi + XN - i, XN), 1 - core], oy_r.at[i])
        for slot in range(XN):
            wait(mixed_all.at[slot], mb_r.at[slot])
            for b in range(2):
                block = (tn(mixed_all[slot], ogx[slot, b]) * grad_scale).reshape(ZN, PIECE, COLS)
                qsum[:, b] = block if slot == 0 else qsum[:, b] + block

    def z_place(side, distance):
        return lax.rem(z + ZN + (distance if side == 0 else -distance), ZN)

    def z_send(side, distance, sums):
        zs[side, distance - 1] = sums.astype(BF16)
        send(
            zs.at[side, distance - 1], zr.at[side, distance - 1],
            pz_s.at[side, distance - 1], pz_r.at[side, distance - 1],
            at_z(1 if side == 0 else -1),
        )

    def z_first():
        sums = qsum[z_place(0, 4)].astype(BF16)
        for side in range(2):
            zs[side, 3, side] = sums[side]
            send(
                zs.at[side, 3, side], zr.at[side, 3, side],
                pz_s.at[side, 3], pz_r.at[side, 3], at_z(1 if side == 0 else -1),
            )

    def z_arrived(side, distance):
        if distance == 4:
            wait(zr.at[side, 3, side], pz_r.at[side, 3])
        else:
            wait(zr.at[side, distance - 1], pz_r.at[side, distance - 1])
        return zr[side, distance - 1].astype(F32)

    def z_next(distance):
        for side in range(2):
            sums = qsum[z_place(side, distance)] + z_arrived(side, distance + 1)
            z_send(side, distance, sums)

    def pass_z(side, distance, piece):
        send(
            piece, piece, gz_s.at[side, distance - 1], gz_r.at[side, distance - 1],
            at_z(1 if side == 0 else -1),
        )

    def pass_x(slot, place):
        piece = allq.at[xi, place]
        for side in range(2):
            send(
                piece, piece, gx_s.at[side, slot], gx_r.at[side, slot],
                at_x(1 if side == 0 else -1),
            )

    def z_last():
        allq[xi, z] = (qsum[z] + z_arrived(0, 1) + z_arrived(1, 1)).astype(BF16)
        for side in range(2):
            pass_z(side, 1, allq.at[xi, z])
        pass_x(0, z)

    def z_gather(distance):
        for side in range(2):
            place = z_place(side, -distance)
            wait(allq.at[xi, place], gz_r.at[side, distance - 1])
            if distance < 3:
                pass_z(side, distance + 1, allq.at[xi, place])
            else:
                pass_z(side, 4, allq.at[xi, place, side])
            pass_x(distance + 3 * side, place)
        if distance == 1:
            x_relay(0)
        else:
            x_relay(distance - 1)
            x_relay(distance + 2)

    def z_gather_far():
        place = z_place(0, 4)
        for side in range(2):
            wait(allq.at[xi, place, side], gz_r.at[side, 3])
        pass_x(7, place)

    def put(quarter, i):
        pltpu.make_async_copy(allq.at[quarter], quarters_out.at[quarter], out_sem.at[i]).start()

    def slot_place(slot):
        if slot == 7:
            return z_place(0, 4)
        return z_place(0, -slot) if slot <= 3 else z_place(0, slot - 3)

    def x_relay(slot):
        place = slot_place(slot)
        wait(allq.at[left, place], gx_r.at[0, slot])
        here = allq.at[left, place, 0]
        send(here, here, gy_s.at[0, slot], gy_r.at[0, slot], at_x(1))
        wait(allq.at[right, place], gx_r.at[1, slot])
        here = allq.at[right, place, 1]
        send(here, here, gy_s.at[1, slot], gy_r.at[1, slot], at_x(-1))

    def depth_z():
        for slot in range(XN):
            wait(dx.at[slot], dx_r.at[slot])
        sums = dx[0].astype(F32) + dx[1].astype(F32) + dx[2].astype(F32) + dx[3].astype(F32)
        dz[0] = sums.astype(BF16)
        for i in range(1, ZN):
            send(dz.at[0], dz.at[i], dz_s.at[i], dz_r.at[i], at_z(i))

    def both(*events):
        def run():
            for event in events:
                event()

        return run

    def ev(f, *values):
        return lambda: f(*values)

    def nothing():
        pass

    bwd_pair(7, target, mix)
    total = shared(7).astype(BF16)
    sbuf[0, 3, 0] = total[0]
    sbuf[1, 3, 1] = total[1]
    for part in range(2):
        terms_to(0, 4, part, at_z(1))
        terms_to(1, 4, 2 + part, at_z(-1))
    bwd_step(3, [tap_sums, nothing, nothing, both(*[terms_send(3, part) for part in (1, 2, 3)])])
    products()
    z_first()
    bwd_step(2, [
        nothing,
        ev(z_next, 3),
        nothing,
        both(ev(z_next, 2), terms_send(2, 1)),
    ])
    bwd_step(1, [
        both(ev(z_next, 1), terms_send(2, 2)),
        both(z_last, terms_send(2, 3)),
        ev(z_gather, 1),
        both(ev(z_gather, 2), terms_send(1, 1)),
    ])
    bwd_pair(0, chunk, both(ev(z_gather, 3), terms_send(1, 2), terms_send(1, 3), depth_z))
    for head in range(HEADS):
        lanes = slice(head * HD, (head + 1) * HD)
        fin[0, :, lanes] = (jnp.transpose(dq_acc[head]) * scaling).astype(BF16)
    swap(7, fin.at[0], finr.at[0])
    z_gather_far()
    put(xi, 1)
    total = shared(0)
    for part in range(2):
        for side in range(2):
            terms_wait(side, 1, 2 * part)
            terms_wait(side, 1, 2 * part + 1)
        done = total[part] + rbuf[0, 0, part].astype(F32) + rbuf[1, 0, part].astype(F32)
        fin[1 + part] = done.astype(BF16)
        swap(8 if part == 0 else 5, fin.at[1 + part], finr.at[1 + part])
        if part == 0:
            x_relay(3)
            x_relay(6)
    x_relay(7)

    sums = dz[0].astype(F32)
    for i in range(1, ZN):
        wait(dz.at[i], dz_r.at[i])
        sums = sums + dz[i].astype(F32)
    depth[...] = sums[0:27]
    depth_copy = pltpu.make_async_copy(depth, depth_out, out_sem.at[5])
    depth_copy.start()
    wait(finr.at[0], swap_r.at[7])
    wait(finr.at[1], swap_r.at[8])
    wait(finr.at[2], swap_r.at[5])
    rows_copy = pltpu.make_async_copy(finr, rows_out, out_sem.at[6])
    rows_copy.start()
    put(left, 2)
    put(right, 3)
    for slot in range(ZN):
        for side in range(2):
            wait(allq.at[across, 0, side], gy_r.at[side, slot])
    put(across, 4)

    @pl.when(off)
    def _():
        wait(k_in, swap_s.at[0])
        wait(v_in, swap_s.at[1])
        wait(q_in, swap_s.at[2])
        wait(kern_send, swap_s.at[3])
        wait(mg_send, swap_s.at[4])
        wait(mixed, mb_s.at[0])
        wait(dsum_send, dx_s.at[0])
        wait(fin.at[0], swap_s.at[7])
        wait(fin.at[1], swap_s.at[8])
        wait(fin.at[2], swap_s.at[5])

    for i in range(1, TN):
        wait(g_in, og_s.at[i])
    for direction in range(2):
        for distance in range(1, 5):
            for part in range(2):
                if distance < 4 or part == direction:
                    wait(kv.at[part, chunk], ring_s.at[direction, distance - 1, part])
                    for rows in range(2):
                        wait(mg_send.at[rows], bs_s.at[direction, distance - 1, 2 * part + rows])
    for slot in range(8):
        wait(kv.at[:, chunk], sib_s.at[slot])
        wait(xsend.at[slot], bx_s.at[slot])
    for i in range(1, XN):
        wait(mixed, mb_s.at[i])
        wait(dsum_send, dx_s.at[i])
        wait(mixed, ox_s.at[i])
        wait(mixed, oy_s.at[i])
    for i in range(1, ZN):
        wait(dz.at[0], dz_s.at[i])
    for side in range(2):
        for distance in range(1, 4):
            wait(zs.at[side, 0], pz_s.at[side, distance - 1])
            wait(zs.at[side, 0], gz_s.at[side, distance - 1])
        wait(zs.at[side, 3, side], pz_s.at[side, 3])
        wait(zs.at[side, 3, side], gz_s.at[side, 3])
        for slot in range(ZN):
            wait(zs.at[side, 0], gx_s.at[side, slot])
            wait(zs.at[side, 0, 0], gy_s.at[side, slot])
    for i in range(1, 5):
        wait(allq.at[xi], out_sem.at[i])
    depth_copy.wait()
    rows_copy.wait()


def finish(
    rows_in, quarters, depth_in, dq_out, dk_out, dv_out, point_out, depth_out,
    blocks, cells, rows, depth, load, store, small,
):
    loads = [
        pltpu.make_async_copy(quarters.at[i // 2, :, i % 2], blocks.at[i], load.at[i])
        for i in range(TN)
    ]
    for copy in loads:
        copy.start()
    rows_load = pltpu.make_async_copy(rows_in, rows, small.at[0])
    rows_load.start()
    depth_load = pltpu.make_async_copy(depth_in, depth, small.at[1])
    depth_load.start()
    stores = []
    for i in range(TN):
        loads[i].wait()
        cells[i] = blocks[i].reshape(COLS, COLS).astype(F32)
        stores.append(
            pltpu.make_async_copy(
                cells.at[i], point_out.at[:, i * COLS : (i + 1) * COLS], store.at[i]
            )
        )
        stores[i].start()
    rows_load.wait()
    depth_load.wait()
    stores += [
        pltpu.make_async_copy(rows.at[0], dq_out.at[0], small.at[2]),
        pltpu.make_async_copy(rows.at[1], dk_out.at[0], small.at[3]),
        pltpu.make_async_copy(rows.at[2], dv_out.at[0], small.at[4]),
        pltpu.make_async_copy(depth, depth_out, small.at[5]),
    ]
    for copy in stores[TN:]:
        copy.start()
    for copy in stores:
        copy.wait()


def local(queries, keys, values, out_grad, depth_kernel, point_weight, block_of_frame):
    vmem = pl.BlockSpec(memory_space=pltpu.VMEM)
    hbm = pl.BlockSpec(memory_space=pl.ANY)
    dma = pltpu.SemaphoreType.DMA
    wide = (2, ROWS, COLS)
    scratch = [
        pltpu.VMEM((ROWS, COLS), BF16),
        pltpu.VMEM((2, CN, ROWS, COLS), BF16),
        pltpu.VMEM((TN, ROWS, COLS), BF16),
        pltpu.VMEM((32, COLS), F32),
        pltpu.VMEM((32, COLS), F32),
        pltpu.VMEM((HEADS, 1, ROWS), F32),
        pltpu.VMEM((HEADS, 1, ROWS), F32),
        pltpu.VMEM((HEADS, HD, ROWS), F32),
        pltpu.VMEM((HEADS, 1, ROWS), F32),
        pltpu.VMEM((HEADS, 1, ROWS), F32),
        pltpu.VMEM(point_weight.shape, BF16),
        pltpu.VMEM((2, FRAME, COLS), BF16),
        pltpu.VMEM((4, FRAME, COLS), BF16),
        pltpu.VMEM((4, FRAME, COLS), BF16),
        pltpu.VMEM((3, 4, FRAME + 2 * WW, COLS), F32),
        pltpu.VMEM((ROWS, COLS), BF16),
        pltpu.VMEM((XN, ROWS, COLS), BF16),
        pltpu.VMEM((32, COLS), F32),
        pltpu.VMEM((32, COLS), BF16),
        pltpu.VMEM((XN, 2, ROWS, COLS), BF16),
        pltpu.VMEM((ROWS, COLS), BF16),
        pltpu.VMEM((HEADS, HD, ROWS), F32),
        pltpu.VMEM(wide, F32),
        pltpu.VMEM((8,) + wide, BF16),
        pltpu.VMEM((8,) + wide, BF16),
        pltpu.VMEM((2, 4) + wide, BF16),
        pltpu.VMEM((2, 4) + wide, BF16),
        pltpu.VMEM((ZN, 2, PIECE, COLS), F32),
        pltpu.VMEM((2, 4, 2, PIECE, COLS), BF16),
        pltpu.VMEM((2, 4, 2, PIECE, COLS), BF16),
        pltpu.VMEM((XN, ZN, 2, PIECE, COLS), BF16),
        pltpu.VMEM((XN, 32, COLS), BF16),
        pltpu.VMEM((ZN, 32, COLS), BF16),
        pltpu.VMEM((27, COLS), F32),
        pltpu.VMEM((3, ROWS, COLS), BF16),
        pltpu.VMEM((3, ROWS, COLS), BF16),
        dma((7,)),
        dma((9,)), dma((9,)),
        dma((TN,)), dma((TN,)),
        dma((2, 4, 2)), dma((2, 4, 2)),
        dma((8,)), dma((8,)),
        dma((2, 2)), dma((2, 2)),
        dma((2, 4, 4)), dma((2, 4, 4)),
        dma((8,)), dma((8,)),
        dma((XN,)), dma((XN,)),
        dma((XN,)), dma((XN,)),
        dma((2, 4)), dma((2, 4)),
        dma((2, 4)), dma((2, 4)),
        dma((2, ZN)), dma((2, ZN)),
        dma((2, ZN)), dma((2, ZN)),
        dma((XN,)), dma((XN,)),
        dma((XN,)), dma((XN,)),
        dma((ZN,)), dma((ZN,)),
    ]
    rows, quarters, depth = pl.pallas_call(
        body,
        out_shape=(
            jax.ShapeDtypeStruct((3, ROWS, COLS), BF16),
            jax.ShapeDtypeStruct((XN, ZN, 2, PIECE, COLS), BF16),
            jax.ShapeDtypeStruct(depth_kernel.shape, F32),
        ),
        in_specs=[hbm] * 5 + [vmem, pl.BlockSpec(memory_space=pltpu.SMEM)],
        out_specs=(hbm,) * 3,
        scratch_shapes=scratch,
        compiler_params=pltpu.CompilerParams(
            collective_id=0, has_side_effects=True, vmem_limit_bytes=60 * 1024 * 1024
        ),
        name="layer_backward",
    )(queries[0], keys[0], values[0], out_grad[0], point_weight, depth_kernel, block_of_frame)
    part = jax.ShapeDtypeStruct((1, ROWS, COLS), BF16)
    return pl.pallas_call(
        finish,
        out_shape=(
            part, part, part,
            jax.ShapeDtypeStruct(point_weight.shape, F32),
            jax.ShapeDtypeStruct(depth_kernel.shape, F32),
        ),
        in_specs=[hbm] * 3,
        out_specs=(hbm,) * 5,
        scratch_shapes=[
            pltpu.VMEM((TN, ZN, PIECE, COLS), BF16),
            pltpu.VMEM((TN, COLS, COLS), F32),
            pltpu.VMEM((3, ROWS, COLS), BF16),
            pltpu.VMEM(depth_kernel.shape, F32),
            dma((TN,)), dma((TN,)), dma((6,)),
        ],
        compiler_params=pltpu.CompilerParams(vmem_limit_bytes=60 * 1024 * 1024),
        name="write_outputs",
    )(rows, quarters, depth)


def solution(mesh):
    placed = (
        P("dp", "ctx", "tp"),
        P("dp", "ctx", "tp"),
        P("dp", "ctx", "tp"),
        P("dp", "ctx", "tp"),
        P(None, "tp"),
        P("tp", None),
        P(),
    )
    return jax.shard_map(
        local,
        mesh=mesh,
        in_specs=placed,
        out_specs=(
            P("dp", "ctx", "tp"),
            P("dp", "ctx", "tp"),
            P("dp", "ctx", "tp"),
            P("tp", None),
            P(None, "tp"),
        ),
        check_vma=False,
    )
```
